32 devices in a mesh: lon: 2 (over x), lat: 4 (over z), grp: 4 (over y, core).
Axes of the slice: x: 2, y: 2, z: 4, core: 2. Of those that a mesh axis runs over, the one named last changes fastest.
Arguments:
- sea_surface: float32 [16, 256, 1024], P('grp', 'lat', 'lon'), may hold values from -6 to 6
- velocity: float32 [2, 16, 256, 1024], P(None, 'grp', 'lat', 'lon'), may hold values from -2 to 2
- levels: int32 [256, 1024], P('lat', 'lon'), may hold values from 1 to 50
- wind_basis: bfloat16 [16, 256, 1024], P(None, 'lat', 'lon'), may hold values from -1.5 to 1.5
- proposals: float32 [16, 16], replicated, may hold values from -4 to 4
- member_ids: int32 [16], replicated, may hold values from 0 to 15, each once
- conv_weight: bfloat16 [128, 256], replicated, may hold values from -0.5 to 0.5
- couple_in: float32 [264, 512], replicated, may hold values from -0.375 to 0.375
- couple_in_bias: float32 [512], replicated, may hold values from -3 to 3
- couple_out: float32 [512, 16], replicated, may hold values from -0.25 to 0.25
- couple_out_bias: float32 [16], replicated, may hold values from -3 to 3
Outputs:
- surface_out: float32 [16, 256, 1024], P('grp', 'lat', 'lon')
- velocity_out: float32 [2, 16, 256, 1024], P(None, 'grp', 'lat', 'lon')
- summary: float32 [2, 4, 4, 16, 256], P('lon', 'lat', 'grp')
- weight_step: float32 [176656], replicated
The draws below stay inside these ranges and needn't reach their ends.
Inputs may be any that keep to these rules, and one draw needn't show every extreme that they name: member_ids is a permutation of 0 to 15.
All inputs are finite; a program needn't handle non-finite values.
Results may differ from the reference program's by a relative error of at most 0.0031.
Values may be sent and summed in bfloat16 or wider, within the bound.
No kernel may reach another device: no remote copies, remote signals or barrier semaphores. Data moves between devices by JAX's collectives and lax.ppermute only.
A program may use at most 128 MiB of HBM per device.

```python
import math
from functools import partial
import jax
import jax.numpy as jnp
from jax import lax

CY = 64
MEM_DEV = 4
STEPS = 8
NLEV = 50
PH = 8
PW = 16
FEAT = 256
HID = 512
PDIM = 16
HALF = 8
MEMBERS = 16
NY = 256
NX = 1024
ITEMS_DEV = 16
N_LON = 2
N_LAT = 4
N_GRP = 4


def set_ends(entries, stream_key, least, top_value):
    extent = entries.shape
    index_at = [jax.random.randint(jax.random.fold_in(stream_key, axis), (), 0, extent[axis]) for axis in range(len(extent))]
    entries = entries.at[tuple(index_at)].set(least)
    longest = extent.index(max(extent))
    index_at[longest] = (index_at[longest] + 1) % extent[longest]
    return entries.at[tuple(index_at)].set(top_value)


def steps_of(stream_key, dims, pieces, low, high):
    gain, own = 1.0, jax.random.fold_in(stream_key, 6)
    for dim, blocks in pieces:
        steps = jnp.exp(jax.random.uniform(jax.random.fold_in(own, dim), (blocks,), jnp.float32, low / len(pieces), high / len(pieces)))
        gain = gain * jnp.repeat(steps, dims[dim] // blocks).reshape([-1 if axis == dim else 1 for axis in range(len(dims))])
    return gain


def scatter_about(own_key, shape, spread, most, cuts=(), held_as=jnp.bfloat16):
    loudness = steps_of(own_key, shape, cuts, -0.22, 0.18) if cuts else 1.0
    entries = jax.random.normal(own_key, shape, jnp.float32) * spread * loudness
    return jnp.minimum(jnp.maximum(entries, -most), most).astype(held_as)


def setup_inputs(seed: int = 0) -> dict:
    arg_keys = jax.random.split(jax.random.key(seed), 12)
    return {
        "sea_surface": scatter_about(arg_keys[0], (MEMBERS, NY, NX), 1.0, 6.0, ((0, 4), (1, 4), (2, 2)), jnp.float32),
        "velocity": scatter_about(arg_keys[1], (2, MEMBERS, NY, NX), 0.3, 2.0, ((1, 4), (2, 4), (3, 2)), jnp.float32),
        "levels": set_ends(jax.random.randint(arg_keys[2], (NY, NX), 1, NLEV + 1), jax.random.fold_in(arg_keys[2], 1), 1, NLEV).astype(jnp.int32),
        "wind_basis": scatter_about(arg_keys[3], (PDIM, NY, NX), PDIM ** -0.5, 1.5, ((1, 4), (2, 2))),
        "proposals": scatter_about(arg_keys[4], (MEMBERS, PDIM), 1.0, 4.0, (), jnp.float32),
        "member_ids": jax.random.permutation(arg_keys[5], MEMBERS).astype(jnp.int32),
        "conv_weight": scatter_about(arg_keys[6], (PH * PW, FEAT), (PH * PW) ** -0.5, 0.5),
        "couple_in": scatter_about(arg_keys[7], (HALF + FEAT, HID), (HALF + FEAT) ** -0.5, 0.375, (), jnp.float32),
        "couple_in_bias": scatter_about(arg_keys[8], (HID,), 0.5, 3.0, (), jnp.float32),
        "couple_out": scatter_about(arg_keys[9], (HID, PDIM), HID ** -0.5, 0.25, (), jnp.float32),
        "couple_out_bias": scatter_about(arg_keys[10], (PDIM,), 0.5, 3.0, (), jnp.float32),
    }


GRAVITY = 0.45
DRAG_RATE = 0.02
CORI_BASE = 0.05
CORI_SLOPE = 0.1
WIND_SCALE = 0.05
EPSILON = 1e-06
PRECISE = lax.Precision.HIGHEST

def advance(sea_level, east_flow, north_flow, hu_face, hv_face, forcing, cori_u, cori_v):
    flux_x = hu_face * east_flow
    flux_y = hv_face * north_flow
    zero_row = jnp.zeros_like(flux_y[:1])
    flux_y_up = jnp.concatenate([flux_y[1:], zero_row], axis=0)
    new_level = sea_level - (jnp.roll(flux_x, -1, axis=1) - flux_x + flux_y_up - flux_y)
    north_up = jnp.concatenate([north_flow[1:], zero_row], axis=0)
    east_down = jnp.concatenate([zero_row, east_flow[:-1]], axis=0)
    v_mean = 0.25 * (north_flow + north_up + jnp.roll(north_flow, 1, axis=1) + jnp.roll(north_up, 1, axis=1))
    u_mean = 0.25 * (east_flow + jnp.roll(east_flow, -1, axis=1) + east_down + jnp.roll(east_down, -1, axis=1))
    level_down = jnp.concatenate([zero_row, new_level[:-1]], axis=0)
    new_east = east_flow + cori_u * v_mean - GRAVITY * (new_level - jnp.roll(new_level, 1, axis=1)) - DRAG_RATE * east_flow + forcing
    new_north = north_flow - cori_v * u_mean - GRAVITY * (new_level - level_down) - DRAG_RATE * north_flow
    return (new_level, new_east, new_north)

def to_patches(band_rows, kernel_rows, kernel_cols):
    count, height, breadth = band_rows.shape
    blocks = band_rows.reshape(count, height // kernel_rows, kernel_rows, breadth // kernel_cols, kernel_cols)
    return blocks.transpose(0, 1, 3, 2, 4).reshape(-1, kernel_rows * kernel_cols)

def flow_loss(params, w_in, b_in, w_out, b_out, summary):
    half_count = params.shape[1] // 2
    lower = params[:, :half_count]
    upper = params[:, half_count:]
    context = jnp.concatenate([lower, summary], axis=1)
    hidden = jnp.tanh(jnp.dot(context, w_in, precision=PRECISE) + b_in)
    out_raw = jnp.dot(hidden, w_out, precision=PRECISE) + b_out
    log_scale = jnp.tanh(out_raw[:, :half_count])
    latent = upper * jnp.exp(log_scale) + out_raw[:, half_count:]
    return jnp.sum(0.5 * latent * latent - log_scale)

def reference(sea_surface, velocity, levels, wind_basis, proposals, member_ids, conv_weight, couple_in, couple_in_bias, couple_out, couple_out_bias):
    sea_depth = levels.astype(jnp.float32) / NLEV
    hu_face = 0.5 * (sea_depth + jnp.roll(sea_depth, 1, axis=1))
    hv_face = 0.5 * (sea_depth + jnp.concatenate([jnp.zeros_like(sea_depth[:1]), sea_depth[:-1]], axis=0))
    row_index = jnp.arange(NY).astype(jnp.float32)[:, None]
    cori_u = CORI_BASE + CORI_SLOPE * (row_index + 0.5) / NY
    cori_v = CORI_BASE + CORI_SLOPE * row_index / NY
    coeff_rows = proposals[member_ids].astype(jnp.bfloat16)
    basis_flat = wind_basis.reshape(PDIM, NY * NX)

    def evolve(inputs):
        sea_level, east_flow, north_flow, coeffs = inputs
        forcing = WIND_SCALE * jnp.dot(coeffs[None, :], basis_flat, preferred_element_type=jnp.float32).reshape(NY, NX)
        frames = []
        for step_index in range(STEPS):
            sea_level, east_flow, north_flow = advance(sea_level, east_flow, north_flow, hu_face, hv_face, forcing, cori_u, cori_v)
            frames.append(sea_level.astype(jnp.bfloat16))
        return (sea_level, east_flow, north_flow, jnp.stack(frames))
    surface_out, east_out, north_out, frames = lax.map(evolve, (sea_surface, velocity[0], velocity[1], coeff_rows))
    velocity_out = jnp.stack([east_out, north_out])
    band_rows = frames.reshape(N_GRP, MEM_DEV, STEPS, N_LAT, CY, NX).transpose(3, 0, 2, 1, 4, 5)
    band_rows = band_rows.reshape(N_LAT, N_GRP, N_LON, ITEMS_DEV, CY, NX).transpose(2, 0, 1, 3, 4, 5).reshape(-1, CY, NX)
    lon_ids = jnp.arange(N_LON, dtype=jnp.int32)[:, None, None, None]
    grp_ids = jnp.arange(N_GRP, dtype=jnp.int32)[None, None, :, None]
    item_ids = jnp.arange(ITEMS_DEV, dtype=jnp.int32)[None, None, None, :]
    members = grp_ids * MEM_DEV + (lon_ids * ITEMS_DEV + item_ids) % MEM_DEV
    members = jnp.broadcast_to(members, (N_LON, N_LAT, N_GRP, ITEMS_DEV)).reshape(-1)
    params = proposals[member_ids[members]]
    inv_root = 1.0 / math.sqrt(CY // PH * (NX // PW))

    def embed_band(band):
        patch_rows = to_patches(band[None], PH, PW)
        activation = jnp.tanh(jnp.dot(patch_rows, conv_weight, preferred_element_type=jnp.float32))
        return lax.optimization_barrier(jnp.sum(activation, axis=0)) * inv_root
    summary = lax.map(embed_band, band_rows)
    loss_value, pullback = jax.vjp(partial(flow_loss, params), couple_in, couple_in_bias, couple_out, couple_out_bias, summary)
    g_in, g_in_b, g_out, g_out_b, d_summary = pullback(jnp.ones_like(loss_value))

    def conv_grad(running, inputs):
        band, d_item = inputs
        patch_rows = to_patches(band[None], PH, PW)
        activation = jnp.tanh(jnp.dot(patch_rows, conv_weight, preferred_element_type=jnp.float32))
        d_pre = ((d_item * inv_root)[None, :] * (1.0 - activation * activation)).astype(jnp.bfloat16)
        return (running + lax.dot_general(patch_rows, d_pre, (((0,), (0,)), ((), ())), preferred_element_type=jnp.float32), None)
    g_conv, unused = lax.scan(conv_grad, jnp.zeros((PH * PW, FEAT), jnp.float32), (band_rows, d_summary))
    grad_total = jnp.concatenate([g_conv.reshape(-1), g_in.reshape(-1), g_in_b, g_out.reshape(-1), g_out_b])
    weight_step = -grad_total / jnp.sqrt(jnp.mean(grad_total * grad_total) + EPSILON)
    return (surface_out, velocity_out, summary.reshape(N_LON, N_LAT, N_GRP, ITEMS_DEV, FEAT), weight_step)
```

```python
import math

import jax
import jax.numpy as jnp
from jax import lax
from jax.experimental import pallas as pl
from jax.experimental.pallas import tpu as pltpu
from jax.sharding import PartitionSpec as P

STEPS = 8
NLEV = 50
PH = 8
PW = 16
HALO = 8
PAD = 16

GRAVITY = 0.45
DRAG_RATE = 0.02
CORI_BASE = 0.05
CORI_SLOPE = 0.1
WIND_SCALE = 0.05
EPSILON = 1e-06
PRECISE = lax.Precision.HIGHEST
F32 = jnp.float32
BF16 = jnp.bfloat16
LANES = 128
MEBI = 2**20


def vmem():
    return pl.BlockSpec(memory_space=pltpu.VMEM)


def smem():
    return pl.BlockSpec(memory_space=pltpu.SMEM)


def params_of(mebi, **rest):
    return pltpu.CompilerParams(vmem_limit_bytes=mebi * MEBI, **rest)


def lane_ids(rows):
    return lax.broadcasted_iota(jnp.int32, (rows, LANES), 1)


def plane_matrix(cols, inverse=False):
    patches = cols // PW
    src = lax.broadcasted_iota(jnp.int32, (cols, cols), 1 if inverse else 0)
    dst = lax.broadcasted_iota(jnp.int32, (cols, cols), 0 if inverse else 1)
    return jnp.where(src == (dst % patches) * PW + dst // patches, 1.0, 0.0).astype(BF16)


def moved(value, matrix):
    high = value.astype(BF16)
    rest = (value - high.astype(F32)).astype(BF16)
    return jnp.dot(high, matrix, preferred_element_type=F32) + jnp.dot(
        rest, matrix, preferred_element_type=F32
    )


def by_segment(pieces, segment):
    out = pieces[-1]
    for index in range(len(pieces) - 2, -1, -1):
        out = jnp.where(segment == index, pieces[index], out)
    return out


def turned(value, shift):
    shift = shift % LANES
    return value if shift == 0 else pltpu.roll(value, shift, 1)


def planes_from(parts, patches):
    rows = parts[0].shape[0]
    per = LANES // patches
    segment = lane_ids(rows) // patches
    planes = []
    for k in range(PW):
        group, place = divmod(k, per)
        block = slice(group * LANES, (group + 1) * LANES)
        planes.append(
            by_segment(
                [turned(part[:, block], (m - place) * patches) for m, part in enumerate(parts)],
                segment,
            )
        )
    return planes


def edges_of(firsts, lasts, patches):
    rows = firsts[0].shape[0]
    lane = lane_ids(rows)
    out = jnp.zeros((rows, LANES), F32)
    for m, (first, last) in enumerate(zip(firsts, lasts)):
        both = jnp.where(lane < HALO, first, turned(last, 2 * HALO))
        here = (lane >= m * patches) & (lane < m * patches + 2 * HALO)
        out = jnp.where(here, turned(both, m * patches), out)
    return out


def pack_kernel(members, ids, sea, vel, levels, wind, props, force, low, high, side, low_c, high_c):
    rows, cols = levels.shape
    patches = cols // PW
    base = lax.axis_index("grp") * members
    kinds = wind.shape[0]
    coeff = [
        props[pl.ds(ids[base + m], 1), :].astype(BF16).astype(F32) * WIND_SCALE
        for m in range(members)
    ]
    for r0 in range(0, rows, 16):
        acc = [jnp.zeros((16, cols), F32) for _ in range(members)]
        for k in range(kinds):
            basis = wind[k, r0 : r0 + 16, :].astype(F32)
            for m in range(members):
                acc[m] = acc[m] + coeff[m][:, k : k + 1] * basis
        for m in range(members):
            force[m, r0 : r0 + 16, :] = acc[m]
    depth = levels[...].astype(F32)
    groups = [lambda rs, m=m: sea[m, rs, :] for m in range(members)]
    groups += [lambda rs, m=m, d=d: vel[d, m, rs, :] for d in range(2) for m in range(members)]
    groups += [lambda rs, m=m: force[m, rs, :] for m in range(members)]
    groups += [lambda rs: depth[rs, :], lambda rs: jnp.zeros((HALO, cols), F32)]
    for out, rs in ((low, slice(0, HALO)), (high, slice(rows - HALO, rows))):
        for g in range(0, len(groups), 2):
            pair = jnp.concatenate([groups[g](rs), groups[g + 1](rs)], axis=0)
            out[g * HALO : (g + 2) * HALO, :] = pair.astype(BF16)
    firsts, lasts = slice(0, LANES), slice(cols - LANES, cols)
    fields = [
        [lambda cs, m=m: sea[m, :, cs] for m in range(members)],
        [lambda cs, m=m: vel[0, m, :, cs] for m in range(members)],
        [lambda cs, m=m: vel[1, m, :, cs] for m in range(members)],
        [lambda cs, m=m: force[m, :, cs] for m in range(members)],
        [lambda cs: depth[:, cs]] * members,
    ]
    lows, highs = [], []
    for i, field in enumerate(fields):
        edge = edges_of([f(firsts) for f in field], [f(lasts) for f in field], patches)
        side[i * rows : (i + 1) * rows, :] = edge.astype(BF16)
        lows.append(edge[:HALO])
        highs.append(edge[rows - HALO :])
    blank = jnp.zeros((HALO, LANES), F32)
    low_c[...] = jnp.concatenate(lows + [blank], axis=0).astype(BF16)
    high_c[...] = jnp.concatenate(highs + [blank], axis=0).astype(BF16)


def planar_kernel(members, sea, vel, force, levels, out):
    rows, cols = levels.shape
    patches = cols // PW
    matrix = plane_matrix(cols)
    scale = 1.0 / GRAVITY
    for i, field in enumerate((sea, vel.at[0], vel.at[1], force)):
        value = field[...].reshape(members * rows, cols)
        spread = moved(value if i == 0 else value * scale, matrix)
        parts = [spread[m * rows : (m + 1) * rows] for m in range(members)]
        for k, plane in enumerate(planes_from(parts, patches)):
            out[i, k] = plane
    spread = jnp.dot(levels[...].astype(F32).astype(BF16), matrix, preferred_element_type=F32)
    for k, plane in enumerate(planes_from([spread] * members, patches)):
        out[4, k] = plane


def back_kernel(members, state, sea, vel):
    rows, cols = sea.shape[1:]
    patches = cols // PW
    per = LANES // patches
    matrix = plane_matrix(cols, inverse=True)
    segment = lane_ids(rows) // patches
    for i in range(3):
        parts = []
        for m in range(members):
            groups = []
            for g in range(PW // per):
                pieces = [turned(state[i, g * per + j], (j - m) * patches) for j in range(per)]
                groups.append(by_segment(pieces, segment))
            parts.append(jnp.concatenate(groups, axis=1))
        value = moved(jnp.concatenate(parts, axis=0), matrix)
        for m in range(members):
            part = value[m * rows : (m + 1) * rows]
            if i == 0:
                sea[m] = part
            else:
                vel[i - 1, m] = part * GRAVITY


def flow_step(src, dst, hu, hv, hvu, cu, cv, force, last_mask, rows, patches):
    strip = PW
    end = PAD + rows + HALO
    half = (rows + 2 * HALO) // 2
    keep = 1.0 - DRAG_RATE
    for r0 in range(PAD - HALO, end, half):
        here, up, down = pl.ds(r0, half), pl.ds(r0 + 1, half), pl.ds(r0 - 1, half)
        last = lane_ids(half) % patches == patches - 1

        def wrap_left(plane, rim):
            return pltpu.roll(jnp.where(last, rim, plane), 1, 1)

        def wrap_right(plane, rim):
            return jnp.where(last, pltpu.roll(rim, PW - 1, 1), pltpu.roll(plane, LANES - 1, 1))

        def new_level(p, fx, fx_right):
            n_up = src[2, p, up, :]
            n = src[2, p, here, :]
            fy = hvu[p, here, :] * n_up - hv[p, here, :] * n
            level = src[0, p, here, :] - ((fx_right - fx) + fy)
            dst[0, p, here, :] = level
            return level, n, n + n_up

        def new_flow(p, e, e_right, em, em_right, n, v, level, level_left):
            u = (e + e_right) + (em + em_right)
            dst[1, p, here, :] = (
                keep * e + cu[here, :] * v - (level - level_left) + force[p, here, :]
            )
            level_down = dst[0, p, down, :]
            north = keep * n - cv[here, :] * u - (level - level_down)
            if r0 + half == end:
                dst[2, p, pl.ds(r0, half - HALO), :] = north[: half - HALO]
                dst[2, p, pl.ds(end - HALO, HALO), :] = north[half - HALO :] * last_mask
            else:
                dst[2, p, here, :] = north

        e_rim = src[1, strip, here, :]
        em_rim = src[1, strip, down, :]
        fx_rim = hu[strip, here, :] * e_rim
        level_rim, n_rim, vs_rim = new_level(strip, fx_rim, pltpu.roll(fx_rim, LANES - 1, 1))
        new_flow(
            strip,
            e_rim,
            pltpu.roll(e_rim, LANES - 1, 1),
            em_rim,
            pltpu.roll(em_rim, LANES - 1, 1),
            n_rim,
            vs_rim + pltpu.roll(vs_rim, 1, 1),
            level_rim,
            pltpu.roll(level_rim, 1, 1),
        )
        e_end = wrap_right(src[1, 0, here, :], e_rim)
        em_end = wrap_right(src[1, 0, down, :], em_rim)
        e_last = src[1, PW - 1, here, :]
        level_last, n_last, vs_last = new_level(
            PW - 1, hu[PW - 1, here, :] * e_last, hu[PW + 1, here, :] * e_end
        )
        level_left = wrap_left(level_last, level_rim)
        vs_left = wrap_left(vs_last, vs_rim)
        e = src[1, 0, here, :]
        em = src[1, 0, down, :]
        fx = hu[0, here, :] * e
        for p in range(PW):
            if p < PW - 1:
                e_right = src[1, p + 1, here, :]
                em_right = src[1, p + 1, down, :]
                fx_right = hu[p + 1, here, :] * e_right
                level, n, vs = new_level(p, fx, fx_right)
            else:
                e_right, em_right, fx_right = e_end, em_end, None
                level, n, vs = level_last, n_last, vs_last
            new_flow(p, e, e_right, em, em_right, n, vs + vs_left, level, level_left)
            level_left, vs_left, e, em, fx = level, vs, e_right, em_right, fx_right


def flow_kernel(
    members,
    rows,
    cols,
    lat_count,
    planes,
    south,
    north,
    side,
    east,
    west,
    south_east,
    south_west,
    north_east,
    north_west,
    weight,
    partial,
    gram,
    final,
    state_a,
    state_b,
    force,
    depth,
    hu,
    hv,
    hvu,
    cu,
    cv,
    w_rows,
    w_planes,
    patch_t,
    slope,
):
    patches = cols // PW
    turn = pl.program_id(0)
    lat = lax.axis_index("lat")
    strip = PW
    height = rows + 2 * PAD
    wide = rows + 2 * HALO
    inner = slice(PAD, PAD + rows)
    scale = 1.0 / GRAVITY

    @pl.when(turn == 0)
    def _():
        for state in (state_a, state_b):
            for i in range(3):
                for p in range(PW + 1):
                    state[i, p, 0:HALO, :] = jnp.zeros((HALO, LANES), F32)
                    state[i, p, height - HALO : height, :] = jnp.zeros((HALO, LANES), F32)
        homes = (state_a.at[0], state_a.at[1], state_a.at[2], force, depth)
        for i, home in enumerate(homes):
            for k in range(PW):
                home[k, inner, :] = planes[i, k]
        for p in range(PW + 1):
            depth[p, 0:HALO, :] = jnp.zeros((HALO, LANES), F32)
            depth[p, height - HALO : height, :] = jnp.zeros((HALO, LANES), F32)
        matrix = plane_matrix(cols)

        def strip_of(own, from_east, from_west):
            place = lane_ids(own.shape[0]) % patches
            return jnp.where(
                place < 2 * HALO,
                own,
                jnp.where(
                    place < 3 * HALO,
                    pltpu.roll(from_east, 2 * HALO, 1),
                    pltpu.roll(from_west, LANES - 2 * HALO, 1),
                ),
            )

        for i, home in enumerate(homes):
            factor = 1.0 if i in (0, 4) else scale
            rs = slice(i * rows, (i + 1) * rows)
            rim = strip_of(side[rs, :].astype(F32), east[rs, :].astype(F32), west[rs, :].astype(F32))
            home[strip, inner, :] = rim * factor
        for got, got_east, got_west, r0 in (
            (south, south_east, south_west, PAD - HALO),
            (north, north_east, north_west, PAD + rows),
        ):
            place = slice(r0, r0 + HALO)
            spread = jnp.dot(got[...], matrix, preferred_element_type=F32)
            plain = got[...].astype(F32)
            east_c = got_east[...].astype(F32)
            west_c = got_west[...].astype(F32)
            for i, home in enumerate(homes):
                factor = 1.0 if i in (0, 4) else scale
                if i < 4:
                    starts = [(i * members + m) * HALO for m in range(members)]
                else:
                    starts = [4 * members * HALO] * members
                parts = [spread[s : s + HALO] for s in starts]
                for k, plane in enumerate(planes_from(parts, patches)):
                    home[k, place, :] = plane * factor
                own = edges_of(
                    [plain[s : s + HALO, :LANES] for s in starts],
                    [plain[s : s + HALO, cols - LANES :] for s in starts],
                    patches,
                )
                rs = slice(i * HALO, (i + 1) * HALO)
                home[strip, place, :] = strip_of(own, east_c[rs], west_c[rs]) * factor
        span = slice(PAD - HALO, PAD + rows + HALO)
        row = lax.broadcasted_iota(jnp.int32, (wide, LANES), 0) + (lat * rows - HALO)
        inside = (row >= 0) & (row < lat_count * rows)
        place = row.astype(F32)
        total = lat_count * rows
        cu[span, :] = jnp.where(
            inside, 0.25 * (CORI_BASE + CORI_SLOPE * (place + 0.5) / total), 0.0
        )
        cv[span, :] = jnp.where(inside, 0.25 * (CORI_BASE + CORI_SLOPE * place / total), 0.0)
        half_depth = 0.5 * GRAVITY / NLEV
        last = lane_ids(wide) % patches == patches - 1
        for p in range(PW + 1):
            here = depth[p, span, :]
            if p == 0:
                left = pltpu.roll(
                    jnp.where(last, depth[strip, span, :], depth[PW - 1, span, :]), 1, 1
                )
            elif p == strip:
                left = pltpu.roll(here, 1, 1)
            else:
                left = depth[p - 1, span, :]
            below = depth[p, PAD - HALO - 1 : PAD + rows + HALO - 1, :]
            above = depth[p, PAD - HALO + 1 : PAD + rows + HALO + 1, :]
            hu[p, span, :] = half_depth * (here + left)
            hv[p, span, :] = half_depth * (here + below)
            hvu[p, span, :] = jnp.where(inside, half_depth * (here + above), 0.0)
        hu[PW + 1, span, :] = jnp.where(
            last,
            pltpu.roll(hu[strip, span, :], PW - 1, 1),
            pltpu.roll(hu[0, span, :], LANES - 1, 1),
        )
        for h in range(w_rows.shape[0]):
            cs = slice(h * LANES, (h + 1) * LANES)
            w_rows[h] = weight[:, cs].astype(F32)
            w_planes[:, cs] = jnp.concatenate(
                [w_rows[h, pl.ds(k, PH, stride=PW), :] for k in range(PW)], axis=0
            ).astype(BF16)

    last_mask = jnp.where(lat < lat_count - 1, 1.0, 0.0)
    count = rows // PH
    for sub, (src, dst) in enumerate(((state_a, state_b), (state_b, state_a))):
        flow_step(src, dst, hu, hv, hvu, cu, cv, force, last_mask, rows, patches)
        total = None
        for b in range(count):
            cells = dst[0, 0:PW, PAD + b * PH : PAD + (b + 1) * PH, :].reshape(PW * PH, LANES)
            cells_t = cells.T.astype(BF16)
            act = jnp.tanh(jnp.dot(cells_t, w_planes[...], preferred_element_type=F32))
            total = act if total is None else total + act
            fall = (1.0 - act * act).astype(BF16)
            for m in range(members):
                rs = slice(m * patches, (m + 1) * patches)
                to = slice(b * patches, (b + 1) * patches)
                patch_t[m, to, :] = cells_t[rs]
                slope[m, to, :] = fall[rs]
        sums = jnp.sum(total.reshape(members, patches, total.shape[1]), axis=1)
        partial[sub * members : (sub + 1) * members, :] = sums
        for m in range(members):
            gram[sub * members + m] = lax.dot_general(
                patch_t[m], slope[m], (((0,), (0,)), ((), ())), preferred_element_type=F32
            )

    @pl.when(turn == pl.num_programs(0) - 1)
    def _():
        for i in range(3):
            for k in range(PW):
                final[i, k] = state_a[i, k, inner, :]


def picked(ids_col, props, members_col):
    count = props.shape[0]
    slots = members_col.shape[0]
    slot = lax.broadcasted_iota(jnp.int32, (slots, count), 1)
    first = jnp.where(members_col == slot, 1.0, 0.0).astype(F32)
    second = jnp.where(
        ids_col[...] == lax.broadcasted_iota(jnp.int32, (count, count), 1), 1.0, 0.0
    ).astype(F32)
    rows = jnp.dot(second, props[...], precision=PRECISE, preferred_element_type=F32)
    return jnp.dot(first, rows, precision=PRECISE, preferred_element_type=F32)


def mm(a, b, ca=1, cb=0):
    return lax.dot_general(
        a, b, (((ca,), (cb,)), ((), ())), precision=PRECISE, preferred_element_type=F32
    )


def flow_grads(params, summary, w_in, b_in, w_out, b_out):
    half = params.shape[1] // 2
    lower, upper = params[:, :half], params[:, half:]
    w_low, w_sum = w_in[0:half, :], w_in[half:, :]
    hidden = jnp.tanh(mm(summary, w_sum) + mm(lower, w_low) + b_in[...])
    raw = mm(hidden, w_out[...]) + b_out[...]
    log_scale = jnp.tanh(raw[:, :half])
    grown = upper * jnp.exp(log_scale)
    latent = grown + raw[:, half:]
    d_scale = (latent * grown - 1.0) * (1.0 - log_scale * log_scale)
    d_raw = jnp.concatenate([d_scale, latent], axis=1)
    d_hidden = mm(d_raw, w_out[...], 1, 1) * (1.0 - hidden * hidden)
    return lower, hidden, d_raw, d_hidden


def member_column(count, members, groups):
    row = lax.broadcasted_iota(jnp.int32, (count, 1), 0)
    base = lax.axis_index("grp") * members
    if groups is None:
        return base + row % members
    per, order = groups
    out = jnp.zeros((count, 1), jnp.int32)
    for index, flip in enumerate(order):
        grp = lax.axis_index("grp") ^ flip
        out = jnp.where(row // per == index, grp * members + row % members, out)
    return out


def local_kernel(
    members, inv_root, mine, theirs, ids, props, w_in, b_in, w_out, b_out, gram, summary, kept, sent, held, total, sem
):
    copy = pltpu.make_async_copy(gram, held, sem)
    copy.start()
    sums = (mine[...] + theirs[...]) * inv_root
    summary[...] = sums
    count = sums.shape[0]
    params = picked(ids, props, member_column(count, members, None))
    half = params.shape[1] // 2
    _, _, _, d_hidden = flow_grads(params, sums, w_in, b_in, w_out, b_out)
    d_summary = mm(d_hidden, w_in[half:, :], 1, 1) * inv_root
    copy.wait()
    acc = jnp.zeros(held.shape[1:], F32)
    for i in range(count):
        acc = acc + held[i] * d_summary[i : i + 1, :]
    total[...] = acc
    cells = acc.shape[0] // 2
    core = lax.axis_index("grp") % 2
    kept[...] = total[pl.ds(pl.multiple_of(core * cells, 8), cells), :]
    sent[...] = total[pl.ds(pl.multiple_of((1 - core) * cells, 8), cells), :]


def couple_kernel(members, per, order, summary, ids, props, w_in, b_in, w_out, b_out, rows, square, staged):
    sums = summary[...]
    params = picked(ids, props, member_column(sums.shape[0], members, (per, order)))
    lower, hidden, d_raw, d_hidden = flow_grads(params, sums, w_in, b_in, w_out, b_out)
    g_low = mm(lower, d_hidden, 0, 0)
    g_sum = mm(sums, d_hidden, 0, 0)
    g_out = mm(hidden, d_raw, 0, 0)
    g_in_b = jnp.sum(d_hidden, axis=0, keepdims=True)
    g_out_b = jnp.sum(d_raw, axis=0, keepdims=True)
    hid = d_hidden.shape[1]
    per_row = hid // LANES
    half = lower.shape[1]
    feats = sums.shape[1]
    width = d_raw.shape[1]
    fold = LANES // width
    base = (half + feats) * per_row
    after = base + per_row
    tail = after + hid // fold
    rows[base:, :] = jnp.zeros((rows.shape[0] - base, LANES), F32)
    for q in range(per_row):
        cs = slice(q * LANES, (q + 1) * LANES)
        rows[pl.ds(q, half, stride=per_row), :] = g_low[:, cs]
        rows[pl.ds(half * per_row + q, feats, stride=per_row), :] = g_sum[:, cs]
        rows[base + q : base + q + 1, :] = g_in_b[:, cs]
    staged[...] = jnp.concatenate([g_out, jnp.zeros((hid, LANES - width), F32)], axis=1)
    packed = jnp.zeros((hid // fold, LANES), F32)
    for j in range(fold):
        packed = packed + turned(staged[pl.ds(j, hid // fold, stride=fold), :], j * width)
    rows[after:tail, :] = packed
    rows[tail : tail + 1, :] = jnp.concatenate(
        [g_out_b, jnp.zeros((1, LANES - width), F32)], axis=1
    )
    whole = rows[...]
    square[...] = jnp.sum(whole * whole, axis=0, keepdims=True)


def finish_kernel(count, mine, theirs, couple, square, out, whole):
    core = lax.axis_index("grp") % 2
    cells = mine.shape[0]
    per_row = mine.shape[1] // LANES
    for h in range(per_row):
        cs = slice(h * LANES, (h + 1) * LANES)
        whole[h, pl.ds(pl.multiple_of(core * cells, 8), cells), :] = mine[:, cs]
        whole[h, pl.ds(pl.multiple_of((1 - core) * cells, 8), cells), :] = theirs[:, cs]
    conv = whole[...]
    squares = jnp.sum(conv * conv) + jnp.sum(square[...])
    scale = -lax.rsqrt(jnp.full((1, 1), squares, F32) / count + EPSILON)
    for r in range(PH):
        for h in range(per_row):
            part = whole[h, pl.ds(r, PW, stride=PH), :]
            out[pl.ds(r * PW * per_row + h, PW, stride=per_row), :] = part * scale
    used = 2 * cells * per_row
    out[used : used + couple.shape[0], :] = couple[...] * scale


def neighbour(value, axis, step):
    count = lax.axis_size(axis)
    pairs = [(i, (i + step) % count) for i in range(count)]
    return lax.ppermute(value, axis, pairs)


def from_lat(value, step):
    count = lax.axis_size("lat")
    return lax.ppermute(value, "lat", [(i, i + step) for i in range(count) if 0 <= i + step < count])


def from_corner(value, lon_step, lat_step):
    lon, lat = lax.axis_size("lon"), lax.axis_size("lat")
    pairs = [
        (i * lat + j, (i + lon_step) % lon * lat + j + lat_step)
        for i in range(lon)
        for j in range(lat)
        if 0 <= j + lat_step < lat
    ]
    return lax.ppermute(value, ("lon", "lat"), pairs)


def swapped(value, axis, flip):
    count = lax.axis_size(axis)
    return lax.ppermute(value, axis, [(i, i ^ flip) for i in range(count)])


def flips(axis):
    count = lax.axis_size(axis)
    return [1 << i for i in range(count.bit_length() - 1)]


def shape(*dims, dtype=F32):
    return jax.ShapeDtypeStruct(dims, dtype)


def shards(
    sea_surface,
    velocity,
    levels,
    wind_basis,
    proposals,
    member_ids,
    conv_weight,
    couple_in,
    couple_in_bias,
    couple_out,
    couple_out_bias,
):
    members, rows, cols = sea_surface.shape
    lat_count, lon_count = lax.axis_size("lat"), lax.axis_size("lon")
    cells, feats = conv_weight.shape
    hid, width = couple_out.shape
    patches = cols // PW
    samples = STEPS * members
    groups = (4 * members + 2) * HALO
    height = rows + 2 * PAD
    inv_root = 1.0 / math.sqrt(rows // PH * (cols * lon_count // PW))

    force, low, high, side, low_c, high_c = pl.pallas_call(
        lambda *refs: pack_kernel(members, *refs),
        out_shape=(
            shape(members, rows, cols),
            shape(groups, cols, dtype=BF16),
            shape(groups, cols, dtype=BF16),
            shape(5 * rows, LANES, dtype=BF16),
            shape(6 * HALO, LANES, dtype=BF16),
            shape(6 * HALO, LANES, dtype=BF16),
        ),
        in_specs=[smem()] + [vmem()] * 5,
        out_specs=(vmem(),) * 6,
        compiler_params=params_of(16),
        name="pack_edges",
    )(member_ids, sea_surface, velocity, levels, wind_basis, proposals)

    south = from_lat(high, 1)
    north = from_lat(low, -1)
    west = neighbour(side, "lon", 1)
    south_west = from_corner(high_c, 1, 1)
    north_west = from_corner(low_c, 1, -1)
    if lon_count == 2:
        east, south_east, north_east = west, south_west, north_west
    else:
        east = neighbour(side, "lon", -1)
        south_east = from_corner(high_c, -1, 1)
        north_east = from_corner(low_c, -1, -1)

    planes = pl.pallas_call(
        lambda *refs: planar_kernel(members, *refs),
        out_shape=shape(5, PW, rows, LANES),
        in_specs=[vmem()] * 4,
        out_specs=vmem(),
        compiler_params=params_of(24),
        cost_estimate=pl.CostEstimate(flops=2 * 10**9, bytes_accessed=6 * MEBI, transcendentals=0),
        name="to_planes",
    )(sea_surface, velocity, force, levels)

    whole = lambda *dims: pl.BlockSpec(dims, lambda i: (0,) * len(dims))
    partial, gram, final = pl.pallas_call(
        lambda *refs: flow_kernel(members, rows, cols, lat_count, *refs),
        grid=(STEPS // 2,),
        out_shape=(
            shape(samples, feats),
            shape(samples, cells, feats),
            shape(3, PW, rows, LANES),
        ),
        in_specs=[
            whole(5, PW, rows, LANES),
            whole(groups, cols),
            whole(groups, cols),
            whole(5 * rows, LANES),
            whole(5 * rows, LANES),
            whole(5 * rows, LANES),
            whole(6 * HALO, LANES),
            whole(6 * HALO, LANES),
            whole(6 * HALO, LANES),
            whole(6 * HALO, LANES),
            whole(cells, feats),
        ],
        out_specs=(
            pl.BlockSpec((2 * members, feats), lambda i: (i, 0)),
            pl.BlockSpec((2 * members, cells, feats), lambda i: (i, 0, 0)),
            whole(3, PW, rows, LANES),
        ),
        scratch_shapes=[
            pltpu.VMEM((3, PW + 1, height, LANES), F32),
            pltpu.VMEM((3, PW + 1, height, LANES), F32),
            pltpu.VMEM((PW + 1, height, LANES), F32),
            pltpu.VMEM((PW + 1, height, LANES), F32),
            pltpu.VMEM((PW + 2, height, LANES), F32),
            pltpu.VMEM((PW + 1, height, LANES), F32),
            pltpu.VMEM((PW + 1, height, LANES), F32),
            pltpu.VMEM((height, LANES), F32),
            pltpu.VMEM((height, LANES), F32),
            pltpu.VMEM((feats // LANES, cells, LANES), F32),
            pltpu.VMEM((cells, feats), BF16),
            pltpu.VMEM((members, rows // PH * patches, cells), BF16),
            pltpu.VMEM((members, rows // PH * patches, feats), BF16),
        ],
        compiler_params=params_of(48),
        name="flow_embed",
    )(
        planes,
        south,
        north,
        side,
        east,
        west,
        south_east,
        south_west,
        north_east,
        north_west,
        conv_weight,
    )

    if lon_count == 2:
        others = swapped(partial, "lon", 1)
    else:
        others = lax.psum(partial, "lon") - partial

    surface_out, velocity_out = pl.pallas_call(
        lambda *refs: back_kernel(members, *refs),
        out_shape=(shape(members, rows, cols), shape(2, members, rows, cols)),
        in_specs=[vmem()],
        out_specs=(vmem(), vmem()),
        compiler_params=params_of(24),
        cost_estimate=pl.CostEstimate(flops=2 * 10**9, bytes_accessed=6 * MEBI, transcendentals=0),
        name="from_planes",
    )(final)

    ids_col = member_ids.reshape(-1, 1)
    b_in = couple_in_bias.reshape(1, -1)
    b_out = couple_out_bias.reshape(1, -1)
    summaries, kept, sent = pl.pallas_call(
        lambda *refs: local_kernel(members, inv_root, *refs),
        out_shape=(
            shape(samples, feats),
            shape(cells // 2, feats),
            shape(cells // 2, feats),
        ),
        in_specs=[vmem()] * 8 + [pl.BlockSpec(memory_space=pl.ANY)],
        out_specs=(vmem(),) * 3,
        scratch_shapes=[
            pltpu.VMEM((samples, cells, feats), F32),
            pltpu.VMEM((cells, feats), F32),
            pltpu.SemaphoreType.DMA,
        ],
        compiler_params=params_of(24),
        name="local_loss",
    )(partial, others, ids_col, proposals, couple_in, b_in, couple_out, b_out, gram)

    conv = kept + swapped(sent, "grp", 1)
    for axis in ("grp", "lon", "lat"):
        for flip in flips(axis):
            if axis != "grp" or flip > 1:
                conv = conv + swapped(conv, axis, flip)
    conv_other = swapped(conv, "grp", 1)

    gathered = summaries
    order = [0]
    for axis in ("grp", "lat"):
        for flip in flips(axis):
            if axis != "grp" or flip > 1:
                gathered = jnp.concatenate([gathered, swapped(gathered, axis, flip)], axis=0)
                order = order + [(o ^ flip if axis == "grp" else o) for o in order]
    gathered = jnp.concatenate([gathered, swapped(gathered, "grp", 1)], axis=0)
    order = order + [o ^ 1 for o in order]

    low_rows = (couple_in.size + hid + couple_out.size) // LANES + 1
    low_rows = -(-low_rows // 8) * 8
    count = cells * feats + couple_in.size + hid + couple_out.size + width
    couple, square = pl.pallas_call(
        lambda *refs: couple_kernel(members, samples, order, *refs),
        out_shape=(shape(low_rows, LANES), shape(1, LANES)),
        in_specs=[vmem()] * 7,
        out_specs=(vmem(), vmem()),
        scratch_shapes=[pltpu.VMEM((hid, LANES), F32)],
        compiler_params=params_of(32),
        cost_estimate=pl.CostEstimate(flops=3 * 10**9, bytes_accessed=3 * MEBI, transcendentals=0),
        name="couple_grads",
    )(gathered, ids_col, proposals, couple_in, b_in, couple_out, b_out)

    stepped = pl.pallas_call(
        lambda *refs: finish_kernel(count, *refs),
        out_shape=shape(cells * feats // LANES + low_rows, LANES),
        in_specs=[vmem()] * 4,
        out_specs=vmem(),
        scratch_shapes=[pltpu.VMEM((feats // LANES, cells, LANES), F32)],
        compiler_params=params_of(16),
        name="finish",
    )(conv, conv_other, couple, square)
    weight_step = stepped.reshape(-1)[:count]

    items = samples // lon_count
    own = lax.dynamic_slice_in_dim(summaries, lax.axis_index("lon") * items, items, axis=0)
    return (surface_out, velocity_out, own.reshape(1, 1, 1, items, feats), weight_step)


def solution(mesh):
    in_specs = (
        P("grp", "lat", "lon"),
        P(None, "grp", "lat", "lon"),
        P("lat", "lon"),
        P(None, "lat", "lon"),
        P(),
        P(),
        P(),
        P(),
        P(),
        P(),
        P(),
    )
    out_specs = (
        P("grp", "lat", "lon"),
        P(None, "grp", "lat", "lon"),
        P("lon", "lat", "grp", None, None),
        P(),
    )
    return jax.shard_map(shards, mesh=mesh, in_specs=in_specs, out_specs=out_specs, check_vma=False)
```

```python
import math

import jax
import jax.numpy as jnp
from jax import lax
from jax.experimental import pallas as pl
from jax.experimental.pallas import tpu as pltpu
from jax.sharding import PartitionSpec as P

STEPS = 8
NLEV = 50
PH = 8
PW = 16
HALO = 8
PAD = 16

GRAVITY = 0.45
DRAG_RATE = 0.02
CORI_BASE = 0.05
CORI_SLOPE = 0.1
WIND_SCALE = 0.05
EPSILON = 1e-06
PRECISE = lax.Precision.HIGHEST
F32 = jnp.float32
BF16 = jnp.bfloat16
LANES = 128
MEBI = 2**20


def vmem():
    return pl.BlockSpec(memory_space=pltpu.VMEM)


def smem():
    return pl.BlockSpec(memory_space=pltpu.SMEM)


def params_of(mebi, **rest):
    return pltpu.CompilerParams(vmem_limit_bytes=mebi * MEBI, **rest)


def lane_ids(rows):
    return lax.broadcasted_iota(jnp.int32, (rows, LANES), 1)


def plane_matrix(cols, inverse=False):
    patches = cols // PW
    src = lax.broadcasted_iota(jnp.int32, (cols, cols), 1 if inverse else 0)
    dst = lax.broadcasted_iota(jnp.int32, (cols, cols), 0 if inverse else 1)
    return jnp.where(src == (dst % patches) * PW + dst // patches, 1.0, 0.0).astype(BF16)


def moved(value, matrix):
    high = value.astype(BF16)
    rest = (value - high.astype(F32)).astype(BF16)
    return jnp.dot(high, matrix, preferred_element_type=F32) + jnp.dot(
        rest, matrix, preferred_element_type=F32
    )


def by_segment(pieces, segment):
    out = pieces[-1]
    for index in range(len(pieces) - 2, -1, -1):
        out = jnp.where(segment == index, pieces[index], out)
    return out


def turned(value, shift):
    shift = shift % LANES
    return value if shift == 0 else pltpu.roll(value, shift, 1)


def planes_from(parts, patches):
    rows = parts[0].shape[0]
    per = LANES // patches
    segment = lane_ids(rows) // patches
    planes = []
    for k in range(PW):
        group, place = divmod(k, per)
        block = slice(group * LANES, (group + 1) * LANES)
        planes.append(
            by_segment(
                [turned(part[:, block], (m - place) * patches) for m, part in enumerate(parts)],
                segment,
            )
        )
    return planes


def edges_of(firsts, lasts, patches):
    rows = firsts[0].shape[0]
    lane = lane_ids(rows)
    out = jnp.zeros((rows, LANES), F32)
    for m, (first, last) in enumerate(zip(firsts, lasts)):
        both = jnp.where(lane < HALO, first, turned(last, 2 * HALO))
        here = (lane >= m * patches) & (lane < m * patches + 2 * HALO)
        out = jnp.where(here, turned(both, m * patches), out)
    return out


def forcing_rows(coeff, basis, members):
    acc = [None] * members
    for k in range(basis.shape[0]):
        value = basis[k].astype(F32)
        for m in range(members):
            term = coeff[m][:, k : k + 1] * value
            acc[m] = term if acc[m] is None else acc[m] + term
    return acc


def coefficients(members, ids, props):
    base = lax.axis_index("grp") * members
    return [
        props[pl.ds(ids[base + m], 1), :].astype(BF16).astype(F32) * WIND_SCALE
        for m in range(members)
    ]


def pack_kernel(
    members, ids_in, sea, vel, levels, wind, props_in, low, high, ids, cells, depth, basis, props, sems
):
    rows, cols = levels.shape
    copies = [(ids_in, ids), (props_in, props)]
    ends = ((0, 0), (rows - HALO, rows - 16))
    for side, (r0, w0) in enumerate(ends):
        rs = pl.ds(r0, HALO)
        copies.append((sea.at[:, rs, :], cells.at[side, 0]))
        copies.append((vel.at[0, :, rs, :], cells.at[side, 1]))
        copies.append((vel.at[1, :, rs, :], cells.at[side, 2]))
        copies.append((levels.at[rs, :], depth.at[side]))
        copies.append((wind.at[:, pl.ds(w0, 16), :], basis.at[side]))
    started = [pltpu.make_async_copy(a, b, sems.at[n]) for n, (a, b) in enumerate(copies)]
    for copy in started:
        copy.start()
    for copy in started:
        copy.wait()
    coeff = coefficients(members, ids, props)
    for side, out in ((0, low), (1, high)):
        force = forcing_rows(coeff, basis.at[side], members)
        keep = slice(0, HALO) if side == 0 else slice(16 - HALO, 16)
        blocks = [cells[side, i, m] for i in range(3) for m in range(members)]
        blocks += [force[m][keep] for m in range(members)]
        blocks += [depth[side].astype(F32), jnp.zeros((HALO, cols), F32)]
        for g in range(0, len(blocks), 2):
            pair = jnp.concatenate(blocks[g : g + 2], axis=0)
            out[g * HALO : (g + 2) * HALO, :] = pair.astype(BF16)


def planar_kernel(members, ids, sea, vel, levels, wind, props, out, side):
    rows, cols = levels.shape
    patches = cols // PW
    coeff = coefficients(members, ids, props)
    strips = [
        forcing_rows(coeff, wind.at[:, pl.ds(r0, 16), :], members) for r0 in range(0, rows, 16)
    ]
    force = jnp.concatenate([strip[m] for m in range(members) for strip in strips], axis=0)
    depth = levels[...].astype(F32)
    matrix = plane_matrix(cols)
    scale = 1.0 / GRAVITY
    full = (members * rows, cols)
    fields = [sea[...].reshape(full), vel[0].reshape(full), vel[1].reshape(full), force, depth]
    for i, value in enumerate(fields):
        starts = [m * rows if i < 4 else 0 for m in range(members)]
        edge = edges_of(
            [value[r : r + rows, :LANES] for r in starts],
            [value[r : r + rows, cols - LANES :] for r in starts],
            patches,
        )
        side[i * rows : (i + 1) * rows, :] = edge.astype(BF16)
        if i < 4:
            spread = moved(value if i == 0 else value * scale, matrix)
        else:
            spread = jnp.dot(value.astype(BF16), matrix, preferred_element_type=F32)
        parts = [spread[r : r + rows] for r in starts]
        for k, plane in enumerate(planes_from(parts, patches)):
            out[i, k] = plane


def starts_of(i, members):
    if i < 4:
        return [(i * members + m) * HALO for m in range(members)]
    return [4 * members * HALO] * members


def rim_kernel(members, patches, south, north, side, out):
    rows = side.shape[0] // 5
    cols = south.shape[1]
    low, high = south[...].astype(F32), north[...].astype(F32)
    for i in range(5):
        ends = [
            edges_of(
                [plain[s : s + HALO, :LANES] for s in starts_of(i, members)],
                [plain[s : s + HALO, cols - LANES :] for s in starts_of(i, members)],
                patches,
            )
            for plain in (low, high)
        ]
        own = side[i * rows : (i + 1) * rows, :].astype(F32)
        whole = jnp.concatenate([ends[0], own, ends[1]], axis=0)
        out[i * whole.shape[0] : (i + 1) * whole.shape[0], :] = whole.astype(BF16)


def halo_kernel(members, south, north, out):
    cols = south.shape[1]
    matrix = plane_matrix(cols)
    for end, got in enumerate((south, north)):
        spread = jnp.dot(got[...], matrix, preferred_element_type=F32)
        for i in range(5):
            parts = [spread[s : s + HALO] for s in starts_of(i, members)]
            for k, plane in enumerate(planes_from(parts, cols // PW)):
                out[end, i, k] = plane if i in (0, 4) else plane * (1.0 / GRAVITY)


def back_kernel(members, state, sea, vel):
    rows, cols = sea.shape[1:]
    patches = cols // PW
    per = LANES // patches
    matrix = plane_matrix(cols, inverse=True)
    segment = lane_ids(rows) // patches
    for i in range(3):
        parts = []
        for m in range(members):
            groups = []
            for g in range(PW // per):
                pieces = [
                    turned(state[i, g * per + j, PAD : PAD + rows, :], (j - m) * patches)
                    for j in range(per)
                ]
                groups.append(by_segment(pieces, segment))
            parts.append(jnp.concatenate(groups, axis=1))
        value = moved(jnp.concatenate(parts, axis=0), matrix)
        for m in range(members):
            part = value[m * rows : (m + 1) * rows]
            if i == 0:
                sea[m] = part
            else:
                vel[i - 1, m] = part * GRAVITY


def flow_step(src, src_rim, dst, dst_rim, force, force_rim, hu, hv, hvu, cu, cv, last_mask, rows, patches):
    strip = PW
    end = PAD + rows + HALO
    half = (rows + 2 * HALO) // 2
    keep = 1.0 - DRAG_RATE
    for r0 in range(PAD - HALO, end, half):
        here, up, down = pl.ds(r0, half), pl.ds(r0 + 1, half), pl.ds(r0 - 1, half)
        last = lane_ids(half) % patches == patches - 1

        def wrap_left(plane, rim):
            return pltpu.roll(jnp.where(last, rim, plane), 1, 1)

        def wrap_right(plane, rim):
            return jnp.where(last, pltpu.roll(rim, PW - 1, 1), pltpu.roll(plane, LANES - 1, 1))

        def of(planes, rim, i, p):
            return rim.at[i] if p == strip else planes.at[i, p]

        def new_level(p, fx, fx_right):
            n_up = of(src, src_rim, 2, p)[up, :]
            n = of(src, src_rim, 2, p)[here, :]
            fy = hvu[p, here, :] * n_up - hv[p, here, :] * n
            level = of(src, src_rim, 0, p)[here, :] - ((fx_right - fx) + fy)
            of(dst, dst_rim, 0, p)[here, :] = level
            return level, n, n + n_up

        def new_flow(p, e, e_right, em, em_right, n, v, level, level_left):
            u = (e + e_right) + (em + em_right)
            push = force_rim[here, :] if p == strip else force[p, here, :]
            of(dst, dst_rim, 1, p)[here, :] = (
                keep * e + cu[here, :] * v - (level - level_left) + push
            )
            level_down = of(dst, dst_rim, 0, p)[down, :]
            north = keep * n - cv[here, :] * u - (level - level_down)
            home = of(dst, dst_rim, 2, p)
            if r0 + half == end:
                home[pl.ds(r0, half - HALO), :] = north[: half - HALO]
                home[pl.ds(end - HALO, HALO), :] = north[half - HALO :] * last_mask
            else:
                home[here, :] = north

        e_rim = src_rim[1, here, :]
        em_rim = src_rim[1, down, :]
        fx_rim = hu[strip, here, :] * e_rim
        level_rim, n_rim, vs_rim = new_level(strip, fx_rim, pltpu.roll(fx_rim, LANES - 1, 1))
        new_flow(
            strip,
            e_rim,
            pltpu.roll(e_rim, LANES - 1, 1),
            em_rim,
            pltpu.roll(em_rim, LANES - 1, 1),
            n_rim,
            vs_rim + pltpu.roll(vs_rim, 1, 1),
            level_rim,
            pltpu.roll(level_rim, 1, 1),
        )
        e_end = wrap_right(src[1, 0, here, :], e_rim)
        em_end = wrap_right(src[1, 0, down, :], em_rim)
        e_last = src[1, PW - 1, here, :]
        level_last, n_last, vs_last = new_level(
            PW - 1, hu[PW - 1, here, :] * e_last, hu[PW + 1, here, :] * e_end
        )
        level_left = wrap_left(level_last, level_rim)
        vs_left = wrap_left(vs_last, vs_rim)
        e = src[1, 0, here, :]
        em = src[1, 0, down, :]
        fx = hu[0, here, :] * e
        for p in range(PW):
            if p < PW - 1:
                e_right = src[1, p + 1, here, :]
                em_right = src[1, p + 1, down, :]
                fx_right = hu[p + 1, here, :] * e_right
                level, n, vs = new_level(p, fx, fx_right)
            else:
                e_right, em_right, fx_right = e_end, em_end, None
                level, n, vs = level_last, n_last, vs_last
            new_flow(p, e, e_right, em, em_right, n, vs + vs_left, level, level_left)
            level_left, vs_left, e, em, fx = level, vs, e_right, em_right, fx_right


def flow_kernel(
    members,
    rows,
    cols,
    lat_count,
    planes,
    halo,
    side,
    east,
    west,
    weight,
    partial,
    gram,
    state_a,
    state_b,
    force,
    depth,
    rim_a,
    rim_b,
    force_rim,
    depth_rim,
    hu,
    hv,
    hvu,
    cu,
    cv,
    w_rows,
    w_planes,
    patch_t,
    slope,
):
    patches = cols // PW
    lat = lax.axis_index("lat")
    strip = PW
    height = rows + 2 * PAD
    wide = rows + 2 * HALO
    scale = 1.0 / GRAVITY
    edge_rows = (slice(0, HALO), slice(height - HALO, height))
    for i in range(3):
        for rs in edge_rows:
            rim_a[i, rs, :] = jnp.zeros((HALO, LANES), F32)
            rim_b[i, rs, :] = jnp.zeros((HALO, LANES), F32)
            for p in range(PW):
                state_a[i, p, rs, :] = jnp.zeros((HALO, LANES), F32)
                state_b[i, p, rs, :] = jnp.zeros((HALO, LANES), F32)
    homes = (state_a.at[0], state_a.at[1], state_a.at[2], force, depth)
    for i, home in enumerate(homes):
        home[:, PAD : PAD + rows, :] = planes[i]
        home[:, PAD - HALO : PAD, :] = halo[0, i]
        home[:, PAD + rows : PAD + rows + HALO, :] = halo[1, i]
    for rs in edge_rows:
        depth_rim[rs, :] = jnp.zeros((HALO, LANES), F32)
        for p in range(PW):
            depth[p, rs, :] = jnp.zeros((HALO, LANES), F32)
    place = lane_ids(wide) % patches
    rim_homes = (rim_a.at[0], rim_a.at[1], rim_a.at[2], force_rim, depth_rim)
    for i, home in enumerate(rim_homes):
        rs = slice(i * wide, (i + 1) * wide)
        rim = jnp.where(
            place < 2 * HALO,
            side[rs, :].astype(F32),
            jnp.where(
                place < 3 * HALO,
                pltpu.roll(east[rs, :].astype(F32), 2 * HALO, 1),
                pltpu.roll(west[rs, :].astype(F32), LANES - 2 * HALO, 1),
            ),
        )
        home[PAD - HALO : PAD + rows + HALO, :] = rim * (1.0 if i in (0, 4) else scale)
    for h in range(w_rows.shape[0]):
        cs = slice(h * LANES, (h + 1) * LANES)
        w_rows[h] = weight[:, cs].astype(F32)
        w_planes[:, cs] = jnp.concatenate(
            [w_rows[h, pl.ds(k, PH, stride=PW), :] for k in range(PW)], axis=0
        ).astype(BF16)
    span = slice(PAD - HALO, PAD + rows + HALO)
    row = lax.broadcasted_iota(jnp.int32, (wide, LANES), 0) + (lat * rows - HALO)
    inside = (row >= 0) & (row < lat_count * rows)
    place = row.astype(F32)
    total = lat_count * rows
    cu[span, :] = jnp.where(
        inside, 0.25 * (CORI_BASE + CORI_SLOPE * (place + 0.5) / total), 0.0
    )
    cv[span, :] = jnp.where(inside, 0.25 * (CORI_BASE + CORI_SLOPE * place / total), 0.0)
    half_depth = 0.5 * GRAVITY / NLEV
    last = lane_ids(wide) % patches == patches - 1
    for p in range(PW + 1):
        home = depth_rim if p == strip else depth.at[p]
        here = home[span, :]
        if p == 0:
            left = pltpu.roll(jnp.where(last, depth_rim[span, :], depth[PW - 1, span, :]), 1, 1)
        elif p == strip:
            left = pltpu.roll(here, 1, 1)
        else:
            left = depth[p - 1, span, :]
        below = home[PAD - HALO - 1 : PAD + rows + HALO - 1, :]
        above = home[PAD - HALO + 1 : PAD + rows + HALO + 1, :]
        hu[p, span, :] = half_depth * (here + left)
        hv[p, span, :] = half_depth * (here + below)
        hvu[p, span, :] = jnp.where(inside, half_depth * (here + above), 0.0)
    hu[PW + 1, span, :] = jnp.where(
        last,
        pltpu.roll(hu[strip, span, :], PW - 1, 1),
        pltpu.roll(hu[0, span, :], LANES - 1, 1),
    )

    last_mask = jnp.where(lat < lat_count - 1, 1.0, 0.0)
    count = rows // PH

    def two_steps(turn, carry):
        for sub, (src, src_rim, dst, dst_rim) in enumerate(
            ((state_a, rim_a, state_b, rim_b), (state_b, rim_b, state_a, rim_a))
        ):
            flow_step(
                src, src_rim, dst, dst_rim, force, force_rim, hu, hv, hvu, cu, cv, last_mask, rows, patches
            )
            total = None
            for b in range(count):
                cells = dst[0, :, PAD + b * PH : PAD + (b + 1) * PH, :].reshape(PW * PH, LANES)
                cells_t = cells.T.astype(BF16)
                act = jnp.tanh(jnp.dot(cells_t, w_planes[...], preferred_element_type=F32))
                total = act if total is None else total + act
                fall = (1.0 - act * act).astype(BF16)
                for m in range(members):
                    rs = slice(m * patches, (m + 1) * patches)
                    to = slice(b * patches, (b + 1) * patches)
                    patch_t[m, to, :] = cells_t[rs]
                    slope[m, to, :] = fall[rs]
            sums = jnp.sum(total.reshape(members, patches, total.shape[1]), axis=1)
            partial[turn, sub * members : (sub + 1) * members, :] = sums
            for m in range(members):
                gram[(2 * turn + sub) * members + m] = lax.dot_general(
                    patch_t[m], slope[m], (((0,), (0,)), ((), ())), preferred_element_type=F32
                )
        return carry

    lax.fori_loop(0, STEPS // 2, two_steps, 0)


def split(value):
    high = value.astype(BF16)
    return high, (value - high.astype(F32)).astype(BF16)


def dot(a, b, ca=1, cb=0):
    return lax.dot_general(a, b, (((ca,), (cb,)), ((), ())), preferred_element_type=F32)


def mm(a, b, ca=1, cb=0):
    return dot(a[0], b[0], ca, cb) + (dot(a[0], b[1], ca, cb) + dot(a[1], b[0], ca, cb))


def member_params(ids_col, props):
    count = props.shape[0]
    hot = jnp.where(ids_col[...] == lax.broadcasted_iota(jnp.int32, (count, count), 1), 1.0, 0.0)
    return jnp.dot(hot, props[...], precision=PRECISE, preferred_element_type=F32)


def repeated(rows, count):
    return jnp.concatenate([rows] * count, axis=0)


def flow_grads(lower_in, upper, summary, w_in, w_out, b_out):
    half = upper.shape[1]
    width = 2 * half
    sums = split(summary)
    w_sum = split(w_in[half:, :])
    hidden = jnp.tanh(mm(sums, w_sum) + lower_in)
    hid = split(hidden)
    out_w = split(w_out[...])
    both = dot(hid[0], jnp.concatenate(out_w, axis=1))
    raw = both[:, :width] + both[:, width:] + dot(hid[1], out_w[0]) + b_out[...]
    log_scale = jnp.tanh(raw[:, :half])
    grown = upper * jnp.exp(log_scale)
    latent = grown + raw[:, half:]
    d_scale = (latent * grown - 1.0) * (1.0 - log_scale * log_scale)
    d_raw = jnp.concatenate([d_scale, latent], axis=1)
    d_r = split(d_raw)
    d_hidden = dot(
        jnp.concatenate([d_r[0], d_r[1], d_r[0]], axis=1),
        jnp.concatenate([out_w[0], out_w[0], out_w[1]], axis=1),
        1,
        1,
    )
    d_hidden = d_hidden * (1.0 - hidden * hidden)
    return sums, hid, d_raw, d_r, d_hidden, w_sum


def local_kernel(
    members, inv_root, mine, theirs, ids, props, w_in, b_in, w_out, b_out, gram, kept, sent, total
):
    sums = (mine[...] + theirs[...]) * inv_root
    count = sums.shape[0]
    params = member_params(ids, props)
    half = params.shape[1] // 2
    low = split(params[:, :half])
    low_in = mm(low, split(w_in[:half, :])) + b_in[...]
    slot = lax.broadcasted_iota(jnp.int32, (count, params.shape[0]), 1)
    row = lax.broadcasted_iota(jnp.int32, (count, params.shape[0]), 0)
    hot = jnp.where(slot == lax.axis_index("grp") * members + row % members, 1.0, 0.0)
    low_in = jnp.dot(hot, low_in, precision=PRECISE, preferred_element_type=F32)
    upper = jnp.dot(hot, params[:, half:], precision=PRECISE, preferred_element_type=F32)
    _, _, _, _, d_hidden, w_sum = flow_grads(low_in, upper, sums, w_in, w_out, b_out)
    d_summary = mm(split(d_hidden), w_sum, 1, 1) * inv_root
    acc = gram[0] * d_summary[0:1, :]
    for i in range(1, count):
        acc = acc + gram[i] * d_summary[i : i + 1, :]
    total[...] = acc
    cells = acc.shape[0] // 2
    core = lax.axis_index("grp") % 2
    kept[...] = total[pl.ds(pl.multiple_of(core * cells, 8), cells), :]
    sent[...] = total[pl.ds(pl.multiple_of((1 - core) * cells, 8), cells), :]


def couple_kernel(
    members, lat_count, grp_count, order, summary, ids, props, w_in, b_in, w_out, b_out, rows, square, sorted_sums, staged
):
    per = summary.shape[0] // len(order)
    for index, (lat_flip, grp_flip) in enumerate(order):
        block = (lax.axis_index("lat") ^ lat_flip) * grp_count + (lax.axis_index("grp") ^ grp_flip)
        sorted_sums[pl.ds(pl.multiple_of(block * per, per), per), :] = summary[
            index * per : (index + 1) * per, :
        ]
    params = member_params(ids, props)
    half = params.shape[1] // 2
    low_in = mm(split(params[:, :half]), split(w_in[:half, :])) + b_in[...]
    groups = [slice(g * members, (g + 1) * members) for g in range(grp_count)]
    steps = per // members
    spread = lambda value: jnp.concatenate(
        [repeated(value[rs], steps) for rs in groups] * lat_count, axis=0
    )
    lower = spread(params[:, :half])
    sums, hid, d_raw, d_r, d_hidden, _ = flow_grads(
        spread(low_in), spread(params[:, half:]), sorted_sums[...], w_in, w_out, b_out
    )
    low = split(lower)
    context = [jnp.concatenate([sums[n], low[n]], axis=1) for n in range(2)]
    g_in = mm(context, split(d_hidden), 0, 0)
    width = 2 * half
    both = dot(hid[0], jnp.concatenate(d_r, axis=1), 0, 0)
    g_out = both[:, :width] + both[:, width:] + dot(hid[1], d_r[0], 0, 0)
    g_in_b = jnp.sum(d_hidden, axis=0, keepdims=True)
    g_out_b = jnp.sum(d_raw, axis=0, keepdims=True)
    hidden = d_hidden.shape[1]
    per_row = hidden // LANES
    feats = summary.shape[1]
    fold = LANES // width
    base = (half + feats) * per_row
    after = base + per_row
    tail = after + hidden // fold
    rows[base:, :] = jnp.zeros((rows.shape[0] - base, LANES), F32)
    for q in range(per_row):
        cs = slice(q * LANES, (q + 1) * LANES)
        rows[pl.ds(q, half, stride=per_row), :] = g_in[feats:, cs]
        rows[pl.ds(half * per_row + q, feats, stride=per_row), :] = g_in[:feats, cs]
        rows[base + q : base + q + 1, :] = g_in_b[:, cs]
    staged[...] = jnp.concatenate([g_out, jnp.zeros((hidden, LANES - width), F32)], axis=1)
    packed = jnp.zeros((hidden // fold, LANES), F32)
    for j in range(fold):
        packed = packed + turned(staged[pl.ds(j, hidden // fold, stride=fold), :], j * width)
    rows[after:tail, :] = packed
    rows[tail : tail + 1, :] = jnp.concatenate(
        [g_out_b, jnp.zeros((1, LANES - width), F32)], axis=1
    )
    whole = rows[...]
    square[...] = jnp.sum(whole * whole, axis=0, keepdims=True)


def finish_kernel(count, mine, theirs, couple, square, out, whole):
    core = lax.axis_index("grp") % 2
    cells = mine.shape[0]
    per_row = mine.shape[1] // LANES
    for h in range(per_row):
        cs = slice(h * LANES, (h + 1) * LANES)
        whole[h, pl.ds(pl.multiple_of(core * cells, 8), cells), :] = mine[:, cs]
        whole[h, pl.ds(pl.multiple_of((1 - core) * cells, 8), cells), :] = theirs[:, cs]
    conv = whole[...]
    squares = jnp.sum(conv * conv) + jnp.sum(square[...])
    scale = -lax.rsqrt(jnp.full((1, 1), squares, F32) / count + EPSILON)
    for r in range(PH):
        for h in range(per_row):
            part = whole[h, pl.ds(r, PW, stride=PH), :]
            out[pl.ds(r * PW * per_row + h, PW, stride=per_row), :] = part * scale
    used = 2 * cells * per_row
    out[used : used + couple.shape[0], :] = couple[...] * scale


def neighbour(value, axis, step):
    count = lax.axis_size(axis)
    pairs = [(i, (i + step) % count) for i in range(count)]
    return lax.ppermute(value, axis, pairs)


def from_lat(value, step):
    count = lax.axis_size("lat")
    return lax.ppermute(value, "lat", [(i, i + step) for i in range(count) if 0 <= i + step < count])


def swapped(value, axis, flip):
    count = lax.axis_size(axis)
    return lax.ppermute(value, axis, [(i, i ^ flip) for i in range(count)])


def flips(axis):
    count = lax.axis_size(axis)
    return [1 << i for i in range(count.bit_length() - 1)]


def shape(*dims, dtype=F32):
    return jax.ShapeDtypeStruct(dims, dtype)


def shards(
    sea_surface,
    velocity,
    levels,
    wind_basis,
    proposals,
    member_ids,
    conv_weight,
    couple_in,
    couple_in_bias,
    couple_out,
    couple_out_bias,
):
    members, rows, cols = sea_surface.shape
    lat_count, lon_count = lax.axis_size("lat"), lax.axis_size("lon")
    grp_count = lax.axis_size("grp")
    cells, feats = conv_weight.shape
    hid, width = couple_out.shape
    patches = cols // PW
    samples = STEPS * members
    groups = (4 * members + 2) * HALO
    height = rows + 2 * PAD
    inv_root = 1.0 / math.sqrt(rows // PH * (cols * lon_count // PW))

    anywhere = pl.BlockSpec(memory_space=pl.ANY)
    low, high = pl.pallas_call(
        lambda *refs: pack_kernel(members, *refs),
        out_shape=(shape(groups, cols, dtype=BF16), shape(groups, cols, dtype=BF16)),
        in_specs=[anywhere] * 6,
        out_specs=(vmem(), vmem()),
        scratch_shapes=[
            pltpu.SMEM(member_ids.shape, jnp.int32),
            pltpu.VMEM((2, 3, members, HALO, cols), F32),
            pltpu.VMEM((2, HALO, cols), jnp.int32),
            pltpu.VMEM((2, wind_basis.shape[0], 16, cols), BF16),
            pltpu.VMEM(proposals.shape, F32),
            pltpu.SemaphoreType.DMA((12,)),
        ],
        compiler_params=params_of(60),
        name="pack_rows",
    )(member_ids, sea_surface, velocity, levels, wind_basis, proposals)

    south = from_lat(high, 1)
    north = from_lat(low, -1)

    planes, side = pl.pallas_call(
        lambda *refs: planar_kernel(members, *refs),
        out_shape=(shape(5, PW, rows, LANES), shape(5 * rows, LANES, dtype=BF16)),
        in_specs=[smem()] + [vmem()] * 5,
        out_specs=(vmem(), vmem()),
        compiler_params=params_of(32),
        cost_estimate=pl.CostEstimate(flops=2 * 10**9, bytes_accessed=6 * MEBI, transcendentals=0),
        name="to_planes",
    )(member_ids, sea_surface, velocity, levels, wind_basis, proposals)

    wide = rows + 2 * HALO
    rim = pl.pallas_call(
        lambda *refs: rim_kernel(members, patches, *refs),
        out_shape=shape(5 * wide, LANES, dtype=BF16),
        in_specs=[vmem()] * 3,
        out_specs=vmem(),
        compiler_params=params_of(16),
        name="rim",
    )(south, north, side)
    west = neighbour(rim, "lon", 1)
    east = west if lon_count == 2 else neighbour(rim, "lon", -1)

    halo = pl.pallas_call(
        lambda *refs: halo_kernel(members, *refs),
        out_shape=shape(2, 5, PW, HALO, LANES),
        in_specs=[vmem()] * 2,
        out_specs=vmem(),
        compiler_params=params_of(16),
        cost_estimate=pl.CostEstimate(flops=10**9, bytes_accessed=4 * MEBI, transcendentals=0),
        name="halo_planes",
    )(south, north)

    partial, gram, final = pl.pallas_call(
        lambda *refs: flow_kernel(members, rows, cols, lat_count, *refs),
        out_shape=(
            shape(STEPS // 2, 2 * members, feats),
            shape(samples, cells, feats),
            shape(3, PW, height, LANES),
        ),
        in_specs=[vmem()] * 6,
        out_specs=(vmem(),) * 3,
        scratch_shapes=[
            pltpu.VMEM((3, PW, height, LANES), F32),
            pltpu.VMEM((PW, height, LANES), F32),
            pltpu.VMEM((PW, height, LANES), F32),
            pltpu.VMEM((3, height, LANES), F32),
            pltpu.VMEM((3, height, LANES), F32),
            pltpu.VMEM((height, LANES), F32),
            pltpu.VMEM((height, LANES), F32),
            pltpu.VMEM((PW + 2, height, LANES), F32),
            pltpu.VMEM((PW + 1, height, LANES), F32),
            pltpu.VMEM((PW + 1, height, LANES), F32),
            pltpu.VMEM((height, LANES), F32),
            pltpu.VMEM((height, LANES), F32),
            pltpu.VMEM((feats // LANES, cells, LANES), F32),
            pltpu.VMEM((cells, feats), BF16),
            pltpu.VMEM((members, rows // PH * patches, cells), BF16),
            pltpu.VMEM((members, rows // PH * patches, feats), BF16),
        ],
        compiler_params=params_of(32),
        name="flow_embed",
    )(planes, halo, rim, east, west, conv_weight)
    partial = partial.reshape(samples, feats)

    if lon_count == 2:
        others = swapped(partial, "lon", 1)
    else:
        others = lax.psum(partial, "lon") - partial
    summaries = (partial + others) * inv_root

    ids_col = member_ids.reshape(-1, 1)
    b_in = couple_in_bias.reshape(1, -1)
    b_out = couple_out_bias.reshape(1, -1)
    kept, sent = pl.pallas_call(
        lambda *refs: local_kernel(members, inv_root, *refs),
        out_shape=(shape(cells // 2, feats), shape(cells // 2, feats)),
        in_specs=[vmem()] * 9,
        out_specs=(vmem(),) * 2,
        scratch_shapes=[pltpu.VMEM((cells, feats), F32)],
        compiler_params=params_of(16),
        name="local_loss",
    )(partial, others, ids_col, proposals, couple_in, b_in, couple_out, b_out, gram)

    conv = kept + swapped(sent, "grp", 1)
    if lon_count == 2:
        corner = lax.ppermute(
            conv,
            ("lon", "grp"),
            [(i, (i // grp_count ^ 1) * grp_count + (i % grp_count ^ 2)) for i in range(2 * grp_count)],
        )
        conv = (conv + swapped(conv, "lon", 1)) + (swapped(conv, "grp", 2) + corner)
    else:
        conv = conv + swapped(conv, "grp", 2)
        for flip in flips("lon"):
            conv = conv + swapped(conv, "lon", flip)
    for flip in reversed(flips("lat")):
        conv = conv + swapped(conv, "lat", flip)
    conv_other = swapped(conv, "grp", 1)

    gathered = summaries.astype(jnp.float16)
    order = [(0, 0)]
    for axis, flip in [("grp", 2)] + [("lat", f) for f in reversed(flips("lat"))] + [("grp", 1)]:
        gathered = jnp.concatenate([gathered, swapped(gathered, axis, flip)], axis=0)
        order = order + [(a ^ flip, b) if axis == "lat" else (a, b ^ flip) for a, b in order]

    low_rows = (couple_in.size + hid + couple_out.size) // LANES + 1
    low_rows = -(-low_rows // 8) * 8
    count = cells * feats + couple_in.size + hid + couple_out.size + width
    couple, square = pl.pallas_call(
        lambda *refs: couple_kernel(members, lat_count, grp_count, order, *refs),
        out_shape=(shape(low_rows, LANES), shape(1, LANES)),
        in_specs=[vmem()] * 7,
        out_specs=(vmem(), vmem()),
        scratch_shapes=[
            pltpu.VMEM((len(order) * samples, feats), F32),
            pltpu.VMEM((hid, LANES), F32),
        ],
        compiler_params=params_of(24),
        cost_estimate=pl.CostEstimate(flops=3 * 10**9, bytes_accessed=3 * MEBI, transcendentals=0),
        name="couple_grads",
    )(gathered.astype(F32), ids_col, proposals, couple_in, b_in, couple_out, b_out)

    surface_out, velocity_out = pl.pallas_call(
        lambda *refs: back_kernel(members, *refs),
        out_shape=(shape(members, rows, cols), shape(2, members, rows, cols)),
        in_specs=[vmem()],
        out_specs=(vmem(), vmem()),
        compiler_params=params_of(24),
        cost_estimate=pl.CostEstimate(flops=2 * 10**9, bytes_accessed=6 * MEBI, transcendentals=0),
        name="from_planes",
    )(final)

    stepped = pl.pallas_call(
        lambda *refs: finish_kernel(count, *refs),
        out_shape=shape(cells * feats // LANES + low_rows, LANES),
        in_specs=[vmem()] * 4,
        out_specs=vmem(),
        scratch_shapes=[pltpu.VMEM((feats // LANES, cells, LANES), F32)],
        compiler_params=params_of(16),
        name="finish",
    )(conv, conv_other, couple, square)
    weight_step = stepped.reshape(-1)[:count]

    items = samples // lon_count
    own = lax.dynamic_slice_in_dim(summaries, lax.axis_index("lon") * items, items, axis=0)
    return (surface_out, velocity_out, own.reshape(1, 1, 1, items, feats), weight_step)


def solution(mesh):
    in_specs = (
        P("grp", "lat", "lon"),
        P(None, "grp", "lat", "lon"),
        P("lat", "lon"),
        P(None, "lat", "lon"),
        P(),
        P(),
        P(),
        P(),
        P(),
        P(),
        P(),
    )
    out_specs = (
        P("grp", "lat", "lon"),
        P(None, "grp", "lat", "lon"),
        P("lon", "lat", "grp", None, None),
        P(),
    )
    return jax.shard_map(shards, mesh=mesh, in_specs=in_specs, out_specs=out_specs, check_vma=False)
```

```python
import math

import jax
import jax.numpy as jnp
from jax import lax
from jax.experimental import pallas as pl
from jax.experimental.pallas import tpu as pltpu
from jax.sharding import PartitionSpec as P

STEPS = 8
NLEV = 50
PH = 8
PW = 16
HALO = 8
PAD = 16

GRAVITY = 0.45
DRAG_RATE = 0.02
CORI_BASE = 0.05
CORI_SLOPE = 0.1
WIND_SCALE = 0.05
EPSILON = 1e-06
PRECISE = lax.Precision.HIGHEST
F32 = jnp.float32
BF16 = jnp.bfloat16
LANES = 128
MEBI = 2**20


def vmem():
    return pl.BlockSpec(memory_space=pltpu.VMEM)


def smem():
    return pl.BlockSpec(memory_space=pltpu.SMEM)


def params_of(mebi, **rest):
    return pltpu.CompilerParams(vmem_limit_bytes=mebi * MEBI, **rest)


def lane_ids(rows):
    return lax.broadcasted_iota(jnp.int32, (rows, LANES), 1)


def plane_matrix(cols, inverse=False):
    patches = cols // PW
    src = lax.broadcasted_iota(jnp.int32, (cols, cols), 1 if inverse else 0)
    dst = lax.broadcasted_iota(jnp.int32, (cols, cols), 0 if inverse else 1)
    return jnp.where(src == (dst % patches) * PW + dst // patches, 1.0, 0.0).astype(BF16)


def moved(value, matrix):
    high = value.astype(BF16)
    rest = (value - high.astype(F32)).astype(BF16)
    return jnp.dot(high, matrix, preferred_element_type=F32) + jnp.dot(
        rest, matrix, preferred_element_type=F32
    )


def by_segment(pieces, segment):
    out = pieces[-1]
    for index in range(len(pieces) - 2, -1, -1):
        out = jnp.where(segment == index, pieces[index], out)
    return out


def turned(value, shift):
    shift = shift % LANES
    return value if shift == 0 else pltpu.roll(value, shift, 1)


def planes_from(parts, patches):
    rows = parts[0].shape[0]
    per = LANES // patches
    segment = lane_ids(rows) // patches
    planes = []
    for k in range(PW):
        group, place = divmod(k, per)
        block = slice(group * LANES, (group + 1) * LANES)
        planes.append(
            by_segment(
                [turned(part[:, block], (m - place) * patches) for m, part in enumerate(parts)],
                segment,
            )
        )
    return planes


def edges_of(firsts, lasts, patches):
    rows = firsts[0].shape[0]
    lane = lane_ids(rows)
    out = jnp.zeros((rows, LANES), F32)
    for m, (first, last) in enumerate(zip(firsts, lasts)):
        both = jnp.where(lane < HALO, first, turned(last, 2 * HALO))
        here = (lane >= m * patches) & (lane < m * patches + 2 * HALO)
        out = jnp.where(here, turned(both, m * patches), out)
    return out


def forcing_rows(coeff, basis, members, keep=slice(None)):
    acc = [None] * members
    for k in range(basis.shape[0]):
        value = basis[k].astype(F32)[keep]
        for m in range(members):
            term = coeff[m][:, k : k + 1] * value
            acc[m] = term if acc[m] is None else acc[m] + term
    return acc


def coefficients(members, ids, props):
    base = lax.axis_index("grp") * members
    return [
        props[pl.ds(ids[base + m], 1), :].astype(BF16).astype(F32) * WIND_SCALE
        for m in range(members)
    ]


def pack_kernel(
    members, ids_in, sea, vel, levels, wind, props_in, low, high, ids, cells, depth, basis, props, sems
):
    rows, cols = levels.shape
    copies = [(ids_in, ids), (props_in, props)]
    ends = ((0, 0), (rows - HALO, rows - 16))
    for side, (r0, w0) in enumerate(ends):
        rs = pl.ds(r0, HALO)
        copies.append((sea.at[:, rs, :], cells.at[side, 0]))
        copies.append((vel.at[0, :, rs, :], cells.at[side, 1]))
        copies.append((vel.at[1, :, rs, :], cells.at[side, 2]))
        copies.append((levels.at[rs, :], depth.at[side]))
        copies.append((wind.at[:, pl.ds(w0, 16), :], basis.at[side]))
    started = [pltpu.make_async_copy(a, b, sems.at[n]) for n, (a, b) in enumerate(copies)]
    for copy in started:
        copy.start()
    for copy in started:
        copy.wait()
    coeff = coefficients(members, ids, props)
    for side, out in ((0, low), (1, high)):
        keep = slice(0, HALO) if side == 0 else slice(16 - HALO, 16)
        force = forcing_rows(coeff, basis.at[side], members, keep)
        blocks = [cells[side, i, m] for i in range(3) for m in range(members)]
        blocks += force
        blocks += [depth[side].astype(F32), jnp.zeros((HALO, cols), F32)]
        for g in range(0, len(blocks), 2):
            pair = jnp.concatenate(blocks[g : g + 2], axis=0)
            out[g * HALO : (g + 2) * HALO, :] = pair.astype(BF16)


def planar_kernel(members, ids, sea, vel, levels, wind, props, out, side):
    rows, cols = levels.shape
    patches = cols // PW
    coeff = coefficients(members, ids, props)
    strips = [
        forcing_rows(coeff, wind.at[:, pl.ds(r0, 16), :], members) for r0 in range(0, rows, 16)
    ]
    force = jnp.concatenate([strip[m] for m in range(members) for strip in strips], axis=0)
    depth = levels[...].astype(F32)
    matrix = plane_matrix(cols)
    scale = 1.0 / GRAVITY
    full = (members * rows, cols)
    fields = [sea[...].reshape(full), vel[0].reshape(full), vel[1].reshape(full), force, depth]
    for i, value in enumerate(fields):
        starts = [m * rows if i < 4 else 0 for m in range(members)]
        edge = edges_of(
            [value[r : r + rows, :LANES] for r in starts],
            [value[r : r + rows, cols - LANES :] for r in starts],
            patches,
        )
        side[i * rows : (i + 1) * rows, :] = edge.astype(BF16)
        if i < 4:
            spread = moved(value if i == 0 else value * scale, matrix)
        else:
            spread = jnp.dot(value.astype(BF16), matrix, preferred_element_type=F32)
        parts = [spread[r : r + rows] for r in starts]
        for k, plane in enumerate(planes_from(parts, patches)):
            out[i, k] = plane


def starts_of(i, members):
    if i < 4:
        return [(i * members + m) * HALO for m in range(members)]
    return [4 * members * HALO] * members


def rim_kernel(members, patches, south, north, side, out):
    rows = side.shape[0] // 5
    cols = south.shape[1]
    low, high = south[...].astype(F32), north[...].astype(F32)
    for i in range(5):
        ends = [
            edges_of(
                [plain[s : s + HALO, :LANES] for s in starts_of(i, members)],
                [plain[s : s + HALO, cols - LANES :] for s in starts_of(i, members)],
                patches,
            )
            for plain in (low, high)
        ]
        own = side[i * rows : (i + 1) * rows, :].astype(F32)
        whole = jnp.concatenate([ends[0], own, ends[1]], axis=0)
        out[i * whole.shape[0] : (i + 1) * whole.shape[0], :] = whole.astype(BF16)


def halo_kernel(members, south, north, out):
    cols = south.shape[1]
    matrix = plane_matrix(cols)
    for end, got in enumerate((south, north)):
        spread = jnp.dot(got[...], matrix, preferred_element_type=F32)
        for i in range(5):
            parts = [spread[s : s + HALO] for s in starts_of(i, members)]
            for k, plane in enumerate(planes_from(parts, cols // PW)):
                out[end, i, k] = plane if i in (0, 4) else plane * (1.0 / GRAVITY)


def back_kernel(members, state, sea, vel):
    rows, cols = sea.shape[1:]
    patches = cols // PW
    per = LANES // patches
    matrix = plane_matrix(cols, inverse=True)
    segment = lane_ids(rows) // patches
    for i in range(3):
        parts = []
        for m in range(members):
            groups = []
            for g in range(PW // per):
                pieces = [
                    turned(state[i, g * per + j, PAD : PAD + rows, :], (j - m) * patches)
                    for j in range(per)
                ]
                groups.append(by_segment(pieces, segment))
            parts.append(jnp.concatenate(groups, axis=1))
        value = moved(jnp.concatenate(parts, axis=0), matrix)
        for m in range(members):
            part = value[m * rows : (m + 1) * rows]
            if i == 0:
                sea[m] = part
            else:
                vel[i - 1, m] = part * GRAVITY


def flow_step(src, src_rim, dst, dst_rim, force, force_rim, hu, hv, hvu, cu, cv, last_mask, rows, patches):
    strip = PW
    end = PAD + rows + HALO
    half = (rows + 2 * HALO) // 2
    keep = 1.0 - DRAG_RATE
    for r0 in range(PAD - HALO, end, half):
        here, up, down = pl.ds(r0, half), pl.ds(r0 + 1, half), pl.ds(r0 - 1, half)
        last = lane_ids(half) % patches == patches - 1

        def wrap_left(plane, rim):
            return pltpu.roll(jnp.where(last, rim, plane), 1, 1)

        def wrap_right(plane, rim):
            return jnp.where(last, pltpu.roll(rim, PW - 1, 1), pltpu.roll(plane, LANES - 1, 1))

        def of(planes, rim, i, p):
            return rim.at[i] if p == strip else planes.at[i, p]

        def new_level(p, fx, fx_right):
            n_up = of(src, src_rim, 2, p)[up, :]
            n = of(src, src_rim, 2, p)[here, :]
            fy = hvu[p, here, :] * n_up - hv[p, here, :] * n
            level = of(src, src_rim, 0, p)[here, :] - ((fx_right - fx) + fy)
            of(dst, dst_rim, 0, p)[here, :] = level
            return level, n, n + n_up

        def new_flow(p, e, e_right, em, em_right, n, v, level, level_left):
            u = (e + e_right) + (em + em_right)
            push = force_rim[here, :] if p == strip else force[p, here, :]
            of(dst, dst_rim, 1, p)[here, :] = (
                keep * e + cu[here, :] * v - (level - level_left) + push
            )
            level_down = of(dst, dst_rim, 0, p)[down, :]
            north = keep * n - cv[here, :] * u - (level - level_down)
            home = of(dst, dst_rim, 2, p)
            if r0 + half == end:
                home[pl.ds(r0, half - HALO), :] = north[: half - HALO]
                home[pl.ds(end - HALO, HALO), :] = north[half - HALO :] * last_mask
            else:
                home[here, :] = north

        e_rim = src_rim[1, here, :]
        em_rim = src_rim[1, down, :]
        fx_rim = hu[strip, here, :] * e_rim
        level_rim, n_rim, vs_rim = new_level(strip, fx_rim, pltpu.roll(fx_rim, LANES - 1, 1))
        new_flow(
            strip,
            e_rim,
            pltpu.roll(e_rim, LANES - 1, 1),
            em_rim,
            pltpu.roll(em_rim, LANES - 1, 1),
            n_rim,
            vs_rim + pltpu.roll(vs_rim, 1, 1),
            level_rim,
            pltpu.roll(level_rim, 1, 1),
        )
        e_end = wrap_right(src[1, 0, here, :], e_rim)
        em_end = wrap_right(src[1, 0, down, :], em_rim)
        e_last = src[1, PW - 1, here, :]
        level_last, n_last, vs_last = new_level(
            PW - 1, hu[PW - 1, here, :] * e_last, hu[PW + 1, here, :] * e_end
        )
        level_left = wrap_left(level_last, level_rim)
        vs_left = wrap_left(vs_last, vs_rim)
        e = src[1, 0, here, :]
        em = src[1, 0, down, :]
        fx = hu[0, here, :] * e
        for p in range(PW):
            if p < PW - 1:
                e_right = src[1, p + 1, here, :]
                em_right = src[1, p + 1, down, :]
                fx_right = hu[p + 1, here, :] * e_right
                level, n, vs = new_level(p, fx, fx_right)
            else:
                e_right, em_right, fx_right = e_end, em_end, None
                level, n, vs = level_last, n_last, vs_last
            new_flow(p, e, e_right, em, em_right, n, vs + vs_left, level, level_left)
            level_left, vs_left, e, em, fx = level, vs, e_right, em_right, fx_right


def flow_kernel(
    members,
    rows,
    cols,
    lat_count,
    planes,
    halo,
    side,
    east,
    west,
    weight,
    partial,
    gram,
    state_a,
    state_b,
    force,
    depth,
    rim_a,
    rim_b,
    force_rim,
    depth_rim,
    hu,
    hv,
    hvu,
    cu,
    cv,
    w_rows,
    w_planes,
    patch_t,
    slope,
):
    patches = cols // PW
    lat = lax.axis_index("lat")
    strip = PW
    height = rows + 2 * PAD
    wide = rows + 2 * HALO
    scale = 1.0 / GRAVITY
    edge_rows = (slice(0, HALO), slice(height - HALO, height))
    for i in range(3):
        for rs in edge_rows:
            rim_a[i, rs, :] = jnp.zeros((HALO, LANES), F32)
            rim_b[i, rs, :] = jnp.zeros((HALO, LANES), F32)
            for p in range(PW):
                state_a[i, p, rs, :] = jnp.zeros((HALO, LANES), F32)
                state_b[i, p, rs, :] = jnp.zeros((HALO, LANES), F32)
    homes = (state_a.at[0], state_a.at[1], state_a.at[2], force, depth)
    for i, home in enumerate(homes):
        home[:, PAD : PAD + rows, :] = planes[i]
        home[:, PAD - HALO : PAD, :] = halo[0, i]
        home[:, PAD + rows : PAD + rows + HALO, :] = halo[1, i]
    for rs in edge_rows:
        depth_rim[rs, :] = jnp.zeros((HALO, LANES), F32)
        for p in range(PW):
            depth[p, rs, :] = jnp.zeros((HALO, LANES), F32)
    place = lane_ids(wide) % patches
    rim_homes = (rim_a.at[0], rim_a.at[1], rim_a.at[2], force_rim, depth_rim)
    for i, home in enumerate(rim_homes):
        rs = slice(i * wide, (i + 1) * wide)
        rim = jnp.where(
            place < 2 * HALO,
            side[rs, :].astype(F32),
            jnp.where(
                place < 3 * HALO,
                pltpu.roll(east[rs, :].astype(F32), 2 * HALO, 1),
                pltpu.roll(west[rs, :].astype(F32), LANES - 2 * HALO, 1),
            ),
        )
        home[PAD - HALO : PAD + rows + HALO, :] = rim * (1.0 if i in (0, 4) else scale)
    for h in range(w_rows.shape[0]):
        cs = slice(h * LANES, (h + 1) * LANES)
        w_rows[h] = weight[:, cs].astype(F32)
        w_planes[:, cs] = jnp.concatenate(
            [w_rows[h, pl.ds(k, PH, stride=PW), :] for k in range(PW)], axis=0
        ).astype(BF16)
    span = slice(PAD - HALO, PAD + rows + HALO)
    row = lax.broadcasted_iota(jnp.int32, (wide, LANES), 0) + (lat * rows - HALO)
    inside = (row >= 0) & (row < lat_count * rows)
    place = row.astype(F32)
    total = lat_count * rows
    cu[span, :] = jnp.where(
        inside, 0.25 * (CORI_BASE + CORI_SLOPE * (place + 0.5) / total), 0.0
    )
    cv[span, :] = jnp.where(inside, 0.25 * (CORI_BASE + CORI_SLOPE * place / total), 0.0)
    half_depth = 0.5 * GRAVITY / NLEV
    last = lane_ids(wide) % patches == patches - 1
    for p in range(PW + 1):
        home = depth_rim if p == strip else depth.at[p]
        here = home[span, :]
        if p == 0:
            left = pltpu.roll(jnp.where(last, depth_rim[span, :], depth[PW - 1, span, :]), 1, 1)
        elif p == strip:
            left = pltpu.roll(here, 1, 1)
        else:
            left = depth[p - 1, span, :]
        below = home[PAD - HALO - 1 : PAD + rows + HALO - 1, :]
        above = home[PAD - HALO + 1 : PAD + rows + HALO + 1, :]
        hu[p, span, :] = half_depth * (here + left)
        hv[p, span, :] = half_depth * (here + below)
        hvu[p, span, :] = jnp.where(inside, half_depth * (here + above), 0.0)
    hu[PW + 1, span, :] = jnp.where(
        last,
        pltpu.roll(hu[strip, span, :], PW - 1, 1),
        pltpu.roll(hu[0, span, :], LANES - 1, 1),
    )

    last_mask = jnp.where(lat < lat_count - 1, 1.0, 0.0)
    count = rows // PH

    def two_steps(turn, carry):
        for sub, (src, src_rim, dst, dst_rim) in enumerate(
            ((state_a, rim_a, state_b, rim_b), (state_b, rim_b, state_a, rim_a))
        ):
            flow_step(
                src, src_rim, dst, dst_rim, force, force_rim, hu, hv, hvu, cu, cv, last_mask, rows, patches
            )
            total = None
            for b in range(count):
                cells = dst[0, :, PAD + b * PH : PAD + (b + 1) * PH, :].reshape(PW * PH, LANES)
                cells_t = cells.T.astype(BF16)
                act = jnp.tanh(jnp.dot(cells_t, w_planes[...], preferred_element_type=F32))
                total = act if total is None else total + act
                fall = (1.0 - act * act).astype(BF16)
                for m in range(members):
                    rs = slice(m * patches, (m + 1) * patches)
                    to = slice(b * patches, (b + 1) * patches)
                    patch_t[m, to, :] = cells_t[rs]
                    slope[m, to, :] = fall[rs]
            sums = jnp.sum(total.reshape(members, patches, total.shape[1]), axis=1)
            partial[turn, sub * members : (sub + 1) * members, :] = sums
            for m in range(members):
                gram[(2 * turn + sub) * members + m] = lax.dot_general(
                    patch_t[m], slope[m], (((0,), (0,)), ((), ())), preferred_element_type=F32
                )
        return carry

    lax.fori_loop(0, STEPS // 2, two_steps, 0)


def split(value):
    high = value.astype(BF16)
    return high, (value - high.astype(F32)).astype(BF16)


def dot(a, b, ca=1, cb=0):
    return lax.dot_general(a, b, (((ca,), (cb,)), ((), ())), preferred_element_type=F32)


def mm(a, b, ca=1, cb=0):
    return dot(a[0], b[0], ca, cb) + (dot(a[0], b[1], ca, cb) + dot(a[1], b[0], ca, cb))


def member_params(ids_col, props):
    count = props.shape[0]
    hot = jnp.where(ids_col[...] == lax.broadcasted_iota(jnp.int32, (count, count), 1), 1.0, 0.0)
    return jnp.dot(hot, props[...], precision=PRECISE, preferred_element_type=F32)


def repeated(rows, count):
    return jnp.concatenate([rows] * count, axis=0)


def flow_grads(lower_in, upper, summary, w_in, w_out, b_out):
    half = upper.shape[1]
    width = 2 * half
    sums = split(summary)
    w_sum = split(w_in[half:, :])
    hidden = jnp.tanh(mm(sums, w_sum) + lower_in)
    hid = split(hidden)
    out_w = split(w_out[...])
    both = dot(hid[0], jnp.concatenate(out_w, axis=1))
    raw = both[:, :width] + both[:, width:] + dot(hid[1], out_w[0]) + b_out[...]
    log_scale = jnp.tanh(raw[:, :half])
    grown = upper * jnp.exp(log_scale)
    latent = grown + raw[:, half:]
    d_scale = (latent * grown - 1.0) * (1.0 - log_scale * log_scale)
    d_raw = jnp.concatenate([d_scale, latent], axis=1)
    d_r = split(d_raw)
    d_hidden = dot(
        jnp.concatenate([d_r[0], d_r[1], d_r[0]], axis=1),
        jnp.concatenate([out_w[0], out_w[0], out_w[1]], axis=1),
        1,
        1,
    )
    d_hidden = d_hidden * (1.0 - hidden * hidden)
    return sums, hid, d_raw, d_r, d_hidden, w_sum


def local_kernel(
    members, inv_root, mine, theirs, ids, props, w_in, b_in, w_out, b_out, gram, kept, sent, own, total
):
    sums = (mine[...] + theirs[...]) * inv_root
    count = sums.shape[0]
    items = own.shape[0]
    for part in range(count // items):

        @pl.when(lax.axis_index("lon") == part)
        def _():
            own[...] = sums[part * items : (part + 1) * items, :]

    params = member_params(ids, props)
    half = params.shape[1] // 2
    low = split(params[:, :half])
    low_in = mm(low, split(w_in[:half, :])) + b_in[...]
    slot = lax.broadcasted_iota(jnp.int32, (count, params.shape[0]), 1)
    row = lax.broadcasted_iota(jnp.int32, (count, params.shape[0]), 0)
    hot = jnp.where(slot == lax.axis_index("grp") * members + row % members, 1.0, 0.0)
    low_in = jnp.dot(hot, low_in, precision=PRECISE, preferred_element_type=F32)
    upper = jnp.dot(hot, params[:, half:], precision=PRECISE, preferred_element_type=F32)
    _, _, _, _, d_hidden, w_sum = flow_grads(low_in, upper, sums, w_in, w_out, b_out)
    d_summary = mm(split(d_hidden), w_sum, 1, 1) * inv_root
    acc = gram[0] * d_summary[0:1, :]
    for i in range(1, count):
        acc = acc + gram[i] * d_summary[i : i + 1, :]
    total[...] = acc
    cells = acc.shape[0] // 2
    core = lax.axis_index("grp") % 2
    kept[...] = total[pl.ds(pl.multiple_of(core * cells, 8), cells), :]
    sent[...] = total[pl.ds(pl.multiple_of((1 - core) * cells, 8), cells), :]


def couple_kernel(
    members, lat_count, grp_count, order, summary, ids, props, w_in, b_in, w_out, b_out, rows, square, sorted_sums, staged
):
    per = summary.shape[0] // len(order)
    for index, (lat_flip, grp_flip) in enumerate(order):
        block = (lax.axis_index("lat") ^ lat_flip) * grp_count + (lax.axis_index("grp") ^ grp_flip)
        sorted_sums[pl.ds(pl.multiple_of(block * per, per), per), :] = summary[
            index * per : (index + 1) * per, :
        ]
    params = member_params(ids, props)
    half = params.shape[1] // 2
    low_in = mm(split(params[:, :half]), split(w_in[:half, :])) + b_in[...]
    groups = [slice(g * members, (g + 1) * members) for g in range(grp_count)]
    steps = per // members
    spread = lambda value: jnp.concatenate(
        [repeated(value[rs], steps) for rs in groups] * lat_count, axis=0
    )
    lower = spread(params[:, :half])
    sums, hid, d_raw, d_r, d_hidden, _ = flow_grads(
        spread(low_in), spread(params[:, half:]), sorted_sums[...], w_in, w_out, b_out
    )
    low = split(lower)
    context = [jnp.concatenate([sums[n], low[n]], axis=1) for n in range(2)]
    g_in = mm(context, split(d_hidden), 0, 0)
    width = 2 * half
    both = dot(hid[0], jnp.concatenate(d_r, axis=1), 0, 0)
    g_out = both[:, :width] + both[:, width:] + dot(hid[1], d_r[0], 0, 0)
    g_in_b = jnp.sum(d_hidden, axis=0, keepdims=True)
    g_out_b = jnp.sum(d_raw, axis=0, keepdims=True)
    hidden = d_hidden.shape[1]
    per_row = hidden // LANES
    feats = summary.shape[1]
    fold = LANES // width
    base = (half + feats) * per_row
    after = base + per_row
    tail = after + hidden // fold
    rows[base:, :] = jnp.zeros((rows.shape[0] - base, LANES), F32)
    for q in range(per_row):
        cs = slice(q * LANES, (q + 1) * LANES)
        rows[pl.ds(q, half, stride=per_row), :] = g_in[feats:, cs]
        rows[pl.ds(half * per_row + q, feats, stride=per_row), :] = g_in[:feats, cs]
        rows[base + q : base + q + 1, :] = g_in_b[:, cs]
    staged[...] = jnp.concatenate([g_out, jnp.zeros((hidden, LANES - width), F32)], axis=1)
    packed = jnp.zeros((hidden // fold, LANES), F32)
    for j in range(fold):
        packed = packed + turned(staged[pl.ds(j, hidden // fold, stride=fold), :], j * width)
    rows[after:tail, :] = packed
    rows[tail : tail + 1, :] = jnp.concatenate(
        [g_out_b, jnp.zeros((1, LANES - width), F32)], axis=1
    )
    whole = rows[...]
    square[...] = jnp.sum(whole * whole, axis=0, keepdims=True)


def finish_kernel(count, mine, theirs, couple, square, out, whole):
    core = lax.axis_index("grp") % 2
    cells = mine.shape[0]
    per_row = mine.shape[1] // LANES
    for h in range(per_row):
        cs = slice(h * LANES, (h + 1) * LANES)
        whole[h, pl.ds(pl.multiple_of(core * cells, 8), cells), :] = mine[:, cs]
        whole[h, pl.ds(pl.multiple_of((1 - core) * cells, 8), cells), :] = theirs[:, cs]
    conv = whole[...]
    squares = jnp.sum(conv * conv) + jnp.sum(square[...])
    scale = -lax.rsqrt(jnp.full((1, 1), squares, F32) / count + EPSILON)
    for r in range(PH):
        for h in range(per_row):
            part = whole[h, pl.ds(r, PW, stride=PH), :]
            out[pl.ds(r * PW * per_row + h, PW, stride=per_row), :] = part * scale
    used = 2 * cells * per_row
    out[used : used + couple.shape[0], :] = couple[...] * scale


def neighbour(value, axis, step):
    count = lax.axis_size(axis)
    pairs = [(i, (i + step) % count) for i in range(count)]
    return lax.ppermute(value, axis, pairs)


def from_lat(value, step):
    count = lax.axis_size("lat")
    return lax.ppermute(value, "lat", [(i, i + step) for i in range(count) if 0 <= i + step < count])


def swapped(value, axis, flip):
    count = lax.axis_size(axis)
    return lax.ppermute(value, axis, [(i, i ^ flip) for i in range(count)])


def flips(axis):
    count = lax.axis_size(axis)
    return [1 << i for i in range(count.bit_length() - 1)]


def shape(*dims, dtype=F32):
    return jax.ShapeDtypeStruct(dims, dtype)


def shards(
    sea_surface,
    velocity,
    levels,
    wind_basis,
    proposals,
    member_ids,
    conv_weight,
    couple_in,
    couple_in_bias,
    couple_out,
    couple_out_bias,
):
    members, rows, cols = sea_surface.shape
    lat_count, lon_count = lax.axis_size("lat"), lax.axis_size("lon")
    grp_count = lax.axis_size("grp")
    cells, feats = conv_weight.shape
    hid, width = couple_out.shape
    patches = cols // PW
    samples = STEPS * members
    groups = (4 * members + 2) * HALO
    height = rows + 2 * PAD
    inv_root = 1.0 / math.sqrt(rows // PH * (cols * lon_count // PW))

    anywhere = pl.BlockSpec(memory_space=pl.ANY)
    low, high = pl.pallas_call(
        lambda *refs: pack_kernel(members, *refs),
        out_shape=(shape(groups, cols, dtype=BF16), shape(groups, cols, dtype=BF16)),
        in_specs=[anywhere] * 6,
        out_specs=(vmem(), vmem()),
        scratch_shapes=[
            pltpu.SMEM(member_ids.shape, jnp.int32),
            pltpu.VMEM((2, 3, members, HALO, cols), F32),
            pltpu.VMEM((2, HALO, cols), jnp.int32),
            pltpu.VMEM((2, wind_basis.shape[0], 16, cols), BF16),
            pltpu.VMEM(proposals.shape, F32),
            pltpu.SemaphoreType.DMA((12,)),
        ],
        compiler_params=params_of(60),
        name="pack_rows",
    )(member_ids, sea_surface, velocity, levels, wind_basis, proposals)

    south = from_lat(high, 1)
    north = from_lat(low, -1)

    planes, side = pl.pallas_call(
        lambda *refs: planar_kernel(members, *refs),
        out_shape=(shape(5, PW, rows, LANES), shape(5 * rows, LANES, dtype=BF16)),
        in_specs=[smem()] + [vmem()] * 5,
        out_specs=(vmem(), vmem()),
        compiler_params=params_of(32),
        cost_estimate=pl.CostEstimate(flops=2 * 10**9, bytes_accessed=6 * MEBI, transcendentals=0),
        name="to_planes",
    )(member_ids, sea_surface, velocity, levels, wind_basis, proposals)

    wide = rows + 2 * HALO
    rim = pl.pallas_call(
        lambda *refs: rim_kernel(members, patches, *refs),
        out_shape=shape(5 * wide, LANES, dtype=BF16),
        in_specs=[vmem()] * 3,
        out_specs=vmem(),
        compiler_params=params_of(16),
        name="rim",
    )(south, north, side)
    west = neighbour(rim, "lon", 1)
    east = west if lon_count == 2 else neighbour(rim, "lon", -1)

    halo = pl.pallas_call(
        lambda *refs: halo_kernel(members, *refs),
        out_shape=shape(2, 5, PW, HALO, LANES),
        in_specs=[vmem()] * 2,
        out_specs=vmem(),
        compiler_params=params_of(16),
        cost_estimate=pl.CostEstimate(flops=10**9, bytes_accessed=4 * MEBI, transcendentals=0),
        name="halo_planes",
    )(south, north)

    partial, gram, final = pl.pallas_call(
        lambda *refs: flow_kernel(members, rows, cols, lat_count, *refs),
        out_shape=(
            shape(STEPS // 2, 2 * members, feats),
            shape(samples, cells, feats),
            shape(3, PW, height, LANES),
        ),
        in_specs=[vmem()] * 6,
        out_specs=(vmem(),) * 3,
        scratch_shapes=[
            pltpu.VMEM((3, PW, height, LANES), F32),
            pltpu.VMEM((PW, height, LANES), F32),
            pltpu.VMEM((PW, height, LANES), F32),
            pltpu.VMEM((3, height, LANES), F32),
            pltpu.VMEM((3, height, LANES), F32),
            pltpu.VMEM((height, LANES), F32),
            pltpu.VMEM((height, LANES), F32),
            pltpu.VMEM((PW + 2, height, LANES), F32),
            pltpu.VMEM((PW + 1, height, LANES), F32),
            pltpu.VMEM((PW + 1, height, LANES), F32),
            pltpu.VMEM((height, LANES), F32),
            pltpu.VMEM((height, LANES), F32),
            pltpu.VMEM((feats // LANES, cells, LANES), F32),
            pltpu.VMEM((cells, feats), BF16),
            pltpu.VMEM((members, rows // PH * patches, cells), BF16),
            pltpu.VMEM((members, rows // PH * patches, feats), BF16),
        ],
        compiler_params=params_of(32),
        name="flow_embed",
    )(planes, halo, rim, east, west, conv_weight)
    partial = partial.reshape(samples, feats)

    if lon_count == 2:
        others = swapped(partial, "lon", 1)
    else:
        others = lax.psum(partial, "lon") - partial
    surface_out, velocity_out = pl.pallas_call(
        lambda *refs: back_kernel(members, *refs),
        out_shape=(shape(members, rows, cols), shape(2, members, rows, cols)),
        in_specs=[vmem()],
        out_specs=(vmem(), vmem()),
        compiler_params=params_of(24),
        cost_estimate=pl.CostEstimate(flops=2 * 10**9, bytes_accessed=6 * MEBI, transcendentals=0),
        name="from_planes",
    )(final)

    others, surface_out, velocity_out = lax.optimization_barrier((others, surface_out, velocity_out))
    summaries = (partial + others) * inv_root

    ids_col = member_ids.reshape(-1, 1)
    b_in = couple_in_bias.reshape(1, -1)
    b_out = couple_out_bias.reshape(1, -1)
    items = samples // lon_count
    kept, sent, own = pl.pallas_call(
        lambda *refs: local_kernel(members, inv_root, *refs),
        out_shape=(shape(cells // 2, feats), shape(cells // 2, feats), shape(items, feats)),
        in_specs=[vmem()] * 9,
        out_specs=(vmem(),) * 3,
        scratch_shapes=[pltpu.VMEM((cells, feats), F32)],
        compiler_params=params_of(16),
        name="local_loss",
    )(partial, others, ids_col, proposals, couple_in, b_in, couple_out, b_out, gram)

    def after(value, *others):
        return lax.optimization_barrier((value,) + others)[0]

    def gather(axis, flip):
        both = jnp.concatenate([gathered, swapped(gathered, axis, flip)], axis=0)
        return both, order + [(a ^ flip, b) if axis == "lat" else (a, b ^ flip) for a, b in order]

    gathered, order = summaries.astype(jnp.float16), [(0, 0)]
    gathered, order = gather("grp", 2)
    conv = kept + swapped(sent, "grp", 1)
    if lon_count == 2:
        corner = lax.ppermute(
            conv,
            ("lon", "grp"),
            [(i, (i // grp_count ^ 1) * grp_count + (i % grp_count ^ 2)) for i in range(2 * grp_count)],
        )
        by_lon = swapped(conv, "lon", 1)
        gathered = after(gathered, by_lon)
        conv = (conv + by_lon) + (swapped(conv, "grp", 2) + corner)
    else:
        conv = conv + swapped(conv, "grp", 2)
        for flip in flips("lon"):
            conv = conv + swapped(conv, "lon", flip)
    for flip in reversed(flips("lat")):
        by_lat = swapped(conv, "lat", flip)
        if flip > 1:
            gathered, order = gather("lat", flip)
            gathered = after(gathered, conv)
            conv = conv + by_lat
    gathered, order = gather("lat", 1)
    gathered = after(gathered, conv)
    gathered, order = gather("grp", 1)

    low_rows = (couple_in.size + hid + couple_out.size) // LANES + 1
    low_rows = -(-low_rows // 8) * 8
    count = cells * feats + couple_in.size + hid + couple_out.size + width
    couple, square = pl.pallas_call(
        lambda *refs: couple_kernel(members, lat_count, grp_count, order, *refs),
        out_shape=(shape(low_rows, LANES), shape(1, LANES)),
        in_specs=[vmem()] * 7,
        out_specs=(vmem(), vmem()),
        scratch_shapes=[
            pltpu.VMEM((len(order) * samples, feats), F32),
            pltpu.VMEM((hid, LANES), F32),
        ],
        compiler_params=params_of(24),
        cost_estimate=pl.CostEstimate(flops=3 * 10**9, bytes_accessed=3 * MEBI, transcendentals=0),
        name="couple_grads",
    )(gathered.astype(F32), ids_col, proposals, couple_in, b_in, couple_out, b_out)

    conv = conv + after(by_lat, couple, square)
    conv_other = swapped(conv, "grp", 1)

    stepped = pl.pallas_call(
        lambda *refs: finish_kernel(count, *refs),
        out_shape=shape(cells * feats // LANES + low_rows, LANES),
        in_specs=[vmem()] * 4,
        out_specs=vmem(),
        scratch_shapes=[pltpu.VMEM((feats // LANES, cells, LANES), F32)],
        compiler_params=params_of(16),
        name="finish",
    )(conv, conv_other, couple, square)
    weight_step = stepped.reshape(-1)[:count]

    return (surface_out, velocity_out, own.reshape(1, 1, 1, items, feats), weight_step)


def solution(mesh):
    in_specs = (
        P("grp", "lat", "lon"),
        P(None, "grp", "lat", "lon"),
        P("lat", "lon"),
        P(None, "lat", "lon"),
        P(),
        P(),
        P(),
        P(),
        P(),
        P(),
        P(),
    )
    out_specs = (
        P("grp", "lat", "lon"),
        P(None, "grp", "lat", "lon"),
        P("lon", "lat", "grp", None, None),
        P(),
    )
    return jax.shard_map(shards, mesh=mesh, in_specs=in_specs, out_specs=out_specs, check_vma=False)
```

```python
import math

import jax
import jax.numpy as jnp
from jax import lax
from jax.experimental import pallas as pl
from jax.experimental.pallas import tpu as pltpu
from jax.sharding import PartitionSpec as P

STEPS = 8
NLEV = 50
PH = 8
PW = 16
HALO = 8
PAD = 16

GRAVITY = 0.45
DRAG_RATE = 0.02
CORI_BASE = 0.05
CORI_SLOPE = 0.1
WIND_SCALE = 0.05
EPSILON = 1e-06
PRECISE = lax.Precision.HIGHEST
F32 = jnp.float32
BF16 = jnp.bfloat16
LANES = 128
MEBI = 2**20
HALF_DEPTH = 0.5 * GRAVITY / NLEV


def vmem():
    return pl.BlockSpec(memory_space=pltpu.VMEM)


def smem():
    return pl.BlockSpec(memory_space=pltpu.SMEM)


def params_of(mebi, **rest):
    return pltpu.CompilerParams(vmem_limit_bytes=mebi * MEBI, **rest)


def lane_ids(rows):
    return lax.broadcasted_iota(jnp.int32, (rows, LANES), 1)


def plane_matrix(cols, inverse=False):
    patches = cols // PW
    src = lax.broadcasted_iota(jnp.int32, (cols, cols), 1 if inverse else 0)
    dst = lax.broadcasted_iota(jnp.int32, (cols, cols), 0 if inverse else 1)
    return jnp.where(src == (dst % patches) * PW + dst // patches, 1.0, 0.0).astype(BF16)


def moved(value, matrix):
    high = value.astype(BF16)
    rest = (value - high.astype(F32)).astype(BF16)
    return jnp.dot(high, matrix, preferred_element_type=F32) + jnp.dot(
        rest, matrix, preferred_element_type=F32
    )


def by_segment(pieces, segment):
    out = pieces[-1]
    for index in range(len(pieces) - 2, -1, -1):
        out = jnp.where(segment == index, pieces[index], out)
    return out


def turned(value, shift):
    shift = shift % LANES
    return value if shift == 0 else pltpu.roll(value, shift, 1)


def planes_from(parts, patches):
    rows = parts[0].shape[0]
    per = LANES // patches
    segment = lane_ids(rows) // patches
    planes = []
    for k in range(PW):
        group, place = divmod(k, per)
        block = slice(group * LANES, (group + 1) * LANES)
        planes.append(
            by_segment(
                [turned(part[:, block], (m - place) * patches) for m, part in enumerate(parts)],
                segment,
            )
        )
    return planes


def edges_of(firsts, lasts, patches):
    rows = firsts[0].shape[0]
    lane = lane_ids(rows)
    out = jnp.zeros((rows, LANES), F32)
    for m, (first, last) in enumerate(zip(firsts, lasts)):
        both = jnp.where(lane < HALO, first, turned(last, 2 * HALO))
        here = (lane >= m * patches) & (lane < m * patches + 2 * HALO)
        out = jnp.where(here, turned(both, m * patches), out)
    return out


def forcing_rows(coeff, basis, members, keep=slice(None)):
    acc = [None] * members
    for k in range(basis.shape[0]):
        value = basis[k].astype(F32)[keep]
        for m in range(members):
            term = coeff[m][:, k : k + 1] * value
            acc[m] = term if acc[m] is None else acc[m] + term
    return acc


def coefficients(members, ids, props):
    base = lax.axis_index("grp") * members
    return [
        props[pl.ds(ids[base + m], 1), :].astype(BF16).astype(F32) * WIND_SCALE
        for m in range(members)
    ]


def pack_kernel(
    members, ids_in, sea, vel, levels, wind, props_in, low, high, ids, cells, depth, basis, props, sems
):
    rows, cols = levels.shape
    copies = [(ids_in, ids), (props_in, props)]
    ends = ((0, 0), (rows - HALO, rows - 16))
    for side, (r0, w0) in enumerate(ends):
        rs = pl.ds(r0, HALO)
        copies.append((sea.at[:, rs, :], cells.at[side, 0]))
        copies.append((vel.at[0, :, rs, :], cells.at[side, 1]))
        copies.append((vel.at[1, :, rs, :], cells.at[side, 2]))
        copies.append((levels.at[rs, :], depth.at[side]))
        copies.append((wind.at[:, pl.ds(w0, 16), :], basis.at[side]))
    started = [pltpu.make_async_copy(a, b, sems.at[n]) for n, (a, b) in enumerate(copies)]
    for copy in started:
        copy.start()
    for copy in started:
        copy.wait()
    coeff = coefficients(members, ids, props)
    for side, out in ((0, low), (1, high)):
        keep = slice(0, HALO) if side == 0 else slice(16 - HALO, 16)
        force = forcing_rows(coeff, basis.at[side], members, keep)
        blocks = [cells[side, i, m] for i in range(3) for m in range(members)]
        blocks += force
        blocks += [depth[side].astype(F32), jnp.zeros((HALO, cols), F32)]
        for g in range(0, len(blocks), 2):
            pair = jnp.concatenate(blocks[g : g + 2], axis=0)
            out[g * HALO : (g + 2) * HALO, :] = pair.astype(BF16)


def planar_kernel(members, ids, sea, vel, levels, wind, props, out, side):
    rows, cols = levels.shape
    patches = cols // PW
    coeff = coefficients(members, ids, props)
    strips = [
        forcing_rows(coeff, wind.at[:, pl.ds(r0, 16), :], members) for r0 in range(0, rows, 16)
    ]
    force = jnp.concatenate([strip[m] for m in range(members) for strip in strips], axis=0)
    depth = levels[...].astype(F32)
    matrix = plane_matrix(cols)
    scale = 1.0 / GRAVITY
    full = (members * rows, cols)
    fields = [sea[...].reshape(full), vel[0].reshape(full), vel[1].reshape(full), force, depth]
    for i, value in enumerate(fields):
        starts = [m * rows if i < 4 else 0 for m in range(members)]
        edge = edges_of(
            [value[r : r + rows, :LANES] for r in starts],
            [value[r : r + rows, cols - LANES :] for r in starts],
            patches,
        )
        side[i * rows : (i + 1) * rows, :] = edge.astype(BF16)
        if i < 4:
            spread = moved(value if i == 0 else value * scale, matrix)
        else:
            spread = jnp.dot(value.astype(BF16), matrix, preferred_element_type=F32)
        parts = [spread[r : r + rows] for r in starts]
        for k, plane in enumerate(planes_from(parts, patches)):
            out[i, k] = plane


def starts_of(i, members):
    if i < 4:
        return [(i * members + m) * HALO for m in range(members)]
    return [4 * members * HALO] * members


def rim_kernel(members, patches, south, north, side, out):
    rows = side.shape[0] // 5
    cols = south.shape[1]
    low, high = south[...].astype(F32), north[...].astype(F32)
    wholes = []
    for i in range(5):
        ends = [
            edges_of(
                [plain[s : s + HALO, :LANES] for s in starts_of(i, members)],
                [plain[s : s + HALO, cols - LANES :] for s in starts_of(i, members)],
                patches,
            )
            for plain in (low, high)
        ]
        own = side[i * rows : (i + 1) * rows, :].astype(F32)
        wholes.append(jnp.concatenate([ends[0], own, ends[1]], axis=0))
    wide = rows + 2 * HALO
    for n, i in enumerate((0, 2, 4)):
        pair = wholes[i]
        if i + 1 < len(wholes):
            pair = pair + pltpu.roll(wholes[i + 1], 2 * HALO, 1)
        out[n * wide : (n + 1) * wide, :] = pair.astype(BF16)


def rims_of(own, from_east, from_west, patches):
    place = lane_ids(own.shape[0]) % patches
    out = []
    for shift in (0, 2 * HALO):
        out.append(
            jnp.where(
                place < 2 * HALO,
                turned(own, -shift),
                jnp.where(
                    place < 3 * HALO,
                    turned(from_east, 2 * HALO - shift),
                    turned(from_west, -2 * HALO - shift),
                ),
            )
        )
    return out


def prepare_kernel(
    members, rows, cols, lat_count, south, north, planes, weight, state, force, ends, hu, hv, hvu, cu, cv, w_planes, depth, w_rows
):
    patches = cols // PW
    height = rows + 2 * PAD
    wide = rows + 2 * HALO
    edge_rows = (slice(0, HALO), slice(height - HALO, height))
    homes = (state.at[0], state.at[1], state.at[2], force, depth)
    for i, home in enumerate(homes):
        home[:, PAD : PAD + rows, :] = planes[i]
        if i != 3:
            for p in range(PW):
                for rs in edge_rows:
                    home[p, rs, :] = jnp.zeros((HALO, LANES), F32)
    matrix = plane_matrix(cols)
    for got, r0 in ((south, PAD - HALO), (north, PAD + rows)):
        spread = jnp.dot(got[...], matrix, preferred_element_type=F32)
        for i, home in enumerate(homes):
            parts = [spread[s : s + HALO] for s in starts_of(i, members)]
            for k, plane in enumerate(planes_from(parts, patches)):
                home[k, r0 : r0 + HALO, :] = plane if i in (0, 4) else plane * (1.0 / GRAVITY)
    span = slice(PAD - HALO, PAD + rows + HALO)
    row, inside = row_ids(rows, lat_count)
    place = row.astype(F32)
    total = lat_count * rows
    cu[span, :] = jnp.where(inside, 0.25 * (CORI_BASE + CORI_SLOPE * (place + 0.5) / total), 0.0)
    cv[span, :] = jnp.where(inside, 0.25 * (CORI_BASE + CORI_SLOPE * place / total), 0.0)
    for p in range(PW):
        here = depth[p, span, :]
        if p > 0:
            hu[p, span, :] = HALF_DEPTH * (here + depth[p - 1, span, :])
        vertical(depth.at[p], hv.at[p], hvu.at[p], inside, rows)
    ends[0] = depth[0]
    ends[1] = depth[PW - 1]
    for h in range(w_rows.shape[0]):
        cs = slice(h * LANES, (h + 1) * LANES)
        w_rows[h] = weight[:, cs].astype(F32)
        w_planes[:, cs] = jnp.concatenate(
            [w_rows[h, pl.ds(k, PH, stride=PW), :] for k in range(PW)], axis=0
        ).astype(BF16)


def row_ids(rows, lat_count):
    wide = rows + 2 * HALO
    row = lax.broadcasted_iota(jnp.int32, (wide, LANES), 0) + (lax.axis_index("lat") * rows - HALO)
    return row, (row >= 0) & (row < lat_count * rows)


def vertical(depth, hv, hvu, inside, rows):
    span = slice(PAD - HALO, PAD + rows + HALO)
    here = depth[span, :]
    below = depth[PAD - HALO - 1 : PAD + rows + HALO - 1, :]
    above = depth[PAD - HALO + 1 : PAD + rows + HALO + 1, :]
    hv[span, :] = HALF_DEPTH * (here + below)
    hvu[span, :] = jnp.where(inside, HALF_DEPTH * (here + above), 0.0)


def back_kernel(members, state, sea, vel):
    rows, cols = sea.shape[1:]
    patches = cols // PW
    per = LANES // patches
    matrix = plane_matrix(cols, inverse=True)
    segment = lane_ids(rows) // patches
    for i in range(3):
        parts = []
        for m in range(members):
            groups = []
            for g in range(PW // per):
                pieces = [
                    turned(state[i, g * per + j, PAD : PAD + rows, :], (j - m) * patches)
                    for j in range(per)
                ]
                groups.append(by_segment(pieces, segment))
            parts.append(jnp.concatenate(groups, axis=1))
        value = moved(jnp.concatenate(parts, axis=0), matrix)
        for m in range(members):
            part = value[m * rows : (m + 1) * rows]
            if i == 0:
                sea[m] = part
            else:
                vel[i - 1, m] = part * GRAVITY


def flow_step(src, src_rim, dst, dst_rim, force, force_rim, hus, hvs, hvus, cu, cv, last_mask, rows, patches):
    strip = PW
    end = PAD + rows + HALO
    half = (rows + 2 * HALO) // 2
    keep = 1.0 - DRAG_RATE
    for r0 in range(PAD - HALO, end, half):
        here, up, down = pl.ds(r0, half), pl.ds(r0 + 1, half), pl.ds(r0 - 1, half)
        last = lane_ids(half) % patches == patches - 1

        def wrap_left(plane, rim):
            return pltpu.roll(jnp.where(last, rim, plane), 1, 1)

        def wrap_right(plane, rim):
            return jnp.where(last, pltpu.roll(rim, PW - 1, 1), pltpu.roll(plane, LANES - 1, 1))

        def of(planes, rim, i, p):
            return rim.at[i] if p == strip else planes.at[i, p]

        def new_level(p, fx, fx_right):
            n_up = of(src, src_rim, 2, p)[up, :]
            n = of(src, src_rim, 2, p)[here, :]
            fy = hvus[p][here, :] * n_up - hvs[p][here, :] * n
            level = of(src, src_rim, 0, p)[here, :] - ((fx_right - fx) + fy)
            of(dst, dst_rim, 0, p)[here, :] = level
            return level, n, n + n_up

        def new_flow(p, e, e_right, em, em_right, n, v, level, level_left):
            u = (e + e_right) + (em + em_right)
            push = force_rim[here, :] if p == strip else force[p, here, :]
            of(dst, dst_rim, 1, p)[here, :] = (
                keep * e + cu[here, :] * v - (level - level_left) + push
            )
            level_down = of(dst, dst_rim, 0, p)[down, :]
            north = keep * n - cv[here, :] * u - (level - level_down)
            home = of(dst, dst_rim, 2, p)
            if r0 + half == end:
                home[pl.ds(r0, half - HALO), :] = north[: half - HALO]
                home[pl.ds(end - HALO, HALO), :] = north[half - HALO :] * last_mask
            else:
                home[here, :] = north

        e_rim = src_rim[1, here, :]
        em_rim = src_rim[1, down, :]
        fx_rim = hus[strip][here, :] * e_rim
        level_rim, n_rim, vs_rim = new_level(strip, fx_rim, pltpu.roll(fx_rim, LANES - 1, 1))
        new_flow(
            strip,
            e_rim,
            pltpu.roll(e_rim, LANES - 1, 1),
            em_rim,
            pltpu.roll(em_rim, LANES - 1, 1),
            n_rim,
            vs_rim + pltpu.roll(vs_rim, 1, 1),
            level_rim,
            pltpu.roll(level_rim, 1, 1),
        )
        e_end = wrap_right(src[1, 0, here, :], e_rim)
        em_end = wrap_right(src[1, 0, down, :], em_rim)
        e_last = src[1, PW - 1, here, :]
        level_last, n_last, vs_last = new_level(
            PW - 1, hus[PW - 1][here, :] * e_last, hus[PW + 1][here, :] * e_end
        )
        level_left = wrap_left(level_last, level_rim)
        vs_left = wrap_left(vs_last, vs_rim)
        e = src[1, 0, here, :]
        em = src[1, 0, down, :]
        fx = hus[0][here, :] * e
        for p in range(PW):
            if p < PW - 1:
                e_right = src[1, p + 1, here, :]
                em_right = src[1, p + 1, down, :]
                fx_right = hus[p + 1][here, :] * e_right
                level, n, vs = new_level(p, fx, fx_right)
            else:
                e_right, em_right, fx_right = e_end, em_end, None
                level, n, vs = level_last, n_last, vs_last
            new_flow(p, e, e_right, em, em_right, n, vs + vs_left, level, level_left)
            level_left, vs_left, e, em, fx = level, vs, e_right, em_right, fx_right
            yield


def flow_kernel(
    members,
    rows,
    cols,
    lat_count,
    state,
    force,
    ends,
    hu,
    hv,
    hvu,
    cu,
    cv,
    w_planes,
    side,
    east,
    west,
    partial,
    gram,
    final,
    state_b,
    rim_a,
    rim_b,
    force_rim,
    depth_rim,
    hu_rim,
    hv_rim,
    hvu_rim,
    patch_t,
    slope,
    state_a,
):
    patches = cols // PW
    lat = lax.axis_index("lat")
    height = rows + 2 * PAD
    wide = rows + 2 * HALO
    span = slice(PAD - HALO, PAD + rows + HALO)
    state_a[...] = state[...]
    for rs in (slice(0, HALO), slice(height - HALO, height)):
        depth_rim[rs, :] = jnp.zeros((HALO, LANES), F32)
        for i in range(3):
            rim_a[i, rs, :] = jnp.zeros((HALO, LANES), F32)
            rim_b[i, rs, :] = jnp.zeros((HALO, LANES), F32)
            for p in range(PW):
                state_b[i, p, rs, :] = jnp.zeros((HALO, LANES), F32)
    rim_homes = (rim_a.at[0], rim_a.at[1], rim_a.at[2], force_rim, depth_rim)
    for n in range(3):
        rs = slice(n * wide, (n + 1) * wide)
        got = [ref[rs, :].astype(F32) for ref in (side, east, west)]
        for i, rim in zip((2 * n, 2 * n + 1), rims_of(*got, patches)):
            if i < len(rim_homes):
                rim_homes[i][span, :] = rim if i in (0, 4) else rim * (1.0 / GRAVITY)
    _, inside = row_ids(rows, lat_count)
    last = lane_ids(wide) % patches == patches - 1
    rim = depth_rim[span, :]
    left = pltpu.roll(jnp.where(last, rim, ends[1, span, :]), 1, 1)
    first = HALF_DEPTH * (ends[0, span, :] + left)
    rim = HALF_DEPTH * (rim + pltpu.roll(rim, 1, 1))
    hu_rim[0, span, :] = first
    hu_rim[1, span, :] = rim
    hu_rim[2, span, :] = jnp.where(
        last, pltpu.roll(rim, PW - 1, 1), pltpu.roll(first, LANES - 1, 1)
    )
    vertical(depth_rim, hv_rim, hvu_rim, inside, rows)
    hus = [hu_rim.at[0]] + [hu.at[p] for p in range(1, PW)] + [hu_rim.at[1], hu_rim.at[2]]
    hvs = [hv.at[p] for p in range(PW)] + [hv_rim]
    hvus = [hvu.at[p] for p in range(PW)] + [hvu_rim]

    last_mask = jnp.where(lat < lat_count - 1, 1.0, 0.0)
    count = rows // PH

    def embed_step(state, turn, sub):
        step = 2 * turn + sub
        total = None
        for b in range(count):
            cells = state[0, :, PAD + b * PH : PAD + (b + 1) * PH, :].reshape(PW * PH, LANES)
            cells_t = cells.T.astype(BF16)
            act = jnp.tanh(jnp.dot(cells_t, w_planes[...], preferred_element_type=F32))
            total = act if total is None else total + act
            fall = (1.0 - act * act).astype(BF16)
            for m in range(members):
                rs = slice(m * patches, (m + 1) * patches)
                to = slice(b * patches, (b + 1) * patches)
                patch_t[m, to, :] = cells_t[rs]
                slope[m, to, :] = fall[rs]
            yield
        sums = jnp.sum(total.reshape(members, patches, total.shape[1]), axis=1)
        partial[turn, sub * members : (sub + 1) * members, :] = sums
        for m in range(members):
            gram[step * members + m] = lax.dot_general(
                patch_t[m], slope[m], (((0,), (0,)), ((), ())), preferred_element_type=F32
            )
            yield

    def beside(flow, embed):
        for n, _ in enumerate(flow):
            if n % 3 == 2:
                next(embed, None)
        for _ in embed:
            pass

    def step_of(src, src_rim, dst, dst_rim):
        return flow_step(
            src, src_rim, dst, dst_rim, force, force_rim, hus, hvs, hvus, cu, cv, last_mask, rows, patches
        )

    def two_steps(turn, carry):
        beside(
            step_of(state_a, rim_a, state_b, rim_b),
            embed_step(state_a, jnp.maximum(turn - 1, 0), 1),
        )
        beside(step_of(state_b, rim_b, state_a, rim_a), embed_step(state_b, turn, 0))
        return carry

    lax.fori_loop(0, STEPS // 2, two_steps, 0)
    final[...] = state_a[...]
    for _ in embed_step(state_a, STEPS // 2 - 1, 1):
        pass


def split(value):
    high = value.astype(BF16)
    return high, (value - high.astype(F32)).astype(BF16)


def dot(a, b, ca=1, cb=0):
    return lax.dot_general(a, b, (((ca,), (cb,)), ((), ())), preferred_element_type=F32)


def mm(a, b, ca=1, cb=0):
    return dot(a[0], b[0], ca, cb) + (dot(a[0], b[1], ca, cb) + dot(a[1], b[0], ca, cb))


def member_params(ids_col, props):
    count = props.shape[0]
    hot = jnp.where(ids_col[...] == lax.broadcasted_iota(jnp.int32, (count, count), 1), 1.0, 0.0)
    return jnp.dot(hot, props[...], precision=PRECISE, preferred_element_type=F32)


def repeated(rows, count):
    return jnp.concatenate([rows] * count, axis=0)


def flow_grads(lower_in, upper, summary, w_in, w_out, b_out):
    half = upper.shape[1]
    width = 2 * half
    sums = split(summary)
    w_sum = split(w_in[half:, :])
    hidden = jnp.tanh(mm(sums, w_sum) + lower_in)
    hid = split(hidden)
    out_w = split(w_out[...])
    both = dot(hid[0], jnp.concatenate(out_w, axis=1))
    raw = both[:, :width] + both[:, width:] + dot(hid[1], out_w[0]) + b_out[...]
    log_scale = jnp.tanh(raw[:, :half])
    grown = upper * jnp.exp(log_scale)
    latent = grown + raw[:, half:]
    d_scale = (latent * grown - 1.0) * (1.0 - log_scale * log_scale)
    d_raw = jnp.concatenate([d_scale, latent], axis=1)
    d_r = split(d_raw)
    d_hidden = dot(
        jnp.concatenate([d_r[0], d_r[1], d_r[0]], axis=1),
        jnp.concatenate([out_w[0], out_w[0], out_w[1]], axis=1),
        1,
        1,
    )
    d_hidden = d_hidden * (1.0 - hidden * hidden)
    return sums, hid, d_raw, d_r, d_hidden, w_sum


def local_kernel(
    members, inv_root, mine, theirs, ids, props, w_in, b_in, w_out, b_out, gram, kept, sent, own, total
):
    sums = (mine[...] + theirs[...]) * inv_root
    count = sums.shape[0]
    items = own.shape[0]
    for part in range(count // items):

        @pl.when(lax.axis_index("lon") == part)
        def _():
            own[...] = sums[part * items : (part + 1) * items, :]

    params = member_params(ids, props)
    half = params.shape[1] // 2
    low = split(params[:, :half])
    low_in = mm(low, split(w_in[:half, :])) + b_in[...]
    slot = lax.broadcasted_iota(jnp.int32, (count, params.shape[0]), 1)
    row = lax.broadcasted_iota(jnp.int32, (count, params.shape[0]), 0)
    hot = jnp.where(slot == lax.axis_index("grp") * members + row % members, 1.0, 0.0)
    low_in = jnp.dot(hot, low_in, precision=PRECISE, preferred_element_type=F32)
    upper = jnp.dot(hot, params[:, half:], precision=PRECISE, preferred_element_type=F32)
    _, _, _, _, d_hidden, w_sum = flow_grads(low_in, upper, sums, w_in, w_out, b_out)
    d_summary = mm(split(d_hidden), w_sum, 1, 1) * inv_root
    acc = gram[0] * d_summary[0:1, :]
    for i in range(1, count):
        acc = acc + gram[i] * d_summary[i : i + 1, :]
    total[...] = acc
    cells = acc.shape[0] // 2
    core = lax.axis_index("grp") % 2
    kept[...] = total[pl.ds(pl.multiple_of(core * cells, 8), cells), :]
    sent[...] = total[pl.ds(pl.multiple_of((1 - core) * cells, 8), cells), :]


def couple_kernel(
    members, lat_count, grp_count, order, summary, ids, props, w_in, b_in, w_out, b_out, rows, square, sorted_sums, staged
):
    per = summary.shape[0] // len(order)
    for index, (lat_flip, grp_flip) in enumerate(order):
        block = (lax.axis_index("lat") ^ lat_flip) * grp_count + (lax.axis_index("grp") ^ grp_flip)
        sorted_sums[pl.ds(pl.multiple_of(block * per, per), per), :] = summary[
            index * per : (index + 1) * per, :
        ]
    params = member_params(ids, props)
    half = params.shape[1] // 2
    low_in = mm(split(params[:, :half]), split(w_in[:half, :])) + b_in[...]
    groups = [slice(g * members, (g + 1) * members) for g in range(grp_count)]
    steps = per // members
    spread = lambda value: jnp.concatenate(
        [repeated(value[rs], steps) for rs in groups] * lat_count, axis=0
    )
    lower = spread(params[:, :half])
    sums, hid, d_raw, d_r, d_hidden, _ = flow_grads(
        spread(low_in), spread(params[:, half:]), sorted_sums[...], w_in, w_out, b_out
    )
    low = split(lower)
    context = [jnp.concatenate([sums[n], low[n]], axis=1) for n in range(2)]
    g_in = mm(context, split(d_hidden), 0, 0)
    width = 2 * half
    both = dot(hid[0], jnp.concatenate(d_r, axis=1), 0, 0)
    g_out = both[:, :width] + both[:, width:] + dot(hid[1], d_r[0], 0, 0)
    g_in_b = jnp.sum(d_hidden, axis=0, keepdims=True)
    g_out_b = jnp.sum(d_raw, axis=0, keepdims=True)
    hidden = d_hidden.shape[1]
    per_row = hidden // LANES
    feats = summary.shape[1]
    fold = LANES // width
    base = (half + feats) * per_row
    after = base + per_row
    tail = after + hidden // fold
    rows[base:, :] = jnp.zeros((rows.shape[0] - base, LANES), F32)
    for q in range(per_row):
        cs = slice(q * LANES, (q + 1) * LANES)
        rows[pl.ds(q, half, stride=per_row), :] = g_in[feats:, cs]
        rows[pl.ds(half * per_row + q, feats, stride=per_row), :] = g_in[:feats, cs]
        rows[base + q : base + q + 1, :] = g_in_b[:, cs]
    staged[...] = jnp.concatenate([g_out, jnp.zeros((hidden, LANES - width), F32)], axis=1)
    packed = jnp.zeros((hidden // fold, LANES), F32)
    for j in range(fold):
        packed = packed + turned(staged[pl.ds(j, hidden // fold, stride=fold), :], j * width)
    rows[after:tail, :] = packed
    rows[tail : tail + 1, :] = jnp.concatenate(
        [g_out_b, jnp.zeros((1, LANES - width), F32)], axis=1
    )
    whole = rows[...]
    square[...] = jnp.sum(whole * whole, axis=0, keepdims=True)


def finish_kernel(count, mine, theirs, couple, square, out, whole):
    core = lax.axis_index("grp") % 2
    cells = mine.shape[0]
    per_row = mine.shape[1] // LANES
    for h in range(per_row):
        cs = slice(h * LANES, (h + 1) * LANES)
        whole[h, pl.ds(pl.multiple_of(core * cells, 8), cells), :] = mine[:, cs]
        whole[h, pl.ds(pl.multiple_of((1 - core) * cells, 8), cells), :] = theirs[:, cs]
    conv = whole[...]
    squares = jnp.sum(conv * conv) + jnp.sum(square[...])
    scale = -lax.rsqrt(jnp.full((1, 1), squares, F32) / count + EPSILON)
    for r in range(PH):
        for h in range(per_row):
            part = whole[h, pl.ds(r, PW, stride=PH), :]
            out[pl.ds(r * PW * per_row + h, PW, stride=per_row), :] = part * scale
    used = 2 * cells * per_row
    out[used : used + couple.shape[0], :] = couple[...] * scale


def neighbour(value, axis, step):
    count = lax.axis_size(axis)
    pairs = [(i, (i + step) % count) for i in range(count)]
    return lax.ppermute(value, axis, pairs)


def from_lat(value, step):
    count = lax.axis_size("lat")
    return lax.ppermute(value, "lat", [(i, i + step) for i in range(count) if 0 <= i + step < count])


def swapped(value, axis, flip):
    count = lax.axis_size(axis)
    return lax.ppermute(value, axis, [(i, i ^ flip) for i in range(count)])


def flips(axis):
    count = lax.axis_size(axis)
    return [1 << i for i in range(count.bit_length() - 1)]


def shape(*dims, dtype=F32):
    return jax.ShapeDtypeStruct(dims, dtype)


def shards(
    sea_surface,
    velocity,
    levels,
    wind_basis,
    proposals,
    member_ids,
    conv_weight,
    couple_in,
    couple_in_bias,
    couple_out,
    couple_out_bias,
):
    members, rows, cols = sea_surface.shape
    lat_count, lon_count = lax.axis_size("lat"), lax.axis_size("lon")
    grp_count = lax.axis_size("grp")
    cells, feats = conv_weight.shape
    hid, width = couple_out.shape
    patches = cols // PW
    samples = STEPS * members
    groups = (4 * members + 2) * HALO
    height = rows + 2 * PAD
    inv_root = 1.0 / math.sqrt(rows // PH * (cols * lon_count // PW))

    anywhere = pl.BlockSpec(memory_space=pl.ANY)
    low, high = pl.pallas_call(
        lambda *refs: pack_kernel(members, *refs),
        out_shape=(shape(groups, cols, dtype=BF16), shape(groups, cols, dtype=BF16)),
        in_specs=[anywhere] * 6,
        out_specs=(vmem(), vmem()),
        scratch_shapes=[
            pltpu.SMEM(member_ids.shape, jnp.int32),
            pltpu.VMEM((2, 3, members, HALO, cols), F32),
            pltpu.VMEM((2, HALO, cols), jnp.int32),
            pltpu.VMEM((2, wind_basis.shape[0], 16, cols), BF16),
            pltpu.VMEM(proposals.shape, F32),
            pltpu.SemaphoreType.DMA((12,)),
        ],
        compiler_params=params_of(60),
        name="pack_rows",
    )(member_ids, sea_surface, velocity, levels, wind_basis, proposals)

    south = from_lat(high, 1)
    north = from_lat(low, -1)

    planes, side = pl.pallas_call(
        lambda *refs: planar_kernel(members, *refs),
        out_shape=(shape(5, PW, rows, LANES), shape(5 * rows, LANES, dtype=BF16)),
        in_specs=[smem()] + [vmem()] * 5,
        out_specs=(vmem(), vmem()),
        compiler_params=params_of(32),
        cost_estimate=pl.CostEstimate(flops=2 * 10**9, bytes_accessed=6 * MEBI, transcendentals=0),
        name="to_planes",
    )(member_ids, sea_surface, velocity, levels, wind_basis, proposals)

    wide = rows + 2 * HALO
    rim = pl.pallas_call(
        lambda *refs: rim_kernel(members, patches, *refs),
        out_shape=shape(3 * wide, LANES, dtype=BF16),
        in_specs=[vmem()] * 3,
        out_specs=vmem(),
        compiler_params=params_of(16),
        name="rim",
    )(south, north, side)
    west = neighbour(rim, "lon", 1)
    east = west if lon_count == 2 else neighbour(rim, "lon", -1)

    plane = (PW, height, LANES)
    prepared = pl.pallas_call(
        lambda *refs: prepare_kernel(members, rows, cols, lat_count, *refs),
        out_shape=(
            shape(3, *plane),
            shape(*plane),
            shape(2, height, LANES),
            shape(*plane),
            shape(*plane),
            shape(*plane),
            shape(height, LANES),
            shape(height, LANES),
            shape(cells, feats, dtype=BF16),
        ),
        in_specs=[vmem()] * 4,
        out_specs=(vmem(),) * 9,
        scratch_shapes=[
            pltpu.VMEM(plane, F32),
            pltpu.VMEM((feats // LANES, cells, LANES), F32),
        ],
        compiler_params=params_of(16),
        cost_estimate=pl.CostEstimate(flops=10**9, bytes_accessed=4 * MEBI, transcendentals=0),
        name="prepare",
    )(south, north, planes, conv_weight)

    partial, gram, final = pl.pallas_call(
        lambda *refs: flow_kernel(members, rows, cols, lat_count, *refs),
        out_shape=(
            shape(STEPS // 2, 2 * members, feats),
            shape(samples, cells, feats),
            shape(3, *plane),
        ),
        in_specs=[vmem()] * 12,
        out_specs=(vmem(),) * 3,
        scratch_shapes=[
            pltpu.VMEM((3, *plane), F32),
            pltpu.VMEM((3, height, LANES), F32),
            pltpu.VMEM((3, height, LANES), F32),
            pltpu.VMEM((height, LANES), F32),
            pltpu.VMEM((height, LANES), F32),
            pltpu.VMEM((3, height, LANES), F32),
            pltpu.VMEM((height, LANES), F32),
            pltpu.VMEM((height, LANES), F32),
            pltpu.VMEM((members, rows // PH * patches, cells), BF16),
            pltpu.VMEM((members, rows // PH * patches, feats), BF16),
            pltpu.VMEM((3, *plane), F32),
        ],
        compiler_params=params_of(32),
        name="flow_embed",
    )(*prepared, rim, east, west)
    partial = partial.reshape(samples, feats)

    if lon_count == 2:
        others = swapped(partial, "lon", 1)
    else:
        others = lax.psum(partial, "lon") - partial
    surface_out, velocity_out = pl.pallas_call(
        lambda *refs: back_kernel(members, *refs),
        out_shape=(shape(members, rows, cols), shape(2, members, rows, cols)),
        in_specs=[vmem()],
        out_specs=(vmem(), vmem()),
        compiler_params=params_of(24),
        cost_estimate=pl.CostEstimate(flops=2 * 10**9, bytes_accessed=6 * MEBI, transcendentals=0),
        name="from_planes",
    )(final)

    others, surface_out, velocity_out = lax.optimization_barrier((others, surface_out, velocity_out))
    summaries = (partial + others) * inv_root

    ids_col = member_ids.reshape(-1, 1)
    b_in = couple_in_bias.reshape(1, -1)
    b_out = couple_out_bias.reshape(1, -1)
    items = samples // lon_count
    kept, sent, own = pl.pallas_call(
        lambda *refs: local_kernel(members, inv_root, *refs),
        out_shape=(shape(cells // 2, feats), shape(cells // 2, feats), shape(items, feats)),
        in_specs=[vmem()] * 9,
        out_specs=(vmem(),) * 3,
        scratch_shapes=[pltpu.VMEM((cells, feats), F32)],
        compiler_params=params_of(16),
        name="local_loss",
    )(partial, others, ids_col, proposals, couple_in, b_in, couple_out, b_out, gram)

    def after(value, *others):
        return lax.optimization_barrier((value,) + others)[0]

    def gather(axis, flip):
        both = jnp.concatenate([gathered, swapped(gathered, axis, flip)], axis=0)
        return both, order + [(a ^ flip, b) if axis == "lat" else (a, b ^ flip) for a, b in order]

    gathered, order = summaries.astype(jnp.float16), [(0, 0)]
    gathered, order = gather("grp", 2)
    conv = kept + swapped(sent, "grp", 1)
    if lon_count == 2:
        corner = lax.ppermute(
            conv,
            ("lon", "grp"),
            [(i, (i // grp_count ^ 1) * grp_count + (i % grp_count ^ 2)) for i in range(2 * grp_count)],
        )
        by_lon = swapped(conv, "lon", 1)
        gathered = after(gathered, by_lon)
        conv = (conv + by_lon) + (swapped(conv, "grp", 2) + corner)
    else:
        conv = conv + swapped(conv, "grp", 2)
        for flip in flips("lon"):
            conv = conv + swapped(conv, "lon", flip)
    for flip in reversed(flips("lat")):
        by_lat = swapped(conv, "lat", flip)
        if flip > 1:
            gathered, order = gather("lat", flip)
            gathered = after(gathered, conv)
            conv = conv + by_lat
    gathered, order = gather("lat", 1)
    gathered = after(gathered, conv)
    gathered, order = gather("grp", 1)

    low_rows = (couple_in.size + hid + couple_out.size) // LANES + 1
    low_rows = -(-low_rows // 8) * 8
    count = cells * feats + couple_in.size + hid + couple_out.size + width
    couple, square = pl.pallas_call(
        lambda *refs: couple_kernel(members, lat_count, grp_count, order, *refs),
        out_shape=(shape(low_rows, LANES), shape(1, LANES)),
        in_specs=[vmem()] * 7,
        out_specs=(vmem(), vmem()),
        scratch_shapes=[
            pltpu.VMEM((len(order) * samples, feats), F32),
            pltpu.VMEM((hid, LANES), F32),
        ],
        compiler_params=params_of(24),
        cost_estimate=pl.CostEstimate(flops=3 * 10**9, bytes_accessed=3 * MEBI, transcendentals=0),
        name="couple_grads",
    )(gathered.astype(F32), ids_col, proposals, couple_in, b_in, couple_out, b_out)

    conv = conv + after(by_lat, couple, square)
    conv_other = swapped(conv, "grp", 1)

    stepped = pl.pallas_call(
        lambda *refs: finish_kernel(count, *refs),
        out_shape=shape(cells * feats // LANES + low_rows, LANES),
        in_specs=[vmem()] * 4,
        out_specs=vmem(),
        scratch_shapes=[pltpu.VMEM((feats // LANES, cells, LANES), F32)],
        compiler_params=params_of(16),
        name="finish",
    )(conv, conv_other, couple, square)
    weight_step = stepped.reshape(-1)[:count]

    return (surface_out, velocity_out, own.reshape(1, 1, 1, items, feats), weight_step)


def solution(mesh):
    in_specs = (
        P("grp", "lat", "lon"),
        P(None, "grp", "lat", "lon"),
        P("lat", "lon"),
        P(None, "lat", "lon"),
        P(),
        P(),
        P(),
        P(),
        P(),
        P(),
        P(),
    )
    out_specs = (
        P("grp", "lat", "lon"),
        P(None, "grp", "lat", "lon"),
        P("lon", "lat", "grp", None, None),
        P(),
    )
    return jax.shard_map(shards, mesh=mesh, in_specs=in_specs, out_specs=out_specs, check_vma=False)
```

```python
import math

import jax
import jax.numpy as jnp
from jax import lax
from jax.experimental import pallas as pl
from jax.experimental.pallas import tpu as pltpu
from jax.sharding import PartitionSpec as P

STEPS = 8
NLEV = 50
PH = 8
PW = 16
HALO = 8
PAD = 16

GRAVITY = 0.45
DRAG_RATE = 0.02
CORI_BASE = 0.05
CORI_SLOPE = 0.1
WIND_SCALE = 0.05
EPSILON = 1e-06
PRECISE = lax.Precision.HIGHEST
F32 = jnp.float32
BF16 = jnp.bfloat16
LANES = 128
MEBI = 2**20
HALF_DEPTH = 0.5 * GRAVITY / NLEV


def vmem():
    return pl.BlockSpec(memory_space=pltpu.VMEM)


def smem():
    return pl.BlockSpec(memory_space=pltpu.SMEM)


def params_of(mebi, **rest):
    return pltpu.CompilerParams(vmem_limit_bytes=mebi * MEBI, **rest)


def lane_ids(rows):
    return lax.broadcasted_iota(jnp.int32, (rows, LANES), 1)


def plane_matrix(cols, inverse=False):
    patches = cols // PW
    src = lax.broadcasted_iota(jnp.int32, (cols, cols), 1 if inverse else 0)
    dst = lax.broadcasted_iota(jnp.int32, (cols, cols), 0 if inverse else 1)
    return jnp.where(src == (dst % patches) * PW + dst // patches, 1.0, 0.0).astype(BF16)


def moved(value, matrix):
    both = jnp.dot(jnp.concatenate(split(value), axis=0), matrix, preferred_element_type=F32)
    return both[: value.shape[0]] + both[value.shape[0] :]


def by_segment(pieces, segment):
    out = pieces[-1]
    for index in range(len(pieces) - 2, -1, -1):
        out = jnp.where(segment == index, pieces[index], out)
    return out


def turned(value, shift):
    shift = shift % LANES
    return value if shift == 0 else pltpu.roll(value, shift, 1)


def planes_from(parts, patches):
    rows = parts[0].shape[0]
    per = LANES // patches
    segment = lane_ids(rows) // patches
    planes = []
    for k in range(PW):
        group, place = divmod(k, per)
        block = slice(group * LANES, (group + 1) * LANES)
        planes.append(
            by_segment(
                [turned(part[:, block], (m - place) * patches) for m, part in enumerate(parts)],
                segment,
            )
        )
    return planes


def edges_of(firsts, lasts, patches):
    rows = firsts[0].shape[0]
    lane = lane_ids(rows)
    out = jnp.zeros((rows, LANES), F32)
    for m, (first, last) in enumerate(zip(firsts, lasts)):
        both = jnp.where(lane < HALO, first, turned(last, 2 * HALO))
        here = (lane >= m * patches) & (lane < m * patches + 2 * HALO)
        out = jnp.where(here, turned(both, m * patches), out)
    return out


def forcing_rows(coeff, basis, members, keep=slice(None)):
    acc = [None] * members
    for k in range(basis.shape[0]):
        value = basis[k].astype(F32)[keep]
        for m in range(members):
            term = coeff[m][:, k : k + 1] * value
            acc[m] = term if acc[m] is None else acc[m] + term
    return acc


def coefficients(members, ids, props):
    base = lax.axis_index("grp") * members
    return [
        props[pl.ds(ids[base + m], 1), :].astype(BF16).astype(F32) * WIND_SCALE
        for m in range(members)
    ]


def pack_kernel(
    members, ids_in, sea, vel, levels, wind, props_in, low, high, ids, cells, depth, basis, props, sems
):
    rows, cols = levels.shape
    copies = [(ids_in, ids), (props_in, props)]
    ends = ((0, 0), (rows - HALO, rows - 16))
    for side, (r0, w0) in enumerate(ends):
        rs = pl.ds(r0, HALO)
        copies.append((sea.at[:, rs, :], cells.at[side, 0]))
        copies.append((vel.at[0, :, rs, :], cells.at[side, 1]))
        copies.append((vel.at[1, :, rs, :], cells.at[side, 2]))
        copies.append((levels.at[rs, :], depth.at[side]))
        copies.append((wind.at[:, pl.ds(w0, 16), :], basis.at[side]))
    started = [pltpu.make_async_copy(a, b, sems.at[n]) for n, (a, b) in enumerate(copies)]
    for copy in started:
        copy.start()
    for copy in started:
        copy.wait()
    coeff = coefficients(members, ids, props)
    for side, out in ((0, low), (1, high)):
        keep = slice(0, HALO) if side == 0 else slice(16 - HALO, 16)
        force = forcing_rows(coeff, basis.at[side], members, keep)
        blocks = [cells[side, i, m] for i in range(3) for m in range(members)]
        blocks += force
        blocks += [depth[side].astype(F32), jnp.zeros((HALO, cols), F32)]
        for g in range(0, len(blocks), 2):
            pair = jnp.concatenate(blocks[g : g + 2], axis=0)
            out[g * HALO : (g + 2) * HALO, :] = pair.astype(BF16)


def planar_kernel(members, ids, sea, vel, levels, wind, props, out, side):
    rows, cols = levels.shape
    patches = cols // PW
    coeff = coefficients(members, ids, props)
    strips = [
        forcing_rows(coeff, wind.at[:, pl.ds(r0, 16), :], members) for r0 in range(0, rows, 16)
    ]
    force = jnp.concatenate([strip[m] for m in range(members) for strip in strips], axis=0)
    depth = levels[...].astype(F32)
    matrix = plane_matrix(cols)
    scale = 1.0 / GRAVITY
    full = (members * rows, cols)
    fields = [sea[...].reshape(full), vel[0].reshape(full), vel[1].reshape(full), force, depth]
    for i, value in enumerate(fields):
        starts = [m * rows if i < 4 else 0 for m in range(members)]
        edge = edges_of(
            [value[r : r + rows, :LANES] for r in starts],
            [value[r : r + rows, cols - LANES :] for r in starts],
            patches,
        )
        side[i * rows : (i + 1) * rows, :] = edge.astype(BF16)
        if i < 4:
            spread = moved(value if i == 0 else value * scale, matrix)
        else:
            spread = jnp.dot(value.astype(BF16), matrix, preferred_element_type=F32)
        parts = [spread[r : r + rows] for r in starts]
        for k, plane in enumerate(planes_from(parts, patches)):
            out[i, k] = plane


def starts_of(i, members):
    if i < 4:
        return [(i * members + m) * HALO for m in range(members)]
    return [4 * members * HALO] * members


def rim_kernel(members, patches, south, north, side, out):
    rows = side.shape[0] // 5
    cols = south.shape[1]
    low, high = south[...].astype(F32), north[...].astype(F32)
    wholes = []
    for i in range(5):
        ends = [
            edges_of(
                [plain[s : s + HALO, :LANES] for s in starts_of(i, members)],
                [plain[s : s + HALO, cols - LANES :] for s in starts_of(i, members)],
                patches,
            )
            for plain in (low, high)
        ]
        own = side[i * rows : (i + 1) * rows, :].astype(F32)
        wholes.append(jnp.concatenate([ends[0], own, ends[1]], axis=0))
    wide = rows + 2 * HALO
    for n, i in enumerate((0, 2, 4)):
        pair = wholes[i]
        if i + 1 < len(wholes):
            pair = pair + pltpu.roll(wholes[i + 1], 2 * HALO, 1)
        out[n * wide : (n + 1) * wide, :] = pair.astype(BF16)


def rims_of(own, from_east, from_west, patches):
    place = lane_ids(own.shape[0]) % patches
    out = []
    for shift in (0, 2 * HALO):
        out.append(
            jnp.where(
                place < 2 * HALO,
                turned(own, -shift),
                jnp.where(
                    place < 3 * HALO,
                    turned(from_east, 2 * HALO - shift),
                    turned(from_west, -2 * HALO - shift),
                ),
            )
        )
    return out


def prepare_kernel(
    members,
    rows,
    cols,
    lat_count,
    south,
    north,
    planes,
    weight,
    ids_col,
    props,
    w_in,
    b_in,
    w_out,
    state,
    force,
    ends,
    hu,
    hv,
    hvu,
    cu,
    cv,
    cv_up,
    w_planes,
    low_in,
    params,
    low_own,
    upper_own,
    w_sum,
    out_cat,
    depth,
    w_rows,
):
    member_terms(
        members, ids_col, props, w_in, b_in, w_out, low_in, params, low_own, upper_own, w_sum, out_cat
    )
    patches = cols // PW
    height = rows + 2 * PAD
    wide = rows + 2 * HALO
    edge_rows = (slice(0, HALO), slice(height - HALO, height))
    homes = (state.at[0], state.at[1], state.at[2], force, depth)
    for i, home in enumerate(homes):
        home[0:PW, PAD : PAD + rows, :] = planes[i]
        if i != 3:
            for p in range(PW):
                for rs in edge_rows:
                    home[p, rs, :] = jnp.zeros((HALO, LANES), F32)
    matrix = plane_matrix(cols)
    for got, r0 in ((south, PAD - HALO), (north, PAD + rows)):
        spread = jnp.dot(got[...], matrix, preferred_element_type=F32)
        for i, home in enumerate(homes):
            parts = [spread[s : s + HALO] for s in starts_of(i, members)]
            for k, plane in enumerate(planes_from(parts, patches)):
                home[k, r0 : r0 + HALO, :] = plane if i in (0, 4) else plane * (1.0 / GRAVITY)
    span = slice(PAD - HALO, PAD + rows + HALO)
    row, inside = row_ids(rows, lat_count)
    place = row.astype(F32)
    total = lat_count * rows
    cu[span, :] = jnp.where(inside, 0.25 * (CORI_BASE + CORI_SLOPE * (place + 0.5) / total), 0.0)
    cv[span, :] = jnp.where(inside, 0.25 * (CORI_BASE + CORI_SLOPE * place / total), 0.0)
    above = (row >= -1) & (row < total - 1)
    cv_up[span, :] = jnp.where(above, 0.25 * (CORI_BASE + CORI_SLOPE * (place + 1) / total), 0.0)
    for p in range(PW):
        here = depth[p, span, :]
        if p > 0:
            hu[p, span, :] = HALF_DEPTH * (here + depth[p - 1, span, :])
        vertical(depth.at[p], hv.at[p], hvu.at[p], inside, rows)
    ends[0] = depth[0, 0:height]
    ends[1] = depth[PW - 1, 0:height]
    for h in range(w_rows.shape[0]):
        cs = slice(h * LANES, (h + 1) * LANES)
        w_rows[h] = weight[:, cs].astype(F32)
        w_planes[:, cs] = jnp.concatenate(
            [w_rows[h, pl.ds(k, PH, stride=PW), :] for k in range(PW)], axis=0
        ).astype(BF16)


def row_ids(rows, lat_count):
    wide = rows + 2 * HALO
    row = lax.broadcasted_iota(jnp.int32, (wide, LANES), 0) + (lax.axis_index("lat") * rows - HALO)
    return row, (row >= 0) & (row < lat_count * rows)


def vertical(depth, hv, hvu, inside, rows):
    span = slice(PAD - HALO, PAD + rows + HALO)
    here = depth[span, :]
    below = depth[PAD - HALO - 1 : PAD + rows + HALO - 1, :]
    above = depth[PAD - HALO + 1 : PAD + rows + HALO + 1, :]
    hv[span, :] = HALF_DEPTH * (here + below)
    hvu[span, :] = jnp.where(inside, HALF_DEPTH * (here + above), 0.0)


def back_kernel(members, state, sea, vel):
    rows, cols = sea.shape[1:]
    patches = cols // PW
    per = LANES // patches
    matrix = plane_matrix(cols, inverse=True)
    segment = lane_ids(rows) // patches
    for i in range(3):
        parts = []
        for m in range(members):
            groups = []
            for g in range(PW // per):
                pieces = [
                    turned(state[i, g * per + j, PAD : PAD + rows, :], (j - m) * patches)
                    for j in range(per)
                ]
                groups.append(by_segment(pieces, segment))
            parts.append(jnp.concatenate(groups, axis=1))
        value = moved(jnp.concatenate(parts, axis=0), matrix)
        for m in range(members):
            part = value[m * rows : (m + 1) * rows]
            if i == 0:
                sea[m] = part
            else:
                vel[i - 1, m] = part * GRAVITY


def flow_step(src, src_rim, dst, dst_rim, force, force_rim, hus, hvs, hvus, cu, cv, cv_up, last_mask, rows, patches):
    strip = PW
    wide = rows + 2 * HALO
    start = PAD - HALO
    keep = 1.0 - DRAG_RATE
    here = pl.ds(start, wide)
    last = lane_ids(wide) % patches == patches - 1

    def wrap_left(plane, rim):
        return pltpu.roll(jnp.where(last, rim, plane), 1, 1)

    def wrap_right(plane, rim):
        return jnp.where(last, pltpu.roll(rim, PW - 1, 1), pltpu.roll(plane, LANES - 1, 1))

    def of(planes, rim, i, p):
        return rim.at[i] if p == strip else planes.at[i, p]

    def new_level(p, fx, fx_right):
        n = of(src, src_rim, 2, p)[here, :]
        n_up = pltpu.roll(n, wide - 1, 0)
        fy = hvus[p][here, :] * n_up - hvs[p][here, :] * n
        level = of(src, src_rim, 0, p)[here, :] - ((fx_right - fx) + fy)
        of(dst, dst_rim, 0, p)[here, :] = level
        return level, n, n + n_up

    def new_flow(p, e, e_right, n, v, level, level_left):
        u = e + e_right
        push = force_rim[here, :] if p == strip else force[p, here, :]
        of(dst, dst_rim, 1, p)[here, :] = keep * e + cu[here, :] * v - (level - level_left) + push
        below = pltpu.roll(level - cv_up[here, :] * u, 1, 0)
        north = keep * n - cv[here, :] * u - level + below
        home = of(dst, dst_rim, 2, p)
        home[pl.ds(start, wide - HALO), :] = north[: wide - HALO]
        home[pl.ds(start + wide - HALO, HALO), :] = north[wide - HALO :] * last_mask

    e_rim = src_rim[1, here, :]
    fx_rim = hus[strip][here, :] * e_rim
    level_rim, n_rim, vs_rim = new_level(strip, fx_rim, pltpu.roll(fx_rim, LANES - 1, 1))
    new_flow(
        strip,
        e_rim,
        pltpu.roll(e_rim, LANES - 1, 1),
        n_rim,
        vs_rim + pltpu.roll(vs_rim, 1, 1),
        level_rim,
        pltpu.roll(level_rim, 1, 1),
    )
    e = src[1, 0, here, :]
    e_end = wrap_right(e, e_rim)
    level_last, n_last, vs_last = new_level(
        PW - 1, hus[PW - 1][here, :] * src[1, PW - 1, here, :], hus[PW + 1][here, :] * e_end
    )
    level_left = wrap_left(level_last, level_rim)
    vs_left = wrap_left(vs_last, vs_rim)
    fx = hus[0][here, :] * e
    for p in range(PW):
        if p < PW - 1:
            e_right = src[1, p + 1, here, :]
            fx_right = hus[p + 1][here, :] * e_right
            level, n, vs = new_level(p, fx, fx_right)
        else:
            e_right, fx_right = e_end, None
            level, n, vs = level_last, n_last, vs_last
        new_flow(p, e, e_right, n, vs + vs_left, level, level_left)
        level_left, vs_left, e, fx = level, vs, e_right, fx_right


def flow_kernel(
    members,
    rows,
    cols,
    lat_count,
    state,
    force,
    ends,
    hu,
    hv,
    hvu,
    cu,
    cv,
    cv_up,
    w_planes,
    side,
    east,
    west,
    partial,
    gram,
    final,
    state_b,
    rim_a,
    rim_b,
    force_rim,
    depth_rim,
    hu_rim,
    hv_rim,
    hvu_rim,
    patch_t,
    slope,
    state_a,
):
    patches = cols // PW
    lat = lax.axis_index("lat")
    height = rows + 2 * PAD
    wide = rows + 2 * HALO
    span = slice(PAD - HALO, PAD + rows + HALO)
    state_a[:, :, span, :] = state[:, :, span, :]
    for rs in (slice(0, HALO), slice(height - HALO, height)):
        depth_rim[rs, :] = jnp.zeros((HALO, LANES), F32)
    rim_homes = (rim_a.at[0], rim_a.at[1], rim_a.at[2], force_rim, depth_rim)
    for n in range(3):
        rs = slice(n * wide, (n + 1) * wide)
        got = [ref[rs, :].astype(F32) for ref in (side, east, west)]
        for i, rim in zip((2 * n, 2 * n + 1), rims_of(*got, patches)):
            if i < len(rim_homes):
                rim_homes[i][span, :] = rim if i in (0, 4) else rim * (1.0 / GRAVITY)
    _, inside = row_ids(rows, lat_count)
    last = lane_ids(wide) % patches == patches - 1
    rim = depth_rim[span, :]
    left = pltpu.roll(jnp.where(last, rim, ends[1, span, :]), 1, 1)
    first = HALF_DEPTH * (ends[0, span, :] + left)
    rim = HALF_DEPTH * (rim + pltpu.roll(rim, 1, 1))
    hu_rim[0, span, :] = first
    hu_rim[1, span, :] = rim
    hu_rim[2, span, :] = jnp.where(
        last, pltpu.roll(rim, PW - 1, 1), pltpu.roll(first, LANES - 1, 1)
    )
    vertical(depth_rim, hv_rim, hvu_rim, inside, rows)
    hus = [hu_rim.at[0]] + [hu.at[p] for p in range(1, PW)] + [hu_rim.at[1], hu_rim.at[2]]
    hvs = [hv.at[p] for p in range(PW)] + [hv_rim]
    hvus = [hvu.at[p] for p in range(PW)] + [hvu_rim]

    last_mask = jnp.where(lat < lat_count - 1, 1.0, 0.0)
    count = rows // PH

    def embed_step(state, turn, sub):
        step = 2 * turn + sub
        total = None
        for b in range(count):
            cells = state[0, 0:PW, PAD + b * PH : PAD + (b + 1) * PH, :].reshape(PW * PH, LANES)
            cells_t = cells.T.astype(BF16)
            act = jnp.tanh(jnp.dot(cells_t, w_planes[...], preferred_element_type=F32))
            total = act if total is None else total + act
            fall = (1.0 - act * act).astype(BF16)
            for m in range(members):
                rs = slice(m * patches, (m + 1) * patches)
                to = slice(b * patches, (b + 1) * patches)
                patch_t[m, to, :] = cells_t[rs]
                slope[m, to, :] = fall[rs]
        sums = jnp.sum(total.reshape(members, patches, total.shape[1]), axis=1)
        partial[turn, sub * members : (sub + 1) * members, :] = sums
        for m in range(members):
            gram[step * members + m] = lax.dot_general(
                patch_t[m], slope[m], (((0,), (0,)), ((), ())), preferred_element_type=F32
            )

    def step_of(src, src_rim, dst, dst_rim):
        flow_step(
            src, src_rim, dst, dst_rim, force, force_rim, hus, hvs, hvus, cu, cv, cv_up, last_mask, rows, patches
        )

    def two_steps(turn, carry):
        step_of(state_a, rim_a, state_b, rim_b)
        embed_step(state_a, jnp.maximum(turn - 1, 0), 1)
        step_of(state_b, rim_b, state_a, rim_a)
        embed_step(state_b, turn, 0)
        return carry

    lax.fori_loop(0, STEPS // 2, two_steps, 0)
    inner = slice(PAD, PAD + rows)
    final[:, :, inner, :] = state_a[:, :, inner, :]
    embed_step(state_a, STEPS // 2 - 1, 1)


def split(value):
    high = value.astype(BF16)
    return high, (value - high.astype(F32)).astype(BF16)


def dot(a, b, ca=1, cb=0):
    return lax.dot_general(a, b, (((ca,), (cb,)), ((), ())), preferred_element_type=F32)


def mm(a, b, ca=1, cb=0):
    return dot(a[0], b[0], ca, cb) + (dot(a[0], b[1], ca, cb) + dot(a[1], b[0], ca, cb))


def member_terms(
    members, ids_col, props, w_in, b_in, w_out, low_in, ends, low_own, upper_own, w_sum, out_cat
):
    count = props.shape[0]
    half = props.shape[1] // 2
    hot = jnp.where(ids_col[...] == lax.broadcasted_iota(jnp.int32, (count, count), 1), 1.0, 0.0)
    params = jnp.dot(hot, props[...], precision=PRECISE, preferred_element_type=F32)
    low = mm(split(params[:, :half]), split(w_in[:half, :])) + b_in[...]
    ends[...] = params
    low_in[...] = low
    samples = low_own.shape[0]
    slot = lax.broadcasted_iota(jnp.int32, (samples, count), 1)
    row = lax.broadcasted_iota(jnp.int32, (samples, count), 0)
    hot = jnp.where(slot == lax.axis_index("grp") * members + row % members, 1.0, 0.0)
    low_own[...] = jnp.dot(hot, low, precision=PRECISE, preferred_element_type=F32)
    upper_own[...] = jnp.dot(hot, params[:, half:], precision=PRECISE, preferred_element_type=F32)
    high, rest = split(w_in[half:, :])
    w_sum[0] = high
    w_sum[1] = rest
    high, rest = split(w_out[...].T)
    out_cat[...] = jnp.concatenate([high, high, rest], axis=1)


def repeated(rows, count):
    return jnp.concatenate([rows] * count, axis=0)


def flow_grads(lower_in, upper, summary, w_sum, out_cat, b_out):
    half = upper.shape[1]
    width = 2 * half
    sums = split(summary)
    hidden = jnp.tanh(mm(sums, w_sum) + lower_in)
    hid = split(hidden)
    both = dot(hid[0], out_cat[:, width:])
    raw = both[:, :width] + both[:, width:] + dot(hid[1], out_cat[:, :width]) + b_out[...]
    log_scale = jnp.tanh(raw[:, :half])
    grown = upper * jnp.exp(log_scale)
    latent = grown + raw[:, half:]
    d_scale = (latent * grown - 1.0) * (1.0 - log_scale * log_scale)
    d_raw = jnp.concatenate([d_scale, latent], axis=1)
    d_r = split(d_raw)
    d_hidden = dot(jnp.concatenate([d_r[0], d_r[1], d_r[0]], axis=1), out_cat[...], 1, 1)
    d_hidden = d_hidden * (1.0 - hidden * hidden)
    return sums, hid, d_raw, d_r, d_hidden


def local_kernel(
    inv_root, mine, theirs, low_in, upper, w_sum, out_cat, b_out, gram, kept, sent, own, total
):
    sums = (mine[...] + theirs[...]) * inv_root
    count = sums.shape[0]
    items = own.shape[0]
    for part in range(count // items):

        @pl.when(lax.axis_index("lon") == part)
        def _():
            own[...] = sums[part * items : (part + 1) * items, :]

    w_pair = (w_sum[0], w_sum[1])
    d_hidden = flow_grads(low_in[...], upper[...], sums, w_pair, out_cat, b_out)[-1]
    d_summary = mm(split(d_hidden), w_pair, 1, 1) * inv_root
    acc = gram[0] * d_summary[0:1, :]
    for i in range(1, count):
        acc = acc + gram[i] * d_summary[i : i + 1, :]
    total[...] = acc
    cells = acc.shape[0] // 2
    core = lax.axis_index("grp") % 2
    kept[...] = total[pl.ds(pl.multiple_of(core * cells, 8), cells), :]
    sent[...] = total[pl.ds(pl.multiple_of((1 - core) * cells, 8), cells), :]


def couple_kernel(
    members, lat_count, grp_count, order, summary, low_in, ends, w_sum, out_cat, b_out, rows, square, sorted_sums, staged
):
    per = summary.shape[0] // len(order)
    for index, (lat_flip, grp_flip) in enumerate(order):
        block = (lax.axis_index("lat") ^ lat_flip) * grp_count + (lax.axis_index("grp") ^ grp_flip)
        sorted_sums[pl.ds(pl.multiple_of(block * per, per), per), :] = summary[
            index * per : (index + 1) * per, :
        ]
    params = ends[...]
    half = params.shape[1] // 2
    groups = [slice(g * members, (g + 1) * members) for g in range(grp_count)]
    steps = per // members
    spread = lambda value: jnp.concatenate(
        [repeated(value[rs], steps) for rs in groups] * lat_count, axis=0
    )
    lower = spread(params[:, :half])
    sums, hid, d_raw, d_r, d_hidden = flow_grads(
        spread(low_in[...]),
        spread(params[:, half:]),
        sorted_sums[...],
        (w_sum[0], w_sum[1]),
        out_cat,
        b_out,
    )
    low = split(lower)
    context = [jnp.concatenate([sums[n], low[n]], axis=1) for n in range(2)]
    g_in = mm(context, split(d_hidden), 0, 0)
    width = 2 * half
    both = dot(hid[0], jnp.concatenate(d_r, axis=1), 0, 0)
    g_out = both[:, :width] + both[:, width:] + dot(hid[1], d_r[0], 0, 0)
    g_in_b = jnp.sum(d_hidden, axis=0, keepdims=True)
    g_out_b = jnp.sum(d_raw, axis=0, keepdims=True)
    hidden = d_hidden.shape[1]
    per_row = hidden // LANES
    feats = summary.shape[1]
    fold = LANES // width
    base = (half + feats) * per_row
    after = base + per_row
    tail = after + hidden // fold
    rows[base:, :] = jnp.zeros((rows.shape[0] - base, LANES), F32)
    for q in range(per_row):
        cs = slice(q * LANES, (q + 1) * LANES)
        rows[pl.ds(q, half, stride=per_row), :] = g_in[feats:, cs]
        rows[pl.ds(half * per_row + q, feats, stride=per_row), :] = g_in[:feats, cs]
        rows[base + q : base + q + 1, :] = g_in_b[:, cs]
    staged[...] = jnp.concatenate([g_out, jnp.zeros((hidden, LANES - width), F32)], axis=1)
    packed = jnp.zeros((hidden // fold, LANES), F32)
    for j in range(fold):
        packed = packed + turned(staged[pl.ds(j, hidden // fold, stride=fold), :], j * width)
    rows[after:tail, :] = packed
    rows[tail : tail + 1, :] = jnp.concatenate(
        [g_out_b, jnp.zeros((1, LANES - width), F32)], axis=1
    )
    whole = rows[...]
    square[...] = jnp.sum(whole * whole, axis=0, keepdims=True)


def finish_kernel(count, mine, theirs, couple, square, out, whole):
    core = lax.axis_index("grp") % 2
    cells = mine.shape[0]
    per_row = mine.shape[1] // LANES
    for h in range(per_row):
        cs = slice(h * LANES, (h + 1) * LANES)
        whole[h, pl.ds(pl.multiple_of(core * cells, 8), cells), :] = mine[:, cs]
        whole[h, pl.ds(pl.multiple_of((1 - core) * cells, 8), cells), :] = theirs[:, cs]
    conv = whole[...]
    squares = jnp.sum(conv * conv) + jnp.sum(square[...])
    scale = -lax.rsqrt(jnp.full((1, 1), squares, F32) / count + EPSILON)
    for r in range(PH):
        for h in range(per_row):
            part = whole[h, pl.ds(r, PW, stride=PH), :]
            out[pl.ds(r * PW * per_row + h, PW, stride=per_row), :] = part * scale
    used = 2 * cells * per_row
    out[used : used + couple.shape[0], :] = couple[...] * scale


def neighbour(value, axis, step):
    count = lax.axis_size(axis)
    pairs = [(i, (i + step) % count) for i in range(count)]
    return lax.ppermute(value, axis, pairs)


def from_lat(value, step):
    count = lax.axis_size("lat")
    return lax.ppermute(value, "lat", [(i, i + step) for i in range(count) if 0 <= i + step < count])


def swapped(value, axis, flip):
    count = lax.axis_size(axis)
    return lax.ppermute(value, axis, [(i, i ^ flip) for i in range(count)])


def flips(axis):
    count = lax.axis_size(axis)
    return [1 << i for i in range(count.bit_length() - 1)]


def shape(*dims, dtype=F32):
    return jax.ShapeDtypeStruct(dims, dtype)


def shards(
    sea_surface,
    velocity,
    levels,
    wind_basis,
    proposals,
    member_ids,
    conv_weight,
    couple_in,
    couple_in_bias,
    couple_out,
    couple_out_bias,
):
    members, rows, cols = sea_surface.shape
    lat_count, lon_count = lax.axis_size("lat"), lax.axis_size("lon")
    grp_count = lax.axis_size("grp")
    cells, feats = conv_weight.shape
    hid, width = couple_out.shape
    patches = cols // PW
    samples = STEPS * members
    groups = (4 * members + 2) * HALO
    height = rows + 2 * PAD
    inv_root = 1.0 / math.sqrt(rows // PH * (cols * lon_count // PW))

    anywhere = pl.BlockSpec(memory_space=pl.ANY)
    low, high = pl.pallas_call(
        lambda *refs: pack_kernel(members, *refs),
        out_shape=(shape(groups, cols, dtype=BF16), shape(groups, cols, dtype=BF16)),
        in_specs=[anywhere] * 6,
        out_specs=(vmem(), vmem()),
        scratch_shapes=[
            pltpu.SMEM(member_ids.shape, jnp.int32),
            pltpu.VMEM((2, 3, members, HALO, cols), F32),
            pltpu.VMEM((2, HALO, cols), jnp.int32),
            pltpu.VMEM((2, wind_basis.shape[0], 16, cols), BF16),
            pltpu.VMEM(proposals.shape, F32),
            pltpu.SemaphoreType.DMA((12,)),
        ],
        compiler_params=params_of(60),
        name="pack_rows",
    )(member_ids, sea_surface, velocity, levels, wind_basis, proposals)

    south = from_lat(high, 1)
    north = from_lat(low, -1)

    planes, side = pl.pallas_call(
        lambda *refs: planar_kernel(members, *refs),
        out_shape=(shape(5, PW, rows, LANES), shape(5 * rows, LANES, dtype=BF16)),
        in_specs=[smem()] + [vmem()] * 5,
        out_specs=(vmem(), vmem()),
        compiler_params=params_of(32),
        cost_estimate=pl.CostEstimate(flops=2 * 10**9, bytes_accessed=6 * MEBI, transcendentals=0),
        name="to_planes",
    )(member_ids, sea_surface, velocity, levels, wind_basis, proposals)

    wide = rows + 2 * HALO
    rim = pl.pallas_call(
        lambda *refs: rim_kernel(members, patches, *refs),
        out_shape=shape(3 * wide, LANES, dtype=BF16),
        in_specs=[vmem()] * 3,
        out_specs=vmem(),
        compiler_params=params_of(16),
        name="rim",
    )(south, north, side)
    west = neighbour(rim, "lon", 1)
    east = west if lon_count == 2 else neighbour(rim, "lon", -1)

    def after(value, *others):
        return lax.optimization_barrier((value,) + others)[0]

    b_out = couple_out_bias.reshape(1, -1)
    plane = (PW, height + HALO, LANES)
    prepared = pl.pallas_call(
        lambda *refs: prepare_kernel(members, rows, cols, lat_count, *refs),
        out_shape=(
            shape(3, *plane),
            shape(*plane),
            shape(2, height, LANES),
            shape(*plane),
            shape(*plane),
            shape(*plane),
            shape(height, LANES),
            shape(height, LANES),
            shape(height, LANES),
            shape(cells, feats, dtype=BF16),
            shape(proposals.shape[0], hid),
            shape(*proposals.shape),
            shape(samples, hid),
            shape(samples, width // 2),
            shape(2, feats, hid, dtype=BF16),
            shape(hid, 3 * width, dtype=BF16),
        ),
        in_specs=[vmem()] * 9,
        out_specs=(vmem(),) * 16,
        scratch_shapes=[
            pltpu.VMEM(plane, F32),
            pltpu.VMEM((feats // LANES, cells, LANES), F32),
        ],
        compiler_params=params_of(16),
        cost_estimate=pl.CostEstimate(flops=10**9, bytes_accessed=4 * MEBI, transcendentals=0),
        name="prepare",
    )(
        south,
        north,
        planes,
        conv_weight,
        member_ids.reshape(-1, 1),
        proposals,
        couple_in,
        couple_in_bias.reshape(1, -1),
        couple_out.T,
    )
    prepared, (low_in, ends, low_own, upper_own, w_sum, out_cat) = prepared[:10], prepared[10:]

    partial, gram, final = pl.pallas_call(
        lambda *refs: flow_kernel(members, rows, cols, lat_count, *refs),
        out_shape=(
            shape(STEPS // 2, 2 * members, feats),
            shape(samples, cells, feats),
            shape(3, *plane),
        ),
        in_specs=[vmem()] * 13,
        out_specs=(vmem(),) * 3,
        scratch_shapes=[
            pltpu.VMEM((3, *plane), F32),
            pltpu.VMEM((3, height, LANES), F32),
            pltpu.VMEM((3, height, LANES), F32),
            pltpu.VMEM((height, LANES), F32),
            pltpu.VMEM((height, LANES), F32),
            pltpu.VMEM((3, height, LANES), F32),
            pltpu.VMEM((height, LANES), F32),
            pltpu.VMEM((height, LANES), F32),
            pltpu.VMEM((members, rows // PH * patches, cells), BF16),
            pltpu.VMEM((members, rows // PH * patches, feats), BF16),
            pltpu.VMEM((3, *plane), F32),
        ],
        compiler_params=params_of(32),
        name="flow_embed",
    )(*prepared, rim, east, west)
    partial = partial.reshape(samples, feats)

    if lon_count == 2:
        others = swapped(partial, "lon", 1)
    else:
        others = lax.psum(partial, "lon") - partial
    surface_out, velocity_out = pl.pallas_call(
        lambda *refs: back_kernel(members, *refs),
        out_shape=(shape(members, rows, cols), shape(2, members, rows, cols)),
        in_specs=[vmem()],
        out_specs=(vmem(), vmem()),
        compiler_params=params_of(24),
        cost_estimate=pl.CostEstimate(flops=2 * 10**9, bytes_accessed=6 * MEBI, transcendentals=0),
        name="from_planes",
    )(final)

    others, surface_out, velocity_out = lax.optimization_barrier((others, surface_out, velocity_out))
    summaries = (partial + others) * inv_root

    items = samples // lon_count
    kept, sent, own = pl.pallas_call(
        lambda *refs: local_kernel(inv_root, *refs),
        out_shape=(shape(cells // 2, feats), shape(cells // 2, feats), shape(items, feats)),
        in_specs=[vmem()] * 8,
        out_specs=(vmem(),) * 3,
        scratch_shapes=[pltpu.VMEM((cells, feats), F32)],
        compiler_params=params_of(16),
        name="local_loss",
    )(partial, others, low_own, upper_own, w_sum, out_cat, b_out, gram)

    def gather(axis, flip):
        both = jnp.concatenate([gathered, swapped(gathered, axis, flip)], axis=0)
        return both, order + [(a ^ flip, b) if axis == "lat" else (a, b ^ flip) for a, b in order]

    gathered, order = summaries.astype(jnp.float16), [(0, 0)]
    gathered, order = gather("grp", 2)
    conv = kept + swapped(sent, "grp", 1)
    if lon_count == 2:
        corner = lax.ppermute(
            conv,
            ("lon", "grp"),
            [(i, (i // grp_count ^ 1) * grp_count + (i % grp_count ^ 2)) for i in range(2 * grp_count)],
        )
        by_lon = swapped(conv, "lon", 1)
        gathered = after(gathered, by_lon)
        conv = (conv + corner) + (swapped(conv, "grp", 2) + by_lon)
    else:
        conv = conv + swapped(conv, "grp", 2)
        for flip in flips("lon"):
            conv = conv + swapped(conv, "lon", flip)
    for flip in reversed(flips("lat")):
        by_lat = swapped(conv, "lat", flip)
        if flip > 1:
            gathered, order = gather("lat", flip)
            gathered = after(gathered, conv)
            conv = conv + by_lat
    gathered, order = gather("lat", 1)
    gathered = after(gathered, conv)
    gathered, order = gather("grp", 1)

    low_rows = (couple_in.size + hid + couple_out.size) // LANES + 1
    low_rows = -(-low_rows // 8) * 8
    count = cells * feats + couple_in.size + hid + couple_out.size + width
    couple, square = pl.pallas_call(
        lambda *refs: couple_kernel(members, lat_count, grp_count, order, *refs),
        out_shape=(shape(low_rows, LANES), shape(1, LANES)),
        in_specs=[vmem()] * 6,
        out_specs=(vmem(), vmem()),
        scratch_shapes=[
            pltpu.VMEM((len(order) * samples, feats), F32),
            pltpu.VMEM((hid, LANES), F32),
        ],
        compiler_params=params_of(24),
        cost_estimate=pl.CostEstimate(flops=3 * 10**9, bytes_accessed=3 * MEBI, transcendentals=0),
        name="couple_grads",
    )(gathered.astype(F32), low_in, ends, w_sum, out_cat, b_out)

    conv = conv + after(by_lat, couple, square)
    conv_other = swapped(conv, "grp", 1)

    stepped = pl.pallas_call(
        lambda *refs: finish_kernel(count, *refs),
        out_shape=shape(cells * feats // LANES + low_rows, LANES),
        in_specs=[vmem()] * 4,
        out_specs=vmem(),
        scratch_shapes=[pltpu.VMEM((feats // LANES, cells, LANES), F32)],
        compiler_params=params_of(16),
        name="finish",
    )(conv, conv_other, couple, square)
    weight_step = stepped.reshape(-1)[:count]

    return (surface_out, velocity_out, own.reshape(1, 1, 1, items, feats), weight_step)


def solution(mesh):
    in_specs = (
        P("grp", "lat", "lon"),
        P(None, "grp", "lat", "lon"),
        P("lat", "lon"),
        P(None, "lat", "lon"),
        P(),
        P(),
        P(),
        P(),
        P(),
        P(),
        P(),
    )
    out_specs = (
        P("grp", "lat", "lon"),
        P(None, "grp", "lat", "lon"),
        P("lon", "lat", "grp", None, None),
        P(),
    )
    return jax.shard_map(shards, mesh=mesh, in_specs=in_specs, out_specs=out_specs, check_vma=False)
```

```python
import math

import jax
import jax.numpy as jnp
from jax import lax
from jax.experimental import pallas as pl
from jax.experimental.pallas import tpu as pltpu
from jax.sharding import PartitionSpec as P

STEPS = 8
NLEV = 50
PH = 8
PW = 16
HALO = 8
PAD = 16

GRAVITY = 0.45
DRAG_RATE = 0.02
CORI_BASE = 0.05
CORI_SLOPE = 0.1
WIND_SCALE = 0.05
EPSILON = 1e-06
PRECISE = lax.Precision.HIGHEST
F32 = jnp.float32
BF16 = jnp.bfloat16
LANES = 128
MEBI = 2**20
HALF_DEPTH = 0.5 * GRAVITY / NLEV


def vmem():
    return pl.BlockSpec(memory_space=pltpu.VMEM)


def smem():
    return pl.BlockSpec(memory_space=pltpu.SMEM)


def params_of(mebi, **rest):
    return pltpu.CompilerParams(vmem_limit_bytes=mebi * MEBI, **rest)


def lane_ids(rows):
    return lax.broadcasted_iota(jnp.int32, (rows, LANES), 1)


def plane_matrix(cols, inverse=False):
    patches = cols // PW
    src = lax.broadcasted_iota(jnp.int32, (cols, cols), 1 if inverse else 0)
    dst = lax.broadcasted_iota(jnp.int32, (cols, cols), 0 if inverse else 1)
    return jnp.where(src == (dst % patches) * PW + dst // patches, 1.0, 0.0).astype(BF16)


def moved(value, matrix):
    both = jnp.dot(jnp.concatenate(split(value), axis=0), matrix, preferred_element_type=F32)
    return both[: value.shape[0]] + both[value.shape[0] :]


def by_segment(pieces, segment):
    out = pieces[-1]
    for index in range(len(pieces) - 2, -1, -1):
        out = jnp.where(segment == index, pieces[index], out)
    return out


def turned(value, shift):
    shift = shift % LANES
    return value if shift == 0 else pltpu.roll(value, shift, 1)


def planes_from(parts, patches):
    rows = parts[0].shape[0]
    per = LANES // patches
    segment = lane_ids(rows) // patches
    planes = []
    for k in range(PW):
        group, place = divmod(k, per)
        block = slice(group * LANES, (group + 1) * LANES)
        planes.append(
            by_segment(
                [turned(part[:, block], (m - place) * patches) for m, part in enumerate(parts)],
                segment,
            )
        )
    return planes


def edges_of(firsts, lasts, patches):
    rows = firsts[0].shape[0]
    lane = lane_ids(rows)
    out = jnp.zeros((rows, LANES), F32)
    for m, (first, last) in enumerate(zip(firsts, lasts)):
        both = jnp.where(lane < HALO, first, turned(last, 2 * HALO))
        here = (lane >= m * patches) & (lane < m * patches + 2 * HALO)
        out = jnp.where(here, turned(both, m * patches), out)
    return out


def forcing_rows(coeff, basis, members, keep=slice(None)):
    acc = [None] * members
    for k in range(basis.shape[0]):
        value = basis[k].astype(F32)[keep]
        for m in range(members):
            term = coeff[m][:, k : k + 1] * value
            acc[m] = term if acc[m] is None else acc[m] + term
    return acc


def coefficients(members, ids, props):
    base = lax.axis_index("grp") * members
    return [
        props[pl.ds(ids[base + m], 1), :].astype(BF16).astype(F32) * WIND_SCALE
        for m in range(members)
    ]


def pack_kernel(
    members, ids_in, sea, vel, levels, wind, props_in, low, high, ids, cells, depth, basis, props, sems
):
    rows, cols = levels.shape
    copies = [(ids_in, ids), (props_in, props)]
    ends = ((0, 0), (rows - HALO, rows - 16))
    for side, (r0, w0) in enumerate(ends):
        rs = pl.ds(r0, HALO)
        copies.append((sea.at[:, rs, :], cells.at[side, 0]))
        copies.append((vel.at[0, :, rs, :], cells.at[side, 1]))
        copies.append((vel.at[1, :, rs, :], cells.at[side, 2]))
        copies.append((levels.at[pl.ds(w0, 16), :], depth.at[side]))
        copies.append((wind.at[:, pl.ds(w0, 16), :], basis.at[side]))
    started = [pltpu.make_async_copy(a, b, sems.at[n]) for n, (a, b) in enumerate(copies)]
    for copy in started:
        copy.start()
    for copy in started:
        copy.wait()
    coeff = coefficients(members, ids, props)
    for side, out in ((0, low), (1, high)):
        keep = slice(0, HALO) if side == 0 else slice(16 - HALO, 16)
        force = forcing_rows(coeff, basis.at[side], members, keep)
        blocks = [cells[side, i, m] for i in range(3) for m in range(members)]
        blocks += force
        rest = slice(HALO, 16) if side == 0 else slice(0, 16 - HALO)
        blocks += [depth[side, part, :].astype(F32) for part in (keep, rest)]
        for g in range(0, len(blocks), 2):
            pair = jnp.concatenate(blocks[g : g + 2], axis=0)
            out[g * HALO : (g + 2) * HALO, :] = pair.astype(BF16)


def planar_kernel(members, ids, sea, vel, levels, wind, props, out, side):
    rows, cols = levels.shape
    patches = cols // PW
    coeff = coefficients(members, ids, props)
    strips = [
        forcing_rows(coeff, wind.at[:, pl.ds(r0, 16), :], members) for r0 in range(0, rows, 16)
    ]
    force = jnp.concatenate([strip[m] for m in range(members) for strip in strips], axis=0)
    depth = levels[...].astype(F32)
    matrix = plane_matrix(cols)
    scale = 1.0 / GRAVITY
    full = (members * rows, cols)
    fields = [sea[...].reshape(full), vel[0].reshape(full), vel[1].reshape(full), force, depth]
    west = [pltpu.roll(depth[:, cols - LANES :], 1, 1)] * members
    side[5 * rows : 6 * rows, :] = edges_of(west, west, patches).astype(BF16)
    for i, value in enumerate(fields):
        starts = [m * rows if i < 4 else 0 for m in range(members)]
        edge = edges_of(
            [value[r : r + rows, :LANES] for r in starts],
            [value[r : r + rows, cols - LANES :] for r in starts],
            patches,
        )
        side[i * rows : (i + 1) * rows, :] = edge.astype(BF16)
        if i < 4:
            spread = moved(value if i == 0 else value * scale, matrix)
        else:
            spread = jnp.dot(value.astype(BF16), matrix, preferred_element_type=F32)
        parts = [spread[r : r + rows] for r in starts]
        for k, plane in enumerate(planes_from(parts, patches)):
            out[i, k] = plane


def starts_of(i, members):
    if i < 4:
        return [(i * members + m) * HALO for m in range(members)]
    return [(4 * members + i - 4) * HALO] * members


def rim_kernel(members, patches, south, north, side, out):
    rows = side.shape[0] // 6
    cols = south.shape[1]
    low, high = south[...].astype(F32), north[...].astype(F32)

    def edges(plain, i, turn):
        starts = starts_of(i, members)
        lasts = [plain[s : s + HALO, cols - LANES :] for s in starts]
        return edges_of(
            [plain[s : s + HALO, :LANES] for s in starts],
            [turned(last, turn) for last in lasts],
            patches,
        )

    wholes = []
    for i in range(6):
        ends = [edges(plain, min(i, 4), 1 if i == 5 else 0) for plain in (low, high)]
        own = side[i * rows : (i + 1) * rows, :].astype(F32)
        wholes.append(jnp.concatenate([ends[0], own, ends[1]], axis=0))
    wide = rows + 2 * HALO
    for n in range(3):
        pair = wholes[2 * n] + pltpu.roll(wholes[2 * n + 1], 2 * HALO, 1)
        out[n * wide : (n + 1) * wide, :] = pair.astype(BF16)
    behind = edges(low, 5, 0)
    out[3 * wide : 3 * wide + 2 * HALO, :] = jnp.concatenate([behind, behind], axis=0).astype(BF16)


def rims_of(own, from_east, from_west, patches):
    place = lane_ids(own.shape[0]) % patches
    out = []
    for shift in (0, 2 * HALO):
        out.append(
            jnp.where(
                place < 2 * HALO,
                turned(own, -shift),
                jnp.where(
                    place < 3 * HALO,
                    turned(from_east, 2 * HALO - shift),
                    turned(from_west, -2 * HALO - shift),
                ),
            )
        )
    return out


def prepare_kernel(
    members,
    rows,
    cols,
    lat_count,
    south,
    north,
    planes,
    weight,
    ids_col,
    props,
    w_in,
    b_in,
    w_out,
    state,
    force,
    ends,
    hu,
    hv,
    hvu,
    cu,
    cv,
    cv_up,
    w_planes,
    low_in,
    params,
    low_own,
    upper_own,
    w_sum,
    out_cat,
    depth,
    w_rows,
):
    member_terms(
        members, ids_col, props, w_in, b_in, w_out, low_in, params, low_own, upper_own, w_sum, out_cat
    )
    patches = cols // PW
    height = rows + 2 * PAD
    wide = rows + 2 * HALO
    edge_rows = (slice(0, HALO), slice(height - HALO, height))
    homes = (state.at[0], state.at[1], state.at[2], force, depth)
    for i, home in enumerate(homes):
        home[0:PW, PAD : PAD + rows, :] = planes[i]
        if i != 3:
            for p in range(PW):
                for rs in edge_rows:
                    home[p, rs, :] = jnp.zeros((HALO, LANES), F32)
    matrix = plane_matrix(cols)
    for got, r0 in ((south, PAD - HALO), (north, PAD + rows)):
        spread = jnp.dot(got[...], matrix, preferred_element_type=F32)
        for i, home in enumerate(homes):
            parts = [spread[s : s + HALO] for s in starts_of(i, members)]
            for k, plane in enumerate(planes_from(parts, patches)):
                home[k, r0 : r0 + HALO, :] = plane if i in (0, 4) else plane * (1.0 / GRAVITY)
        if r0 < PAD:
            parts = [spread[s : s + HALO] for s in starts_of(5, members)]
            for k, plane in enumerate(planes_from(parts, patches)):
                depth[k, 0:HALO, :] = plane
    span = slice(PAD - HALO, PAD + rows + HALO)
    row, inside = row_ids(rows, lat_count)
    place = row.astype(F32)
    total = lat_count * rows
    cu[span, :] = jnp.where(inside, 0.25 * (CORI_BASE + CORI_SLOPE * (place + 0.5) / total), 0.0)
    cv[span, :] = jnp.where(inside, 0.25 * (CORI_BASE + CORI_SLOPE * place / total), 0.0)
    above = (row >= -1) & (row < total - 1)
    cv_up[span, :] = jnp.where(above, 0.25 * (CORI_BASE + CORI_SLOPE * (place + 1) / total), 0.0)
    for p in range(PW):
        here = depth[p, span, :]
        if p > 0:
            hu[p, span, :] = HALF_DEPTH * (here + depth[p - 1, span, :])
        vertical(depth.at[p], hv.at[p], hvu.at[p], inside, rows)
    ends[0] = depth[0, 0:height]
    ends[1] = depth[PW - 1, 0:height]
    for h in range(w_rows.shape[0]):
        cs = slice(h * LANES, (h + 1) * LANES)
        w_rows[h] = weight[:, cs].astype(F32)
        w_planes[:, cs] = jnp.concatenate(
            [w_rows[h, pl.ds(k, PH, stride=PW), :] for k in range(PW)], axis=0
        ).astype(BF16)


def row_ids(rows, lat_count):
    wide = rows + 2 * HALO
    row = lax.broadcasted_iota(jnp.int32, (wide, LANES), 0) + (lax.axis_index("lat") * rows - HALO)
    return row, (row >= 0) & (row < lat_count * rows)


def vertical(depth, hv, hvu, inside, rows):
    span = slice(PAD - HALO, PAD + rows + HALO)
    here = depth[span, :]
    below = depth[PAD - HALO - 1 : PAD + rows + HALO - 1, :]
    above = depth[PAD - HALO + 1 : PAD + rows + HALO + 1, :]
    hv[span, :] = HALF_DEPTH * (here + below)
    hvu[span, :] = jnp.where(inside, HALF_DEPTH * (here + above), 0.0)


def back_kernel(members, state, sea, vel):
    rows, cols = sea.shape[1:]
    patches = cols // PW
    per = LANES // patches
    matrix = plane_matrix(cols, inverse=True)
    segment = lane_ids(rows) // patches
    for i in range(3):
        parts = []
        for m in range(members):
            groups = []
            for g in range(PW // per):
                pieces = [
                    turned(state[i, g * per + j, PAD : PAD + rows, :], (j - m) * patches)
                    for j in range(per)
                ]
                groups.append(by_segment(pieces, segment))
            parts.append(jnp.concatenate(groups, axis=1))
        value = moved(jnp.concatenate(parts, axis=0), matrix)
        for m in range(members):
            part = value[m * rows : (m + 1) * rows]
            if i == 0:
                sea[m] = part
            else:
                vel[i - 1, m] = part * GRAVITY


def flow_step(src, src_rim, dst, dst_rim, force, force_rim, hus, hvs, hvus, cu, cv, cv_up, last_mask, rows, patches):
    strip = PW
    wide = rows + 2 * HALO
    start = PAD - HALO
    keep = 1.0 - DRAG_RATE
    here = pl.ds(start, wide)
    last = lane_ids(wide) % patches == patches - 1

    def wrap_left(plane, rim):
        return pltpu.roll(jnp.where(last, rim, plane), 1, 1)

    def wrap_right(plane, rim):
        return jnp.where(last, pltpu.roll(rim, PW - 1, 1), pltpu.roll(plane, LANES - 1, 1))

    def of(planes, rim, i, p):
        return rim.at[i] if p == strip else planes.at[i, p]

    def new_level(p, fx, fx_right):
        n = of(src, src_rim, 2, p)[here, :]
        n_up = pltpu.roll(n, wide - 1, 0)
        fy = hvus[p][here, :] * n_up - hvs[p][here, :] * n
        level = of(src, src_rim, 0, p)[here, :] - ((fx_right - fx) + fy)
        of(dst, dst_rim, 0, p)[here, :] = level
        return level, n, n + n_up

    def new_flow(p, e, e_right, n, v, level, level_left):
        u = e + e_right
        push = force_rim[here, :] if p == strip else force[p, here, :]
        of(dst, dst_rim, 1, p)[here, :] = keep * e + cu[here, :] * v - (level - level_left) + push
        below = pltpu.roll(level - cv_up[here, :] * u, 1, 0)
        north = keep * n - cv[here, :] * u - level + below
        home = of(dst, dst_rim, 2, p)
        home[pl.ds(start, wide - HALO), :] = north[: wide - HALO]
        home[pl.ds(start + wide - HALO, HALO), :] = north[wide - HALO :] * last_mask

    e_rim = src_rim[1, here, :]
    fx_rim = hus[strip][here, :] * e_rim
    level_rim, n_rim, vs_rim = new_level(strip, fx_rim, pltpu.roll(fx_rim, LANES - 1, 1))
    new_flow(
        strip,
        e_rim,
        pltpu.roll(e_rim, LANES - 1, 1),
        n_rim,
        vs_rim + pltpu.roll(vs_rim, 1, 1),
        level_rim,
        pltpu.roll(level_rim, 1, 1),
    )
    e = src[1, 0, here, :]
    e_end = wrap_right(e, e_rim)
    level_last, n_last, vs_last = new_level(
        PW - 1, hus[PW - 1][here, :] * src[1, PW - 1, here, :], hus[PW + 1][here, :] * e_end
    )
    level_left = wrap_left(level_last, level_rim)
    vs_left = wrap_left(vs_last, vs_rim)
    fx = hus[0][here, :] * e
    for p in range(PW):
        if p < PW - 1:
            e_right = src[1, p + 1, here, :]
            fx_right = hus[p + 1][here, :] * e_right
            level, n, vs = new_level(p, fx, fx_right)
        else:
            e_right, fx_right = e_end, None
            level, n, vs = level_last, n_last, vs_last
        new_flow(p, e, e_right, n, vs + vs_left, level, level_left)
        level_left, vs_left, e, fx = level, vs, e_right, fx_right


def flow_kernel(
    members,
    rows,
    cols,
    lat_count,
    state,
    force,
    ends,
    hu,
    hv,
    hvu,
    cu,
    cv,
    cv_up,
    w_planes,
    side,
    east,
    west,
    partial,
    gram,
    final,
    state_b,
    rim_a,
    rim_b,
    force_rim,
    depth_rim,
    west_rim,
    hu_rim,
    hv_rim,
    hvu_rim,
    patch_t,
    slope,
    state_a,
):
    patches = cols // PW
    lat = lax.axis_index("lat")
    height = rows + 2 * PAD
    wide = rows + 2 * HALO
    span = slice(PAD - HALO, PAD + rows + HALO)
    state_a[:, :, span, :] = state[:, :, span, :]
    depth_rim[height - HALO : height, :] = jnp.zeros((HALO, LANES), F32)
    behind = slice(3 * wide, 3 * wide + 2 * HALO)
    got = [ref[behind, :].astype(F32)[:HALO] for ref in (side, east, west)]
    depth_rim[0:HALO, :] = rims_of(*got, patches)[0]
    rim_homes = (rim_a.at[0], rim_a.at[1], rim_a.at[2], force_rim, depth_rim, west_rim)
    for n in range(3):
        rs = slice(n * wide, (n + 1) * wide)
        got = [ref[rs, :].astype(F32) for ref in (side, east, west)]
        for i, rim in zip((2 * n, 2 * n + 1), rims_of(*got, patches)):
            rim_homes[i][span, :] = rim * (1.0 / GRAVITY) if i in (1, 2, 3) else rim
    _, inside = row_ids(rows, lat_count)
    last = lane_ids(wide) % patches == patches - 1
    rim = depth_rim[span, :]
    left = pltpu.roll(jnp.where(last, rim, ends[1, span, :]), 1, 1)
    first = HALF_DEPTH * (ends[0, span, :] + left)
    outer = lane_ids(wide) % patches >= 3 * HALO
    rim = HALF_DEPTH * (rim + jnp.where(outer, west_rim[span, :], pltpu.roll(rim, 1, 1)))
    hu_rim[0, span, :] = first
    hu_rim[1, span, :] = rim
    hu_rim[2, span, :] = jnp.where(
        last, pltpu.roll(rim, PW - 1, 1), pltpu.roll(first, LANES - 1, 1)
    )
    vertical(depth_rim, hv_rim, hvu_rim, inside, rows)
    hus = [hu_rim.at[0]] + [hu.at[p] for p in range(1, PW)] + [hu_rim.at[1], hu_rim.at[2]]
    hvs = [hv.at[p] for p in range(PW)] + [hv_rim]
    hvus = [hvu.at[p] for p in range(PW)] + [hvu_rim]

    last_mask = jnp.where(lat < lat_count - 1, 1.0, 0.0)
    count = rows // PH

    def embed_step(state, turn, sub):
        step = 2 * turn + sub
        total = None
        for b in range(count):
            cells = state[0, 0:PW, PAD + b * PH : PAD + (b + 1) * PH, :].reshape(PW * PH, LANES)
            cells_t = cells.T.astype(BF16)
            act = jnp.tanh(jnp.dot(cells_t, w_planes[...], preferred_element_type=F32))
            total = act if total is None else total + act
            fall = (1.0 - act * act).astype(BF16)
            for m in range(members):
                rs = slice(m * patches, (m + 1) * patches)
                to = slice(b * patches, (b + 1) * patches)
                patch_t[m, to, :] = cells_t[rs]
                slope[m, to, :] = fall[rs]
        sums = jnp.sum(total.reshape(members, patches, total.shape[1]), axis=1)
        partial[turn, sub * members : (sub + 1) * members, :] = sums
        for m in range(members):
            gram[step * members + m] = lax.dot_general(
                patch_t[m], slope[m], (((0,), (0,)), ((), ())), preferred_element_type=F32
            )

    def step_of(src, src_rim, dst, dst_rim):
        flow_step(
            src, src_rim, dst, dst_rim, force, force_rim, hus, hvs, hvus, cu, cv, cv_up, last_mask, rows, patches
        )

    def two_steps(turn, carry):
        step_of(state_a, rim_a, state_b, rim_b)
        embed_step(state_a, jnp.maximum(turn - 1, 0), 1)
        step_of(state_b, rim_b, state_a, rim_a)
        embed_step(state_b, turn, 0)
        return carry

    lax.fori_loop(0, STEPS // 2, two_steps, 0)
    inner = slice(PAD, PAD + rows)
    final[:, :, inner, :] = state_a[:, :, inner, :]
    embed_step(state_a, STEPS // 2 - 1, 1)


def split(value):
    high = value.astype(BF16)
    return high, (value - high.astype(F32)).astype(BF16)


def dot(a, b, ca=1, cb=0):
    return lax.dot_general(a, b, (((ca,), (cb,)), ((), ())), preferred_element_type=F32)


def mm(a, b, ca=1, cb=0):
    return dot(a[0], b[0], ca, cb) + (dot(a[0], b[1], ca, cb) + dot(a[1], b[0], ca, cb))


def member_terms(
    members, ids_col, props, w_in, b_in, w_out, low_in, ends, low_own, upper_own, w_sum, out_cat
):
    count = props.shape[0]
    half = props.shape[1] // 2
    hot = jnp.where(ids_col[...] == lax.broadcasted_iota(jnp.int32, (count, count), 1), 1.0, 0.0)
    params = jnp.dot(hot, props[...], precision=PRECISE, preferred_element_type=F32)
    low = mm(split(params[:, :half]), split(w_in[:half, :])) + b_in[...]
    ends[...] = params
    low_in[...] = low
    samples = low_own.shape[0]
    slot = lax.broadcasted_iota(jnp.int32, (samples, count), 1)
    row = lax.broadcasted_iota(jnp.int32, (samples, count), 0)
    hot = jnp.where(slot == lax.axis_index("grp") * members + row % members, 1.0, 0.0)
    low_own[...] = jnp.dot(hot, low, precision=PRECISE, preferred_element_type=F32)
    upper_own[...] = jnp.dot(hot, params[:, half:], precision=PRECISE, preferred_element_type=F32)
    high, rest = split(w_in[half:, :])
    w_sum[0] = high
    w_sum[1] = rest
    high, rest = split(w_out[...].T)
    out_cat[...] = jnp.concatenate([high, high, rest], axis=1)


def repeated(rows, count):
    return jnp.concatenate([rows] * count, axis=0)


def flow_grads(lower_in, upper, summary, w_sum, out_cat, b_out):
    half = upper.shape[1]
    width = 2 * half
    sums = split(summary)
    hidden = jnp.tanh(mm(sums, w_sum) + lower_in)
    hid = split(hidden)
    both = dot(hid[0], out_cat[:, width:])
    raw = both[:, :width] + both[:, width:] + dot(hid[1], out_cat[:, :width]) + b_out[...]
    log_scale = jnp.tanh(raw[:, :half])
    grown = upper * jnp.exp(log_scale)
    latent = grown + raw[:, half:]
    d_scale = (latent * grown - 1.0) * (1.0 - log_scale * log_scale)
    d_raw = jnp.concatenate([d_scale, latent], axis=1)
    d_r = split(d_raw)
    d_hidden = dot(jnp.concatenate([d_r[0], d_r[1], d_r[0]], axis=1), out_cat[...], 1, 1)
    d_hidden = d_hidden * (1.0 - hidden * hidden)
    return sums, hid, d_raw, d_r, d_hidden


def local_kernel(
    inv_root, mine, theirs, low_in, upper, w_sum, out_cat, b_out, gram, kept, sent, own, total
):
    sums = (mine[...] + theirs[...]) * inv_root
    count = sums.shape[0]
    items = own.shape[0]
    for part in range(count // items):

        @pl.when(lax.axis_index("lon") == part)
        def _():
            own[...] = sums[part * items : (part + 1) * items, :]

    w_pair = (w_sum[0], w_sum[1])
    d_hidden = flow_grads(low_in[...], upper[...], sums, w_pair, out_cat, b_out)[-1]
    d_summary = mm(split(d_hidden), w_pair, 1, 1) * inv_root
    acc = gram[0] * d_summary[0:1, :]
    for i in range(1, count):
        acc = acc + gram[i] * d_summary[i : i + 1, :]
    total[...] = acc
    cells = acc.shape[0] // 2
    core = lax.axis_index("grp") % 2
    kept[...] = total[pl.ds(pl.multiple_of(core * cells, 8), cells), :]
    sent[...] = total[pl.ds(pl.multiple_of((1 - core) * cells, 8), cells), :]


def couple_kernel(
    members, lat_count, grp_count, order, summary, low_in, ends, w_sum, out_cat, b_out, rows, square, sorted_sums, staged
):
    per = summary.shape[0] // len(order)
    for index, (lat_flip, grp_flip) in enumerate(order):
        block = (lax.axis_index("lat") ^ lat_flip) * grp_count + (lax.axis_index("grp") ^ grp_flip)
        sorted_sums[pl.ds(pl.multiple_of(block * per, per), per), :] = summary[
            index * per : (index + 1) * per, :
        ]
    params = ends[...]
    half = params.shape[1] // 2
    groups = [slice(g * members, (g + 1) * members) for g in range(grp_count)]
    steps = per // members
    spread = lambda value: jnp.concatenate(
        [repeated(value[rs], steps) for rs in groups] * lat_count, axis=0
    )
    lower = spread(params[:, :half])
    sums, hid, d_raw, d_r, d_hidden = flow_grads(
        spread(low_in[...]),
        spread(params[:, half:]),
        sorted_sums[...],
        (w_sum[0], w_sum[1]),
        out_cat,
        b_out,
    )
    low = split(lower)
    context = [jnp.concatenate([sums[n], low[n]], axis=1) for n in range(2)]
    g_in = mm(context, split(d_hidden), 0, 0)
    width = 2 * half
    both = dot(hid[0], jnp.concatenate(d_r, axis=1), 0, 0)
    g_out = both[:, :width] + both[:, width:] + dot(hid[1], d_r[0], 0, 0)
    g_in_b = jnp.sum(d_hidden, axis=0, keepdims=True)
    g_out_b = jnp.sum(d_raw, axis=0, keepdims=True)
    hidden = d_hidden.shape[1]
    per_row = hidden // LANES
    feats = summary.shape[1]
    fold = LANES // width
    base = (half + feats) * per_row
    after = base + per_row
    tail = after + hidden // fold
    rows[base:, :] = jnp.zeros((rows.shape[0] - base, LANES), F32)
    for q in range(per_row):
        cs = slice(q * LANES, (q + 1) * LANES)
        rows[pl.ds(q, half, stride=per_row), :] = g_in[feats:, cs]
        rows[pl.ds(half * per_row + q, feats, stride=per_row), :] = g_in[:feats, cs]
        rows[base + q : base + q + 1, :] = g_in_b[:, cs]
    staged[...] = jnp.concatenate([g_out, jnp.zeros((hidden, LANES - width), F32)], axis=1)
    packed = jnp.zeros((hidden // fold, LANES), F32)
    for j in range(fold):
        packed = packed + turned(staged[pl.ds(j, hidden // fold, stride=fold), :], j * width)
    rows[after:tail, :] = packed
    rows[tail : tail + 1, :] = jnp.concatenate(
        [g_out_b, jnp.zeros((1, LANES - width), F32)], axis=1
    )
    whole = rows[...]
    square[...] = jnp.sum(whole * whole, axis=0, keepdims=True)


def finish_kernel(count, mine, theirs, couple, square, out, whole):
    core = lax.axis_index("grp") % 2
    cells = mine.shape[0]
    per_row = mine.shape[1] // LANES
    for h in range(per_row):
        cs = slice(h * LANES, (h + 1) * LANES)
        whole[h, pl.ds(pl.multiple_of(core * cells, 8), cells), :] = mine[:, cs]
        whole[h, pl.ds(pl.multiple_of((1 - core) * cells, 8), cells), :] = theirs[:, cs]
    conv = whole[...]
    squares = jnp.sum(conv * conv) + jnp.sum(square[...])
    scale = -lax.rsqrt(jnp.full((1, 1), squares, F32) / count + EPSILON)
    for r in range(PH):
        for h in range(per_row):
            part = whole[h, pl.ds(r, PW, stride=PH), :]
            out[pl.ds(r * PW * per_row + h, PW, stride=per_row), :] = part * scale
    used = 2 * cells * per_row
    out[used : used + couple.shape[0], :] = couple[...] * scale


def neighbour(value, axis, step):
    count = lax.axis_size(axis)
    pairs = [(i, (i + step) % count) for i in range(count)]
    return lax.ppermute(value, axis, pairs)


def from_lat(value, step):
    count = lax.axis_size("lat")
    return lax.ppermute(value, "lat", [(i, i + step) for i in range(count) if 0 <= i + step < count])


def swapped(value, axis, flip):
    count = lax.axis_size(axis)
    return lax.ppermute(value, axis, [(i, i ^ flip) for i in range(count)])


def flips(axis):
    count = lax.axis_size(axis)
    return [1 << i for i in range(count.bit_length() - 1)]


def shape(*dims, dtype=F32):
    return jax.ShapeDtypeStruct(dims, dtype)


def shards(
    sea_surface,
    velocity,
    levels,
    wind_basis,
    proposals,
    member_ids,
    conv_weight,
    couple_in,
    couple_in_bias,
    couple_out,
    couple_out_bias,
):
    members, rows, cols = sea_surface.shape
    lat_count, lon_count = lax.axis_size("lat"), lax.axis_size("lon")
    grp_count = lax.axis_size("grp")
    cells, feats = conv_weight.shape
    hid, width = couple_out.shape
    patches = cols // PW
    samples = STEPS * members
    groups = (4 * members + 2) * HALO
    height = rows + 2 * PAD
    inv_root = 1.0 / math.sqrt(rows // PH * (cols * lon_count // PW))

    anywhere = pl.BlockSpec(memory_space=pl.ANY)
    low, high = pl.pallas_call(
        lambda *refs: pack_kernel(members, *refs),
        out_shape=(shape(groups, cols, dtype=BF16), shape(groups, cols, dtype=BF16)),
        in_specs=[anywhere] * 6,
        out_specs=(vmem(), vmem()),
        scratch_shapes=[
            pltpu.SMEM(member_ids.shape, jnp.int32),
            pltpu.VMEM((2, 3, members, HALO, cols), F32),
            pltpu.VMEM((2, 16, cols), jnp.int32),
            pltpu.VMEM((2, wind_basis.shape[0], 16, cols), BF16),
            pltpu.VMEM(proposals.shape, F32),
            pltpu.SemaphoreType.DMA((12,)),
        ],
        compiler_params=params_of(60),
        name="pack_rows",
    )(member_ids, sea_surface, velocity, levels, wind_basis, proposals)

    south = from_lat(high, 1)
    north = from_lat(low, -1)

    planes, side = pl.pallas_call(
        lambda *refs: planar_kernel(members, *refs),
        out_shape=(shape(5, PW, rows, LANES), shape(6 * rows, LANES, dtype=BF16)),
        in_specs=[smem()] + [vmem()] * 5,
        out_specs=(vmem(), vmem()),
        compiler_params=params_of(32),
        cost_estimate=pl.CostEstimate(flops=2 * 10**9, bytes_accessed=6 * MEBI, transcendentals=0),
        name="to_planes",
    )(member_ids, sea_surface, velocity, levels, wind_basis, proposals)

    wide = rows + 2 * HALO
    rim = pl.pallas_call(
        lambda *refs: rim_kernel(members, patches, *refs),
        out_shape=shape(3 * wide + 2 * HALO, LANES, dtype=BF16),
        in_specs=[vmem()] * 3,
        out_specs=vmem(),
        compiler_params=params_of(16),
        name="rim",
    )(south, north, side)
    west = neighbour(rim, "lon", 1)
    east = west if lon_count == 2 else neighbour(rim, "lon", -1)

    def after(value, *others):
        return lax.optimization_barrier((value,) + others)[0]

    b_out = couple_out_bias.reshape(1, -1)
    plane = (PW, height + HALO, LANES)
    prepared = pl.pallas_call(
        lambda *refs: prepare_kernel(members, rows, cols, lat_count, *refs),
        out_shape=(
            shape(3, *plane),
            shape(*plane),
            shape(2, height, LANES),
            shape(*plane),
            shape(*plane),
            shape(*plane),
            shape(height, LANES),
            shape(height, LANES),
            shape(height, LANES),
            shape(cells, feats, dtype=BF16),
            shape(proposals.shape[0], hid),
            shape(*proposals.shape),
            shape(samples, hid),
            shape(samples, width // 2),
            shape(2, feats, hid, dtype=BF16),
            shape(hid, 3 * width, dtype=BF16),
        ),
        in_specs=[vmem()] * 9,
        out_specs=(vmem(),) * 16,
        scratch_shapes=[
            pltpu.VMEM(plane, F32),
            pltpu.VMEM((feats // LANES, cells, LANES), F32),
        ],
        compiler_params=params_of(16),
        cost_estimate=pl.CostEstimate(flops=10**9, bytes_accessed=4 * MEBI, transcendentals=0),
        name="prepare",
    )(
        south,
        north,
        planes,
        conv_weight,
        member_ids.reshape(-1, 1),
        proposals,
        couple_in,
        couple_in_bias.reshape(1, -1),
        couple_out.T,
    )
    prepared, (low_in, ends, low_own, upper_own, w_sum, out_cat) = prepared[:10], prepared[10:]

    partial, gram, final = pl.pallas_call(
        lambda *refs: flow_kernel(members, rows, cols, lat_count, *refs),
        out_shape=(
            shape(STEPS // 2, 2 * members, feats),
            shape(samples, cells, feats),
            shape(3, *plane),
        ),
        in_specs=[vmem()] * 13,
        out_specs=(vmem(),) * 3,
        scratch_shapes=[
            pltpu.VMEM((3, *plane), F32),
            pltpu.VMEM((3, height, LANES), F32),
            pltpu.VMEM((3, height, LANES), F32),
            pltpu.VMEM((height, LANES), F32),
            pltpu.VMEM((height, LANES), F32),
            pltpu.VMEM((height, LANES), F32),
            pltpu.VMEM((3, height, LANES), F32),
            pltpu.VMEM((height, LANES), F32),
            pltpu.VMEM((height, LANES), F32),
            pltpu.VMEM((members, rows // PH * patches, cells), BF16),
            pltpu.VMEM((members, rows // PH * patches, feats), BF16),
            pltpu.VMEM((3, *plane), F32),
        ],
        compiler_params=params_of(32),
        name="flow_embed",
    )(*prepared, rim, east, west)
    partial = partial.reshape(samples, feats)

    if lon_count == 2:
        others = swapped(partial, "lon", 1)
    else:
        others = lax.psum(partial, "lon") - partial
    surface_out, velocity_out = pl.pallas_call(
        lambda *refs: back_kernel(members, *refs),
        out_shape=(shape(members, rows, cols), shape(2, members, rows, cols)),
        in_specs=[vmem()],
        out_specs=(vmem(), vmem()),
        compiler_params=params_of(24),
        cost_estimate=pl.CostEstimate(flops=2 * 10**9, bytes_accessed=6 * MEBI, transcendentals=0),
        name="from_planes",
    )(final)

    others, surface_out, velocity_out = lax.optimization_barrier((others, surface_out, velocity_out))
    summaries = (partial + others) * inv_root

    items = samples // lon_count
    kept, sent, own = pl.pallas_call(
        lambda *refs: local_kernel(inv_root, *refs),
        out_shape=(shape(cells // 2, feats), shape(cells // 2, feats), shape(items, feats)),
        in_specs=[vmem()] * 8,
        out_specs=(vmem(),) * 3,
        scratch_shapes=[pltpu.VMEM((cells, feats), F32)],
        compiler_params=params_of(16),
        name="local_loss",
    )(partial, others, low_own, upper_own, w_sum, out_cat, b_out, gram)

    def gather(axis, flip):
        both = jnp.concatenate([gathered, swapped(gathered, axis, flip)], axis=0)
        return both, order + [(a ^ flip, b) if axis == "lat" else (a, b ^ flip) for a, b in order]

    gathered, order = summaries.astype(jnp.float16), [(0, 0)]
    gathered, order = gather("grp", 2)
    conv = kept + swapped(sent, "grp", 1)
    if lon_count == 2:
        corner = lax.ppermute(
            conv,
            ("lon", "grp"),
            [(i, (i // grp_count ^ 1) * grp_count + (i % grp_count ^ 2)) for i in range(2 * grp_count)],
        )
        by_lon = swapped(conv, "lon", 1)
        gathered = after(gathered, by_lon)
        conv = (conv + corner) + (swapped(conv, "grp", 2) + by_lon)
    else:
        conv = conv + swapped(conv, "grp", 2)
        for flip in flips("lon"):
            conv = conv + swapped(conv, "lon", flip)
    for flip in reversed(flips("lat")):
        by_lat = swapped(conv, "lat", flip)
        if flip > 1:
            gathered, order = gather("lat", flip)
            gathered = after(gathered, conv)
            conv = conv + by_lat
    gathered, order = gather("lat", 1)
    gathered = after(gathered, conv)
    gathered, order = gather("grp", 1)

    low_rows = (couple_in.size + hid + couple_out.size) // LANES + 1
    low_rows = -(-low_rows // 8) * 8
    count = cells * feats + couple_in.size + hid + couple_out.size + width
    couple, square = pl.pallas_call(
        lambda *refs: couple_kernel(members, lat_count, grp_count, order, *refs),
        out_shape=(shape(low_rows, LANES), shape(1, LANES)),
        in_specs=[vmem()] * 6,
        out_specs=(vmem(), vmem()),
        scratch_shapes=[
            pltpu.VMEM((len(order) * samples, feats), F32),
            pltpu.VMEM((hid, LANES), F32),
        ],
        compiler_params=params_of(24),
        cost_estimate=pl.CostEstimate(flops=3 * 10**9, bytes_accessed=3 * MEBI, transcendentals=0),
        name="couple_grads",
    )(gathered.astype(F32), low_in, ends, w_sum, out_cat, b_out)

    conv = conv + after(by_lat, couple, square)
    conv_other = swapped(conv, "grp", 1)

    stepped = pl.pallas_call(
        lambda *refs: finish_kernel(count, *refs),
        out_shape=shape(cells * feats // LANES + low_rows, LANES),
        in_specs=[vmem()] * 4,
        out_specs=vmem(),
        scratch_shapes=[pltpu.VMEM((feats // LANES, cells, LANES), F32)],
        compiler_params=params_of(16),
        name="finish",
    )(conv, conv_other, couple, square)
    weight_step = stepped.reshape(-1)[:count]

    return (surface_out, velocity_out, own.reshape(1, 1, 1, items, feats), weight_step)


def solution(mesh):
    in_specs = (
        P("grp", "lat", "lon"),
        P(None, "grp", "lat", "lon"),
        P("lat", "lon"),
        P(None, "lat", "lon"),
        P(),
        P(),
        P(),
        P(),
        P(),
        P(),
        P(),
    )
    out_specs = (
        P("grp", "lat", "lon"),
        P(None, "grp", "lat", "lon"),
        P("lon", "lat", "grp", None, None),
        P(),
    )
    return jax.shard_map(shards, mesh=mesh, in_specs=in_specs, out_specs=out_specs, check_vma=False)
```

```python
import math

import jax
import jax.numpy as jnp
from jax import lax
from jax.experimental import pallas as pl
from jax.experimental.pallas import tpu as pltpu
from jax.sharding import PartitionSpec as P

STEPS = 8
NLEV = 50
PH = 8
PW = 16
HALO = 8
PAD = 16

GRAVITY = 0.45
DRAG_RATE = 0.02
CORI_BASE = 0.05
CORI_SLOPE = 0.1
WIND_SCALE = 0.05
EPSILON = 1e-06
PRECISE = lax.Precision.HIGHEST
F32 = jnp.float32
BF16 = jnp.bfloat16
LANES = 128
MEBI = 2**20
HALF_DEPTH = 0.5 * GRAVITY / NLEV


def vmem():
    return pl.BlockSpec(memory_space=pltpu.VMEM)


def smem():
    return pl.BlockSpec(memory_space=pltpu.SMEM)


def params_of(mebi, **rest):
    return pltpu.CompilerParams(vmem_limit_bytes=mebi * MEBI, **rest)


def lane_ids(rows):
    return lax.broadcasted_iota(jnp.int32, (rows, LANES), 1)


def plane_matrix(cols, inverse=False):
    patches = cols // PW
    src = lax.broadcasted_iota(jnp.int32, (cols, cols), 1 if inverse else 0)
    dst = lax.broadcasted_iota(jnp.int32, (cols, cols), 0 if inverse else 1)
    return jnp.where(src == (dst % patches) * PW + dst // patches, 1.0, 0.0).astype(BF16)


def moved(value, matrix):
    both = jnp.dot(jnp.concatenate(split(value), axis=0), matrix, preferred_element_type=F32)
    return both[: value.shape[0]] + both[value.shape[0] :]


def by_segment(pieces, segment):
    out = pieces[-1]
    for index in range(len(pieces) - 2, -1, -1):
        out = jnp.where(segment == index, pieces[index], out)
    return out


def turned(value, shift):
    shift = shift % LANES
    return value if shift == 0 else pltpu.roll(value, shift, 1)


def planes_from(parts, patches):
    rows = parts[0].shape[0]
    per = LANES // patches
    segment = lane_ids(rows) // patches
    planes = []
    for k in range(PW):
        group, place = divmod(k, per)
        block = slice(group * LANES, (group + 1) * LANES)
        planes.append(
            by_segment(
                [turned(part[:, block], (m - place) * patches) for m, part in enumerate(parts)],
                segment,
            )
        )
    return planes


def edges_of(firsts, lasts, patches):
    rows = firsts[0].shape[0]
    lane = lane_ids(rows)
    out = jnp.zeros((rows, LANES), F32)
    for m, (first, last) in enumerate(zip(firsts, lasts)):
        both = jnp.where(lane < HALO, first, turned(last, 2 * HALO))
        here = (lane >= m * patches) & (lane < m * patches + 2 * HALO)
        out = jnp.where(here, turned(both, m * patches), out)
    return out


def forcing_rows(coeff, basis, members, keep=slice(None)):
    acc = [None] * members
    for k in range(basis.shape[0]):
        value = basis[k].astype(F32)[keep]
        for m in range(members):
            term = coeff[m][:, k : k + 1] * value
            acc[m] = term if acc[m] is None else acc[m] + term
    return acc


def coefficients(members, ids, props):
    base = lax.axis_index("grp") * members
    return [
        props[pl.ds(ids[base + m], 1), :].astype(BF16).astype(F32) * WIND_SCALE
        for m in range(members)
    ]


def pack_kernel(
    members, ids_in, sea, vel, levels, wind, props_in, low, high, ids, cells, depth, basis, props, sems
):
    rows, cols = levels.shape
    copies = [(ids_in, ids), (props_in, props)]
    ends = ((0, 0), (rows - HALO, rows - 16))
    for side, (r0, w0) in enumerate(ends):
        rs = pl.ds(r0, HALO)
        copies.append((sea.at[:, rs, :], cells.at[side, 0]))
        copies.append((vel.at[0, :, rs, :], cells.at[side, 1]))
        copies.append((vel.at[1, :, rs, :], cells.at[side, 2]))
        copies.append((levels.at[pl.ds(w0, 16), :], depth.at[side]))
        copies.append((wind.at[:, pl.ds(w0, 16), :], basis.at[side]))
    started = [pltpu.make_async_copy(a, b, sems.at[n]) for n, (a, b) in enumerate(copies)]
    for copy in started:
        copy.start()
    for copy in started:
        copy.wait()
    coeff = coefficients(members, ids, props)
    for side, out in ((0, low), (1, high)):
        keep = slice(0, HALO) if side == 0 else slice(16 - HALO, 16)
        force = forcing_rows(coeff, basis.at[side], members, keep)
        blocks = [cells[side, i, m] for i in range(3) for m in range(members)]
        blocks += force
        rest = slice(HALO, 16) if side == 0 else slice(0, 16 - HALO)
        blocks += [depth[side, part, :].astype(F32) for part in (keep, rest)]
        for g in range(0, len(blocks), 2):
            pair = jnp.concatenate(blocks[g : g + 2], axis=0)
            out[g * HALO : (g + 2) * HALO, :] = pair.astype(BF16)


def planar_kernel(members, ids, sea, vel, levels, wind, props, out, side):
    rows, cols = levels.shape
    patches = cols // PW
    coeff = coefficients(members, ids, props)
    strips = [
        forcing_rows(coeff, wind.at[:, pl.ds(r0, 16), :], members) for r0 in range(0, rows, 16)
    ]
    force = jnp.concatenate([strip[m] for m in range(members) for strip in strips], axis=0)
    depth = levels[...].astype(F32)
    matrix = plane_matrix(cols)
    scale = 1.0 / GRAVITY
    full = (members * rows, cols)
    fields = [sea[...].reshape(full), vel[0].reshape(full), vel[1].reshape(full), force, depth]
    west = [pltpu.roll(depth[:, cols - LANES :], 1, 1)] * members
    side[5 * rows : 6 * rows, :] = edges_of(west, west, patches).astype(BF16)
    for i, value in enumerate(fields):
        starts = [m * rows if i < 4 else 0 for m in range(members)]
        edge = edges_of(
            [value[r : r + rows, :LANES] for r in starts],
            [value[r : r + rows, cols - LANES :] for r in starts],
            patches,
        )
        side[i * rows : (i + 1) * rows, :] = edge.astype(BF16)
        if i < 4:
            spread = moved(value if i == 0 else value * scale, matrix)
        else:
            spread = jnp.dot(value.astype(BF16), matrix, preferred_element_type=F32)
        parts = [spread[r : r + rows] for r in starts]
        for k, plane in enumerate(planes_from(parts, patches)):
            out[i, k] = plane


def starts_of(i, members):
    if i < 4:
        return [(i * members + m) * HALO for m in range(members)]
    return [(4 * members + i - 4) * HALO] * members


def rim_kernel(members, patches, south, north, side, out):
    rows = side.shape[0] // 6
    cols = south.shape[1]
    low, high = south[...].astype(F32), north[...].astype(F32)

    def edges(plain, i, turn):
        starts = starts_of(i, members)
        lasts = [plain[s : s + HALO, cols - LANES :] for s in starts]
        return edges_of(
            [plain[s : s + HALO, :LANES] for s in starts],
            [turned(last, turn) for last in lasts],
            patches,
        )

    wholes = []
    for i in range(6):
        ends = [edges(plain, min(i, 4), 1 if i == 5 else 0) for plain in (low, high)]
        own = side[i * rows : (i + 1) * rows, :].astype(F32)
        wholes.append(jnp.concatenate([ends[0], own, ends[1]], axis=0))
    wide = rows + 2 * HALO
    for n in range(3):
        pair = wholes[2 * n] + pltpu.roll(wholes[2 * n + 1], 2 * HALO, 1)
        out[n * wide : (n + 1) * wide, :] = pair.astype(BF16)
    behind = edges(low, 5, 0)
    out[3 * wide : 3 * wide + 2 * HALO, :] = jnp.concatenate([behind, behind], axis=0).astype(BF16)


def rims_of(own, from_east, from_west, patches):
    place = lane_ids(own.shape[0]) % patches
    out = []
    for shift in (0, 2 * HALO):
        out.append(
            jnp.where(
                place < 2 * HALO,
                turned(own, -shift),
                jnp.where(
                    place < 3 * HALO,
                    turned(from_east, 2 * HALO - shift),
                    turned(from_west, -2 * HALO - shift),
                ),
            )
        )
    return out


def prepare_kernel(
    members,
    rows,
    cols,
    lat_count,
    south,
    north,
    planes,
    weight,
    ids_col,
    props,
    w_in,
    b_in,
    w_out,
    state,
    force,
    ends,
    hu,
    hv,
    hvu,
    cu,
    cv,
    cv_up,
    w_planes,
    low_in,
    params,
    low_own,
    upper_own,
    w_sum,
    out_cat,
    depth,
    w_rows,
):
    member_terms(
        members, ids_col, props, w_in, b_in, w_out, low_in, params, low_own, upper_own, w_sum, out_cat
    )
    patches = cols // PW
    height = rows + 2 * PAD
    wide = rows + 2 * HALO
    edge_rows = (slice(0, HALO), slice(height - HALO, height))
    homes = (state.at[0], state.at[1], state.at[2], force, depth)
    for i, home in enumerate(homes):
        home[0:PW, PAD : PAD + rows, :] = planes[i]
        if i != 3:
            for p in range(PW):
                for rs in edge_rows:
                    home[p, rs, :] = jnp.zeros((HALO, LANES), F32)
    matrix = plane_matrix(cols)
    for got, r0 in ((south, PAD - HALO), (north, PAD + rows)):
        spread = jnp.dot(got[...], matrix, preferred_element_type=F32)
        for i, home in enumerate(homes):
            parts = [spread[s : s + HALO] for s in starts_of(i, members)]
            for k, plane in enumerate(planes_from(parts, patches)):
                home[k, r0 : r0 + HALO, :] = plane if i in (0, 4) else plane * (1.0 / GRAVITY)
        if r0 < PAD:
            parts = [spread[s : s + HALO] for s in starts_of(5, members)]
            for k, plane in enumerate(planes_from(parts, patches)):
                depth[k, 0:HALO, :] = plane
    span = slice(PAD - HALO, PAD + rows + HALO)
    row, inside = row_ids(rows, lat_count)
    place = row.astype(F32)
    total = lat_count * rows
    cu[span, :] = jnp.where(inside, 0.25 * (CORI_BASE + CORI_SLOPE * (place + 0.5) / total), 0.0)
    cv[span, :] = jnp.where(inside, 0.25 * (CORI_BASE + CORI_SLOPE * place / total), 0.0)
    above = (row >= -1) & (row < total - 1)
    cv_up[span, :] = jnp.where(above, 0.25 * (CORI_BASE + CORI_SLOPE * (place + 1) / total), 0.0)
    for p in range(PW):
        here = depth[p, span, :]
        if p > 0:
            hu[p, span, :] = HALF_DEPTH * (here + depth[p - 1, span, :])
        vertical(depth.at[p], hv.at[p], hvu.at[p], inside, rows)
    ends[0] = depth[0, 0:height]
    ends[1] = depth[PW - 1, 0:height]
    for h in range(w_rows.shape[0]):
        cs = slice(h * LANES, (h + 1) * LANES)
        w_rows[h] = weight[:, cs].astype(F32)
        w_planes[:, cs] = jnp.concatenate(
            [w_rows[h, pl.ds(k, PH, stride=PW), :] for k in range(PW)], axis=0
        ).astype(BF16)


def row_ids(rows, lat_count):
    wide = rows + 2 * HALO
    row = lax.broadcasted_iota(jnp.int32, (wide, LANES), 0) + (lax.axis_index("lat") * rows - HALO)
    return row, (row >= 0) & (row < lat_count * rows)


def vertical(depth, hv, hvu, inside, rows):
    span = slice(PAD - HALO, PAD + rows + HALO)
    here = depth[span, :]
    below = depth[PAD - HALO - 1 : PAD + rows + HALO - 1, :]
    above = depth[PAD - HALO + 1 : PAD + rows + HALO + 1, :]
    hv[span, :] = HALF_DEPTH * (here + below)
    hvu[span, :] = jnp.where(inside, HALF_DEPTH * (here + above), 0.0)


def back_kernel(members, state, sea, vel):
    rows, cols = sea.shape[1:]
    patches = cols // PW
    per = LANES // patches
    matrix = plane_matrix(cols, inverse=True)
    segment = lane_ids(rows) // patches
    for i in range(3):
        parts = []
        for m in range(members):
            groups = []
            for g in range(PW // per):
                pieces = [
                    turned(state[i, g * per + j, PAD : PAD + rows, :], (j - m) * patches)
                    for j in range(per)
                ]
                groups.append(by_segment(pieces, segment))
            parts.append(jnp.concatenate(groups, axis=1))
        value = moved(jnp.concatenate(parts, axis=0), matrix)
        for m in range(members):
            part = value[m * rows : (m + 1) * rows]
            if i == 0:
                sea[m] = part
            else:
                vel[i - 1, m] = part * GRAVITY


def flow_step(src, src_rim, dst, dst_rim, force, force_rim, hus, hvs, hvus, cu, cv, cv_up, last_mask, rows, patches, ending):
    strip = PW
    wide = rows + 2 * HALO
    start = PAD - HALO
    keep = 1.0 - DRAG_RATE
    here = pl.ds(start, wide)
    last = lane_ids(wide) % patches == patches - 1

    def wrap_left(plane, rim):
        return pltpu.roll(jnp.where(last, rim, plane), 1, 1)

    def wrap_right(plane, rim):
        return jnp.where(last, pltpu.roll(rim, PW - 1, 1), pltpu.roll(plane, LANES - 1, 1))

    def of(planes, rim, i, p):
        return rim.at[i] if p == strip else planes.at[i, p]

    def new_level(p, fx, fx_right):
        n = of(src, src_rim, 2, p)[here, :]
        n_up = pltpu.roll(n, wide - 1, 0)
        fy = hvus[p][here, :] * n_up - hvs[p][here, :] * n
        level = of(src, src_rim, 0, p)[here, :] - ((fx_right - fx) + fy)
        of(dst, dst_rim, 0, p)[here, :] = level
        return level, n, n + n_up

    def new_flow(p, e, e_right, n, v, level, level_left):
        u = e + e_right
        push = force_rim[here, :] if p == strip else force[p, here, :]
        of(dst, dst_rim, 1, p)[here, :] = keep * e + cu[here, :] * v - (level - level_left) + push
        below = pltpu.roll(level - cv_up[here, :] * u, 1, 0)
        north = keep * n - cv[here, :] * u - level + below
        home = of(dst, dst_rim, 2, p)
        home[pl.ds(start, wide - HALO), :] = north[: wide - HALO]
        home[pl.ds(start + wide - HALO, HALO), :] = north[wide - HALO :] * last_mask

    e_rim = src_rim[1, here, :]
    fx_rim = hus[strip][here, :] * e_rim
    level_rim, n_rim, vs_rim = new_level(strip, fx_rim, pltpu.roll(fx_rim, LANES - 1, 1))
    if not ending:
        new_flow(
            strip,
            e_rim,
            pltpu.roll(e_rim, LANES - 1, 1),
            n_rim,
            vs_rim + pltpu.roll(vs_rim, 1, 1),
            level_rim,
            pltpu.roll(level_rim, 1, 1),
        )
    e = src[1, 0, here, :]
    e_end = wrap_right(e, e_rim)
    level_last, n_last, vs_last = new_level(
        PW - 1, hus[PW - 1][here, :] * src[1, PW - 1, here, :], hus[PW + 1][here, :] * e_end
    )
    level_left = wrap_left(level_last, level_rim)
    vs_left = wrap_left(vs_last, vs_rim)
    fx = hus[0][here, :] * e
    for p in range(PW):
        if p < PW - 1:
            e_right = src[1, p + 1, here, :]
            fx_right = hus[p + 1][here, :] * e_right
            level, n, vs = new_level(p, fx, fx_right)
        else:
            e_right, fx_right = e_end, None
            level, n, vs = level_last, n_last, vs_last
        new_flow(p, e, e_right, n, vs + vs_left, level, level_left)
        level_left, vs_left, e, fx = level, vs, e_right, fx_right


def flow_kernel(
    members,
    rows,
    cols,
    lat_count,
    state,
    force,
    ends,
    hu,
    hv,
    hvu,
    cu,
    cv,
    cv_up,
    w_planes,
    side,
    east,
    west,
    partial,
    gram,
    final,
    state_b,
    rim_a,
    rim_b,
    force_rim,
    depth_rim,
    west_rim,
    hu_rim,
    hv_rim,
    hvu_rim,
    patch_t,
    slope,
    state_a,
):
    patches = cols // PW
    lat = lax.axis_index("lat")
    height = rows + 2 * PAD
    wide = rows + 2 * HALO
    span = slice(PAD - HALO, PAD + rows + HALO)
    state_a[:, :, span, :] = state[:, :, span, :]
    depth_rim[height - HALO : height, :] = jnp.zeros((HALO, LANES), F32)
    behind = slice(3 * wide, 3 * wide + 2 * HALO)
    got = [ref[behind, :].astype(F32)[:HALO] for ref in (side, east, west)]
    depth_rim[0:HALO, :] = rims_of(*got, patches)[0]
    rim_homes = (rim_a.at[0], rim_a.at[1], rim_a.at[2], force_rim, depth_rim, west_rim)
    for n in range(3):
        rs = slice(n * wide, (n + 1) * wide)
        got = [ref[rs, :].astype(F32) for ref in (side, east, west)]
        for i, rim in zip((2 * n, 2 * n + 1), rims_of(*got, patches)):
            rim_homes[i][span, :] = rim * (1.0 / GRAVITY) if i in (1, 2, 3) else rim
    _, inside = row_ids(rows, lat_count)
    last = lane_ids(wide) % patches == patches - 1
    rim = depth_rim[span, :]
    left = pltpu.roll(jnp.where(last, rim, ends[1, span, :]), 1, 1)
    first = HALF_DEPTH * (ends[0, span, :] + left)
    outer = lane_ids(wide) % patches >= 3 * HALO
    rim = HALF_DEPTH * (rim + jnp.where(outer, west_rim[span, :], pltpu.roll(rim, 1, 1)))
    hu_rim[0, span, :] = first
    hu_rim[1, span, :] = rim
    hu_rim[2, span, :] = jnp.where(
        last, pltpu.roll(rim, PW - 1, 1), pltpu.roll(first, LANES - 1, 1)
    )
    vertical(depth_rim, hv_rim, hvu_rim, inside, rows)
    hus = [hu_rim.at[0]] + [hu.at[p] for p in range(1, PW)] + [hu_rim.at[1], hu_rim.at[2]]
    hvs = [hv.at[p] for p in range(PW)] + [hv_rim]
    hvus = [hvu.at[p] for p in range(PW)] + [hvu_rim]

    last_mask = jnp.where(lat < lat_count - 1, 1.0, 0.0)
    count = rows // PH

    def embed_step(state, turn, sub):
        step = 2 * turn + sub
        total = None
        for b in range(count):
            cells = state[0, 0:PW, PAD + b * PH : PAD + (b + 1) * PH, :].reshape(PW * PH, LANES)
            cells_t = cells.T.astype(BF16)
            act = jnp.tanh(jnp.dot(cells_t, w_planes[...], preferred_element_type=F32))
            total = act if total is None else total + act
            fall = (1.0 - act * act).astype(BF16)
            for m in range(members):
                rs = slice(m * patches, (m + 1) * patches)
                to = slice(b * patches, (b + 1) * patches)
                patch_t[m, to, :] = cells_t[rs]
                slope[m, to, :] = fall[rs]
        sums = jnp.sum(total.reshape(members, patches, total.shape[1]), axis=1)
        partial[turn, sub * members : (sub + 1) * members, :] = sums
        for m in range(members):
            gram[step * members + m] = lax.dot_general(
                patch_t[m], slope[m], (((0,), (0,)), ((), ())), preferred_element_type=F32
            )

    def step_of(src, src_rim, dst, dst_rim, ending=False):
        flow_step(
            src, src_rim, dst, dst_rim, force, force_rim, hus, hvs, hvus, cu, cv, cv_up, last_mask, rows, patches, ending
        )

    one, two = (state_a, rim_a), (state_b, rim_b)
    step_of(*one, *two)
    for step in range(1, STEPS):
        src, dst = (two, one) if step % 2 else (one, two)
        step_of(*src, *dst, step == STEPS - 1)
        embed_step(src[0], (step - 1) // 2, (step - 1) % 2)
    inner = slice(PAD, PAD + rows)
    final[:, :, inner, :] = state_a[:, :, inner, :]
    embed_step(state_a, STEPS // 2 - 1, 1)


def split(value):
    high = value.astype(BF16)
    return high, (value - high.astype(F32)).astype(BF16)


def dot(a, b, ca=1, cb=0):
    return lax.dot_general(a, b, (((ca,), (cb,)), ((), ())), preferred_element_type=F32)


def mm(a, b, ca=1, cb=0):
    return dot(a[0], b[0], ca, cb) + (dot(a[0], b[1], ca, cb) + dot(a[1], b[0], ca, cb))


def member_terms(
    members, ids_col, props, w_in, b_in, w_out, low_in, ends, low_own, upper_own, w_sum, out_cat
):
    count = props.shape[0]
    half = props.shape[1] // 2
    hot = jnp.where(ids_col[...] == lax.broadcasted_iota(jnp.int32, (count, count), 1), 1.0, 0.0)
    params = jnp.dot(hot, props[...], precision=PRECISE, preferred_element_type=F32)
    low = mm(split(params[:, :half]), split(w_in[:half, :])) + b_in[...]
    ends[...] = params
    low_in[...] = low
    samples = low_own.shape[0]
    slot = lax.broadcasted_iota(jnp.int32, (samples, count), 1)
    row = lax.broadcasted_iota(jnp.int32, (samples, count), 0)
    hot = jnp.where(slot == lax.axis_index("grp") * members + row % members, 1.0, 0.0)
    low_own[...] = jnp.dot(hot, low, precision=PRECISE, preferred_element_type=F32)
    upper_own[...] = jnp.dot(hot, params[:, half:], precision=PRECISE, preferred_element_type=F32)
    high, rest = split(w_in[half:, :])
    w_sum[0] = high
    w_sum[1] = rest
    high, rest = split(w_out[...].T)
    out_cat[...] = jnp.concatenate([high, high, rest], axis=1)


def repeated(rows, count):
    return jnp.concatenate([rows] * count, axis=0)


def flow_grads(lower_in, upper, summary, w_sum, out_cat, b_out):
    half = upper.shape[1]
    width = 2 * half
    sums = split(summary)
    hidden = jnp.tanh(mm(sums, w_sum) + lower_in)
    hid = split(hidden)
    both = dot(hid[0], out_cat[:, width:])
    raw = both[:, :width] + both[:, width:] + dot(hid[1], out_cat[:, :width]) + b_out[...]
    log_scale = jnp.tanh(raw[:, :half])
    grown = upper * jnp.exp(log_scale)
    latent = grown + raw[:, half:]
    d_scale = (latent * grown - 1.0) * (1.0 - log_scale * log_scale)
    d_raw = jnp.concatenate([d_scale, latent], axis=1)
    d_r = split(d_raw)
    d_hidden = dot(jnp.concatenate([d_r[0], d_r[1], d_r[0]], axis=1), out_cat[...], 1, 1)
    d_hidden = d_hidden * (1.0 - hidden * hidden)
    return sums, hid, d_raw, d_r, d_hidden


def local_kernel(
    inv_root, mine, theirs, low_in, upper, w_sum, out_cat, b_out, gram, kept, sent, own, total
):
    sums = (mine[...] + theirs[...]) * inv_root
    count = sums.shape[0]
    items = own.shape[0]
    for part in range(count // items):

        @pl.when(lax.axis_index("lon") == part)
        def _():
            own[...] = sums[part * items : (part + 1) * items, :]

    w_pair = (w_sum[0], w_sum[1])
    d_hidden = flow_grads(low_in[...], upper[...], sums, w_pair, out_cat, b_out)[-1]
    d_summary = mm(split(d_hidden), w_pair, 1, 1) * inv_root
    acc = gram[0] * d_summary[0:1, :]
    for i in range(1, count):
        acc = acc + gram[i] * d_summary[i : i + 1, :]
    total[...] = acc
    cells = acc.shape[0] // 2
    core = lax.axis_index("grp") % 2
    kept[...] = total[pl.ds(pl.multiple_of(core * cells, 8), cells), :]
    sent[...] = total[pl.ds(pl.multiple_of((1 - core) * cells, 8), cells), :]


def couple_kernel(
    members, lat_count, grp_count, order, summary, low_in, ends, w_sum, out_cat, b_out, rows, square, sorted_sums, staged
):
    per = summary.shape[0] // len(order)
    for index, (lat_flip, grp_flip) in enumerate(order):
        block = (lax.axis_index("lat") ^ lat_flip) * grp_count + (lax.axis_index("grp") ^ grp_flip)
        sorted_sums[pl.ds(pl.multiple_of(block * per, per), per), :] = summary[
            index * per : (index + 1) * per, :
        ]
    params = ends[...]
    half = params.shape[1] // 2
    groups = [slice(g * members, (g + 1) * members) for g in range(grp_count)]
    steps = per // members
    spread = lambda value: jnp.concatenate(
        [repeated(value[rs], steps) for rs in groups] * lat_count, axis=0
    )
    lower = spread(params[:, :half])
    sums, hid, d_raw, d_r, d_hidden = flow_grads(
        spread(low_in[...]),
        spread(params[:, half:]),
        sorted_sums[...],
        (w_sum[0], w_sum[1]),
        out_cat,
        b_out,
    )
    low = split(lower)
    context = [jnp.concatenate([sums[n], low[n]], axis=1) for n in range(2)]
    g_in = mm(context, split(d_hidden), 0, 0)
    width = 2 * half
    both = dot(hid[0], jnp.concatenate(d_r, axis=1), 0, 0)
    g_out = both[:, :width] + both[:, width:] + dot(hid[1], d_r[0], 0, 0)
    g_in_b = jnp.sum(d_hidden, axis=0, keepdims=True)
    g_out_b = jnp.sum(d_raw, axis=0, keepdims=True)
    hidden = d_hidden.shape[1]
    per_row = hidden // LANES
    feats = summary.shape[1]
    fold = LANES // width
    base = (half + feats) * per_row
    after = base + per_row
    tail = after + hidden // fold
    rows[base:, :] = jnp.zeros((rows.shape[0] - base, LANES), F32)
    for q in range(per_row):
        cs = slice(q * LANES, (q + 1) * LANES)
        rows[pl.ds(q, half, stride=per_row), :] = g_in[feats:, cs]
        rows[pl.ds(half * per_row + q, feats, stride=per_row), :] = g_in[:feats, cs]
        rows[base + q : base + q + 1, :] = g_in_b[:, cs]
    staged[...] = jnp.concatenate([g_out, jnp.zeros((hidden, LANES - width), F32)], axis=1)
    packed = jnp.zeros((hidden // fold, LANES), F32)
    for j in range(fold):
        packed = packed + turned(staged[pl.ds(j, hidden // fold, stride=fold), :], j * width)
    rows[after:tail, :] = packed
    rows[tail : tail + 1, :] = jnp.concatenate(
        [g_out_b, jnp.zeros((1, LANES - width), F32)], axis=1
    )
    whole = rows[...]
    square[...] = jnp.sum(whole * whole, axis=0, keepdims=True)


def finish_kernel(count, mine, theirs, couple, square, out, whole):
    core = lax.axis_index("grp") % 2
    cells = mine.shape[0]
    per_row = mine.shape[1] // LANES
    for h in range(per_row):
        cs = slice(h * LANES, (h + 1) * LANES)
        whole[h, pl.ds(pl.multiple_of(core * cells, 8), cells), :] = mine[:, cs]
        whole[h, pl.ds(pl.multiple_of((1 - core) * cells, 8), cells), :] = theirs[:, cs]
    conv = whole[...]
    squares = jnp.sum(conv * conv) + jnp.sum(square[...])
    scale = -lax.rsqrt(jnp.full((1, 1), squares, F32) / count + EPSILON)
    for r in range(PH):
        for h in range(per_row):
            part = whole[h, pl.ds(r, PW, stride=PH), :]
            out[pl.ds(r * PW * per_row + h, PW, stride=per_row), :] = part * scale
    used = 2 * cells * per_row
    out[used : used + couple.shape[0], :] = couple[...] * scale


def neighbour(value, axis, step):
    count = lax.axis_size(axis)
    pairs = [(i, (i + step) % count) for i in range(count)]
    return lax.ppermute(value, axis, pairs)


def from_lat(value, step):
    count = lax.axis_size("lat")
    return lax.ppermute(value, "lat", [(i, i + step) for i in range(count) if 0 <= i + step < count])


def swapped(value, axis, flip):
    count = lax.axis_size(axis)
    return lax.ppermute(value, axis, [(i, i ^ flip) for i in range(count)])


def flips(axis):
    count = lax.axis_size(axis)
    return [1 << i for i in range(count.bit_length() - 1)]


def shape(*dims, dtype=F32):
    return jax.ShapeDtypeStruct(dims, dtype)


def shards(
    sea_surface,
    velocity,
    levels,
    wind_basis,
    proposals,
    member_ids,
    conv_weight,
    couple_in,
    couple_in_bias,
    couple_out,
    couple_out_bias,
):
    members, rows, cols = sea_surface.shape
    lat_count, lon_count = lax.axis_size("lat"), lax.axis_size("lon")
    grp_count = lax.axis_size("grp")
    cells, feats = conv_weight.shape
    hid, width = couple_out.shape
    patches = cols // PW
    samples = STEPS * members
    groups = (4 * members + 2) * HALO
    height = rows + 2 * PAD
    inv_root = 1.0 / math.sqrt(rows // PH * (cols * lon_count // PW))

    anywhere = pl.BlockSpec(memory_space=pl.ANY)
    low, high = pl.pallas_call(
        lambda *refs: pack_kernel(members, *refs),
        out_shape=(shape(groups, cols, dtype=BF16), shape(groups, cols, dtype=BF16)),
        in_specs=[anywhere] * 6,
        out_specs=(vmem(), vmem()),
        scratch_shapes=[
            pltpu.SMEM(member_ids.shape, jnp.int32),
            pltpu.VMEM((2, 3, members, HALO, cols), F32),
            pltpu.VMEM((2, 16, cols), jnp.int32),
            pltpu.VMEM((2, wind_basis.shape[0], 16, cols), BF16),
            pltpu.VMEM(proposals.shape, F32),
            pltpu.SemaphoreType.DMA((12,)),
        ],
        compiler_params=params_of(60),
        name="pack_rows",
    )(member_ids, sea_surface, velocity, levels, wind_basis, proposals)

    south = from_lat(high, 1)
    north = from_lat(low, -1)

    planes, side = pl.pallas_call(
        lambda *refs: planar_kernel(members, *refs),
        out_shape=(shape(5, PW, rows, LANES), shape(6 * rows, LANES, dtype=BF16)),
        in_specs=[smem()] + [vmem()] * 5,
        out_specs=(vmem(), vmem()),
        compiler_params=params_of(32),
        cost_estimate=pl.CostEstimate(flops=2 * 10**9, bytes_accessed=6 * MEBI, transcendentals=0),
        name="to_planes",
    )(member_ids, sea_surface, velocity, levels, wind_basis, proposals)

    wide = rows + 2 * HALO
    rim = pl.pallas_call(
        lambda *refs: rim_kernel(members, patches, *refs),
        out_shape=shape(3 * wide + 2 * HALO, LANES, dtype=BF16),
        in_specs=[vmem()] * 3,
        out_specs=vmem(),
        compiler_params=params_of(16),
        name="rim",
    )(south, north, side)
    west = neighbour(rim, "lon", 1)
    east = west if lon_count == 2 else neighbour(rim, "lon", -1)

    def after(value, *others):
        return lax.optimization_barrier((value,) + others)[0]

    b_out = couple_out_bias.reshape(1, -1)
    plane = (PW, height + HALO, LANES)
    prepared = pl.pallas_call(
        lambda *refs: prepare_kernel(members, rows, cols, lat_count, *refs),
        out_shape=(
            shape(3, *plane),
            shape(*plane),
            shape(2, height, LANES),
            shape(*plane),
            shape(*plane),
            shape(*plane),
            shape(height, LANES),
            shape(height, LANES),
            shape(height, LANES),
            shape(cells, feats, dtype=BF16),
            shape(proposals.shape[0], hid),
            shape(*proposals.shape),
            shape(samples, hid),
            shape(samples, width // 2),
            shape(2, feats, hid, dtype=BF16),
            shape(hid, 3 * width, dtype=BF16),
        ),
        in_specs=[vmem()] * 9,
        out_specs=(vmem(),) * 16,
        scratch_shapes=[
            pltpu.VMEM(plane, F32),
            pltpu.VMEM((feats // LANES, cells, LANES), F32),
        ],
        compiler_params=params_of(16),
        cost_estimate=pl.CostEstimate(flops=10**9, bytes_accessed=4 * MEBI, transcendentals=0),
        name="prepare",
    )(
        south,
        north,
        planes,
        conv_weight,
        member_ids.reshape(-1, 1),
        proposals,
        couple_in,
        couple_in_bias.reshape(1, -1),
        couple_out.T,
    )
    prepared, (low_in, ends, low_own, upper_own, w_sum, out_cat) = prepared[:10], prepared[10:]

    partial, gram, final = pl.pallas_call(
        lambda *refs: flow_kernel(members, rows, cols, lat_count, *refs),
        out_shape=(
            shape(STEPS // 2, 2 * members, feats),
            shape(samples, cells, feats),
            shape(3, *plane),
        ),
        in_specs=[vmem()] * 13,
        out_specs=(vmem(),) * 3,
        scratch_shapes=[
            pltpu.VMEM((3, *plane), F32),
            pltpu.VMEM((3, height, LANES), F32),
            pltpu.VMEM((3, height, LANES), F32),
            pltpu.VMEM((height, LANES), F32),
            pltpu.VMEM((height, LANES), F32),
            pltpu.VMEM((height, LANES), F32),
            pltpu.VMEM((3, height, LANES), F32),
            pltpu.VMEM((height, LANES), F32),
            pltpu.VMEM((height, LANES), F32),
            pltpu.VMEM((members, rows // PH * patches, cells), BF16),
            pltpu.VMEM((members, rows // PH * patches, feats), BF16),
            pltpu.VMEM((3, *plane), F32),
        ],
        compiler_params=params_of(32),
        name="flow_embed",
    )(*prepared, rim, east, west)
    partial = partial.reshape(samples, feats)

    if lon_count == 2:
        others = swapped(partial, "lon", 1)
    else:
        others = lax.psum(partial, "lon") - partial
    surface_out, velocity_out = pl.pallas_call(
        lambda *refs: back_kernel(members, *refs),
        out_shape=(shape(members, rows, cols), shape(2, members, rows, cols)),
        in_specs=[vmem()],
        out_specs=(vmem(), vmem()),
        compiler_params=params_of(24),
        cost_estimate=pl.CostEstimate(flops=2 * 10**9, bytes_accessed=6 * MEBI, transcendentals=0),
        name="from_planes",
    )(final)

    others, surface_out, velocity_out = lax.optimization_barrier((others, surface_out, velocity_out))
    summaries = (partial + others) * inv_root

    items = samples // lon_count
    kept, sent, own = pl.pallas_call(
        lambda *refs: local_kernel(inv_root, *refs),
        out_shape=(shape(cells // 2, feats), shape(cells // 2, feats), shape(items, feats)),
        in_specs=[vmem()] * 8,
        out_specs=(vmem(),) * 3,
        scratch_shapes=[pltpu.VMEM((cells, feats), F32)],
        compiler_params=params_of(16),
        name="local_loss",
    )(partial, others, low_own, upper_own, w_sum, out_cat, b_out, gram)

    def gather(axis, flip):
        both = jnp.concatenate([gathered, swapped(gathered, axis, flip)], axis=0)
        return both, order + [(a ^ flip, b) if axis == "lat" else (a, b ^ flip) for a, b in order]

    gathered, order = summaries.astype(jnp.float16), [(0, 0)]
    gathered, order = gather("grp", 2)
    conv = kept + swapped(sent, "grp", 1)
    if lon_count == 2:
        corner = lax.ppermute(
            conv,
            ("lon", "grp"),
            [(i, (i // grp_count ^ 1) * grp_count + (i % grp_count ^ 2)) for i in range(2 * grp_count)],
        )
        by_lon = swapped(conv, "lon", 1)
        gathered = after(gathered, by_lon)
        conv = (conv + corner) + (swapped(conv, "grp", 2) + by_lon)
    else:
        conv = conv + swapped(conv, "grp", 2)
        for flip in flips("lon"):
            conv = conv + swapped(conv, "lon", flip)
    for flip in reversed(flips("lat")):
        by_lat = swapped(conv, "lat", flip)
        if flip > 1:
            gathered, order = gather("lat", flip)
            gathered = after(gathered, conv)
            conv = conv + by_lat
    gathered, order = gather("lat", 1)
    gathered = after(gathered, conv)
    gathered, order = gather("grp", 1)

    low_rows = (couple_in.size + hid + couple_out.size) // LANES + 1
    low_rows = -(-low_rows // 8) * 8
    count = cells * feats + couple_in.size + hid + couple_out.size + width
    couple, square = pl.pallas_call(
        lambda *refs: couple_kernel(members, lat_count, grp_count, order, *refs),
        out_shape=(shape(low_rows, LANES), shape(1, LANES)),
        in_specs=[vmem()] * 6,
        out_specs=(vmem(), vmem()),
        scratch_shapes=[
            pltpu.VMEM((len(order) * samples, feats), F32),
            pltpu.VMEM((hid, LANES), F32),
        ],
        compiler_params=params_of(24),
        cost_estimate=pl.CostEstimate(flops=3 * 10**9, bytes_accessed=3 * MEBI, transcendentals=0),
        name="couple_grads",
    )(gathered.astype(F32), low_in, ends, w_sum, out_cat, b_out)

    conv = conv + after(by_lat, couple, square)
    conv_other = swapped(conv, "grp", 1)

    stepped = pl.pallas_call(
        lambda *refs: finish_kernel(count, *refs),
        out_shape=shape(cells * feats // LANES + low_rows, LANES),
        in_specs=[vmem()] * 4,
        out_specs=vmem(),
        scratch_shapes=[pltpu.VMEM((feats // LANES, cells, LANES), F32)],
        compiler_params=params_of(16),
        name="finish",
    )(conv, conv_other, couple, square)
    weight_step = stepped.reshape(-1)[:count]

    return (surface_out, velocity_out, own.reshape(1, 1, 1, items, feats), weight_step)


def solution(mesh):
    in_specs = (
        P("grp", "lat", "lon"),
        P(None, "grp", "lat", "lon"),
        P("lat", "lon"),
        P(None, "lat", "lon"),
        P(),
        P(),
        P(),
        P(),
        P(),
        P(),
        P(),
    )
    out_specs = (
        P("grp", "lat", "lon"),
        P(None, "grp", "lat", "lon"),
        P("lon", "lat", "grp", None, None),
        P(),
    )
    return jax.shard_map(shards, mesh=mesh, in_specs=in_specs, out_specs=out_specs, check_vma=False)
```

```python
import math

import jax
import jax.numpy as jnp
from jax import lax
from jax.experimental import pallas as pl
from jax.experimental.pallas import tpu as pltpu
from jax.sharding import PartitionSpec as P

STEPS = 8
NLEV = 50
PH = 8
PW = 16
HALO = 8
PAD = 16

GRAVITY = 0.45
DRAG_RATE = 0.02
CORI_BASE = 0.05
CORI_SLOPE = 0.1
WIND_SCALE = 0.05
EPSILON = 1e-06
PRECISE = lax.Precision.HIGHEST
F32 = jnp.float32
BF16 = jnp.bfloat16
LANES = 128
MEBI = 2**20
HALF_DEPTH = 0.5 * GRAVITY / NLEV


def vmem():
    return pl.BlockSpec(memory_space=pltpu.VMEM)


def smem():
    return pl.BlockSpec(memory_space=pltpu.SMEM)


def params_of(mebi, **rest):
    return pltpu.CompilerParams(vmem_limit_bytes=mebi * MEBI, **rest)


def lane_ids(rows):
    return lax.broadcasted_iota(jnp.int32, (rows, LANES), 1)


def plane_matrix(cols, inverse=False):
    patches = cols // PW
    src = lax.broadcasted_iota(jnp.int32, (cols, cols), 1 if inverse else 0)
    dst = lax.broadcasted_iota(jnp.int32, (cols, cols), 0 if inverse else 1)
    return jnp.where(src == (dst % patches) * PW + dst // patches, 1.0, 0.0).astype(BF16)


def moved(value, matrix):
    both = jnp.dot(jnp.concatenate(split(value), axis=0), matrix, preferred_element_type=F32)
    return both[: value.shape[0]] + both[value.shape[0] :]


def by_segment(pieces, segment):
    out = pieces[-1]
    for index in range(len(pieces) - 2, -1, -1):
        out = jnp.where(segment == index, pieces[index], out)
    return out


def turned(value, shift):
    shift = shift % LANES
    return value if shift == 0 else pltpu.roll(value, shift, 1)


def planes_from(parts, patches):
    rows = parts[0].shape[0]
    per = LANES // patches
    segment = lane_ids(rows) // patches
    planes = []
    for k in range(PW):
        group, place = divmod(k, per)
        block = slice(group * LANES, (group + 1) * LANES)
        planes.append(
            by_segment(
                [turned(part[:, block], (m - place) * patches) for m, part in enumerate(parts)],
                segment,
            )
        )
    return planes


def edges_of(firsts, lasts, patches):
    rows = firsts[0].shape[0]
    lane = lane_ids(rows)
    out = jnp.zeros((rows, LANES), F32)
    for m, (first, last) in enumerate(zip(firsts, lasts)):
        both = jnp.where(lane < HALO, first, turned(last, 2 * HALO))
        here = (lane >= m * patches) & (lane < m * patches + 2 * HALO)
        out = jnp.where(here, turned(both, m * patches), out)
    return out


def forcing_rows(coeff, basis, members, keep=slice(None)):
    acc = [None] * members
    for k in range(basis.shape[0]):
        value = basis[k].astype(F32)[keep]
        for m in range(members):
            term = coeff[m][:, k : k + 1] * value
            acc[m] = term if acc[m] is None else acc[m] + term
    return acc


def coefficients(members, ids, props):
    base = lax.axis_index("grp") * members
    return [
        props[pl.ds(ids[base + m], 1), :].astype(BF16).astype(F32) * WIND_SCALE
        for m in range(members)
    ]


def pack_kernel(
    members, ids_in, sea, vel, levels, wind, props_in, low, high, ids, cells, depth, basis, props, sems
):
    rows, cols = levels.shape
    copies = [(ids_in, ids), (props_in, props)]
    ends = ((0, 0), (rows - HALO, rows - 16))
    for side, (r0, w0) in enumerate(ends):
        rs = pl.ds(r0, HALO)
        copies.append((sea.at[:, rs, :], cells.at[side, 0]))
        copies.append((vel.at[0, :, rs, :], cells.at[side, 1]))
        copies.append((vel.at[1, :, rs, :], cells.at[side, 2]))
        copies.append((levels.at[pl.ds(w0, 16), :], depth.at[side]))
        copies.append((wind.at[:, pl.ds(w0, 16), :], basis.at[side]))
    started = [pltpu.make_async_copy(a, b, sems.at[n]) for n, (a, b) in enumerate(copies)]
    for copy in started:
        copy.start()
    for copy in started[:2]:
        copy.wait()
    coeff = coefficients(members, ids, props)
    each = (len(copies) - 2) // 2
    for side, out in ((0, low), (1, high)):
        for copy in started[2 + side * each : 2 + (side + 1) * each]:
            copy.wait()
        keep = slice(0, HALO) if side == 0 else slice(16 - HALO, 16)
        force = forcing_rows(coeff, basis.at[side], members, keep)
        blocks = [cells[side, i, m] for i in range(3) for m in range(members)]
        blocks += force
        rest = slice(HALO, 16) if side == 0 else slice(0, 16 - HALO)
        blocks += [depth[side, part, :].astype(F32) for part in (keep, rest)]
        for g in range(0, len(blocks), 2):
            pair = jnp.concatenate(blocks[g : g + 2], axis=0)
            out[g * HALO : (g + 2) * HALO, :] = pair.astype(BF16)


def planar_kernel(members, ids, sea, vel, levels, wind, props, out, side):
    rows, cols = levels.shape
    patches = cols // PW
    coeff = coefficients(members, ids, props)
    strips = [
        forcing_rows(coeff, wind.at[:, pl.ds(r0, 16), :], members) for r0 in range(0, rows, 16)
    ]
    force = jnp.concatenate([strip[m] for m in range(members) for strip in strips], axis=0)
    depth = levels[...].astype(F32)
    matrix = plane_matrix(cols)
    scale = 1.0 / GRAVITY
    full = (members * rows, cols)
    fields = [sea[...].reshape(full), vel[0].reshape(full), vel[1].reshape(full), force, depth]
    west = [pltpu.roll(depth[:, cols - LANES :], 1, 1)] * members
    side[5 * rows : 6 * rows, :] = edges_of(west, west, patches).astype(BF16)
    for i, value in enumerate(fields):
        starts = [m * rows if i < 4 else 0 for m in range(members)]
        edge = edges_of(
            [value[r : r + rows, :LANES] for r in starts],
            [value[r : r + rows, cols - LANES :] for r in starts],
            patches,
        )
        side[i * rows : (i + 1) * rows, :] = edge.astype(BF16)
        if i < 4:
            spread = moved(value if i == 0 else value * scale, matrix)
        else:
            spread = jnp.dot(value.astype(BF16), matrix, preferred_element_type=F32)
        parts = [spread[r : r + rows] for r in starts]
        for k, plane in enumerate(planes_from(parts, patches)):
            out[i, k] = plane


def starts_of(i, members):
    if i < 4:
        return [(i * members + m) * HALO for m in range(members)]
    return [(4 * members + i - 4) * HALO] * members


def rim_kernel(members, patches, south, north, side, out):
    rows = side.shape[0] // 6
    cols = south.shape[1]
    low, high = south[...].astype(F32), north[...].astype(F32)

    def edges(plain, i, turn):
        starts = starts_of(i, members)
        lasts = [plain[s : s + HALO, cols - LANES :] for s in starts]
        return edges_of(
            [plain[s : s + HALO, :LANES] for s in starts],
            [turned(last, turn) for last in lasts],
            patches,
        )

    wholes = []
    for i in range(6):
        ends = [edges(plain, min(i, 4), 1 if i == 5 else 0) for plain in (low, high)]
        own = side[i * rows : (i + 1) * rows, :].astype(F32)
        wholes.append(jnp.concatenate([ends[0], own, ends[1]], axis=0))
    wide = rows + 2 * HALO
    for n in range(3):
        pair = wholes[2 * n] + pltpu.roll(wholes[2 * n + 1], 2 * HALO, 1)
        out[n * wide : (n + 1) * wide, :] = pair.astype(BF16)
    behind = edges(low, 5, 0)
    out[3 * wide : 3 * wide + 2 * HALO, :] = jnp.concatenate([behind, behind], axis=0).astype(BF16)


def rims_of(own, from_east, from_west, patches):
    place = lane_ids(own.shape[0]) % patches
    out = []
    for shift in (0, 2 * HALO):
        out.append(
            jnp.where(
                place < 2 * HALO,
                turned(own, -shift),
                jnp.where(
                    place < 3 * HALO,
                    turned(from_east, 2 * HALO - shift),
                    turned(from_west, -2 * HALO - shift),
                ),
            )
        )
    return out


def prepare_kernel(
    members,
    rows,
    cols,
    lat_count,
    south,
    north,
    planes,
    weight,
    ids_col,
    props,
    w_in,
    b_in,
    w_out,
    state,
    force,
    ends,
    hu,
    hv,
    hvu,
    cu,
    cv,
    cv_up,
    w_planes,
    low_in,
    params,
    low_own,
    upper_own,
    w_sum,
    out_cat,
    depth,
    w_rows,
):
    member_terms(
        members, ids_col, props, w_in, b_in, w_out, low_in, params, low_own, upper_own, w_sum, out_cat
    )
    patches = cols // PW
    height = rows + 2 * PAD
    wide = rows + 2 * HALO
    edge_rows = (slice(0, HALO), slice(height - HALO, height))
    homes = (state.at[0], state.at[1], state.at[2], force, depth)
    for i, home in enumerate(homes):
        home[0:PW, PAD : PAD + rows, :] = planes[i]
        if i != 3:
            for p in range(PW):
                for rs in edge_rows:
                    home[p, rs, :] = jnp.zeros((HALO, LANES), F32)
    matrix = plane_matrix(cols)
    for got, r0 in ((south, PAD - HALO), (north, PAD + rows)):
        spread = jnp.dot(got[...], matrix, preferred_element_type=F32)
        for i, home in enumerate(homes):
            parts = [spread[s : s + HALO] for s in starts_of(i, members)]
            for k, plane in enumerate(planes_from(parts, patches)):
                home[k, r0 : r0 + HALO, :] = plane if i in (0, 4) else plane * (1.0 / GRAVITY)
        if r0 < PAD:
            parts = [spread[s : s + HALO] for s in starts_of(5, members)]
            for k, plane in enumerate(planes_from(parts, patches)):
                depth[k, 0:HALO, :] = plane
    span = slice(PAD - HALO, PAD + rows + HALO)
    row, inside = row_ids(rows, lat_count)
    place = row.astype(F32)
    total = lat_count * rows
    cu[span, :] = jnp.where(inside, 0.25 * (CORI_BASE + CORI_SLOPE * (place + 0.5) / total), 0.0)
    cv[span, :] = jnp.where(inside, 0.25 * (CORI_BASE + CORI_SLOPE * place / total), 0.0)
    above = (row >= -1) & (row < total - 1)
    cv_up[span, :] = jnp.where(above, 0.25 * (CORI_BASE + CORI_SLOPE * (place + 1) / total), 0.0)
    for p in range(PW):
        here = depth[p, span, :]
        if p > 0:
            hu[p, span, :] = HALF_DEPTH * (here + depth[p - 1, span, :])
        vertical(depth.at[p], hv.at[p], hvu.at[p], inside, rows)
    ends[0] = depth[0, 0:height]
    ends[1] = depth[PW - 1, 0:height]
    for h in range(w_rows.shape[0]):
        cs = slice(h * LANES, (h + 1) * LANES)
        w_rows[h] = weight[:, cs].astype(F32)
        w_planes[:, cs] = jnp.concatenate(
            [w_rows[h, pl.ds(k, PH, stride=PW), :] for k in range(PW)], axis=0
        ).astype(BF16)


def row_ids(rows, lat_count):
    wide = rows + 2 * HALO
    row = lax.broadcasted_iota(jnp.int32, (wide, LANES), 0) + (lax.axis_index("lat") * rows - HALO)
    return row, (row >= 0) & (row < lat_count * rows)


def vertical(depth, hv, hvu, inside, rows):
    span = slice(PAD - HALO, PAD + rows + HALO)
    here = depth[span, :]
    below = depth[PAD - HALO - 1 : PAD + rows + HALO - 1, :]
    above = depth[PAD - HALO + 1 : PAD + rows + HALO + 1, :]
    hv[span, :] = HALF_DEPTH * (here + below)
    hvu[span, :] = jnp.where(inside, HALF_DEPTH * (here + above), 0.0)


def back_kernel(members, state, sea, vel):
    rows, cols = sea.shape[1:]
    patches = cols // PW
    per = LANES // patches
    matrix = plane_matrix(cols, inverse=True)
    segment = lane_ids(rows) // patches
    for i in range(3):
        parts = []
        for m in range(members):
            groups = []
            for g in range(PW // per):
                pieces = [
                    turned(state[i, g * per + j, PAD : PAD + rows, :], (j - m) * patches)
                    for j in range(per)
                ]
                groups.append(by_segment(pieces, segment))
            parts.append(jnp.concatenate(groups, axis=1))
        value = moved(jnp.concatenate(parts, axis=0), matrix)
        for m in range(members):
            part = value[m * rows : (m + 1) * rows]
            if i == 0:
                sea[m] = part
            else:
                vel[i - 1, m] = part * GRAVITY


def flow_step(src, src_rim, dst, dst_rim, force, force_rim, hus, hvs, hvus, cu, cv, cv_up, last_mask, rows, patches, ending):
    strip = PW
    wide = rows + 2 * HALO
    start = PAD - HALO
    keep = 1.0 - DRAG_RATE
    here = pl.ds(start, wide)
    last = lane_ids(wide) % patches == patches - 1

    def wrap_left(plane, rim):
        return pltpu.roll(jnp.where(last, rim, plane), 1, 1)

    def wrap_right(plane, rim):
        return jnp.where(last, pltpu.roll(rim, PW - 1, 1), pltpu.roll(plane, LANES - 1, 1))

    def of(planes, rim, i, p):
        return rim.at[i] if p == strip else planes.at[i, p]

    def new_level(p, fx, fx_right):
        n = of(src, src_rim, 2, p)[here, :]
        n_up = pltpu.roll(n, wide - 1, 0)
        fy = hvus[p][here, :] * n_up - hvs[p][here, :] * n
        level = of(src, src_rim, 0, p)[here, :] - ((fx_right - fx) + fy)
        of(dst, dst_rim, 0, p)[here, :] = level
        return level, n, n + n_up

    def new_flow(p, e, e_right, n, v, level, level_left):
        u = e + e_right
        push = force_rim[here, :] if p == strip else force[p, here, :]
        of(dst, dst_rim, 1, p)[here, :] = keep * e + cu[here, :] * v - (level - level_left) + push
        below = pltpu.roll(level - cv_up[here, :] * u, 1, 0)
        north = keep * n - cv[here, :] * u - level + below
        home = of(dst, dst_rim, 2, p)
        home[pl.ds(start, wide - HALO), :] = north[: wide - HALO]
        home[pl.ds(start + wide - HALO, HALO), :] = north[wide - HALO :] * last_mask

    e_rim = src_rim[1, here, :]
    fx_rim = hus[strip][here, :] * e_rim
    level_rim, n_rim, vs_rim = new_level(strip, fx_rim, pltpu.roll(fx_rim, LANES - 1, 1))
    if not ending:
        new_flow(
            strip,
            e_rim,
            pltpu.roll(e_rim, LANES - 1, 1),
            n_rim,
            vs_rim + pltpu.roll(vs_rim, 1, 1),
            level_rim,
            pltpu.roll(level_rim, 1, 1),
        )
    e = src[1, 0, here, :]
    e_end = wrap_right(e, e_rim)
    level_last, n_last, vs_last = new_level(
        PW - 1, hus[PW - 1][here, :] * src[1, PW - 1, here, :], hus[PW + 1][here, :] * e_end
    )
    level_left = wrap_left(level_last, level_rim)
    vs_left = wrap_left(vs_last, vs_rim)
    fx = hus[0][here, :] * e
    for p in range(PW):
        if p < PW - 1:
            e_right = src[1, p + 1, here, :]
            fx_right = hus[p + 1][here, :] * e_right
            level, n, vs = new_level(p, fx, fx_right)
        else:
            e_right, fx_right = e_end, None
            level, n, vs = level_last, n_last, vs_last
        new_flow(p, e, e_right, n, vs + vs_left, level, level_left)
        level_left, vs_left, e, fx = level, vs, e_right, fx_right


def flow_kernel(
    members,
    rows,
    cols,
    lat_count,
    state,
    force,
    ends,
    hu,
    hv,
    hvu,
    cu,
    cv,
    cv_up,
    w_planes,
    side,
    east,
    west,
    partial,
    gram,
    final,
    state_b,
    rim_a,
    rim_b,
    force_rim,
    depth_rim,
    west_rim,
    hu_rim,
    hv_rim,
    hvu_rim,
    patch_t,
    slope,
    state_a,
):
    patches = cols // PW
    lat = lax.axis_index("lat")
    height = rows + 2 * PAD
    wide = rows + 2 * HALO
    span = slice(PAD - HALO, PAD + rows + HALO)
    state_a[:, :, span, :] = state[:, :, span, :]
    depth_rim[height - HALO : height, :] = jnp.zeros((HALO, LANES), F32)
    behind = slice(3 * wide, 3 * wide + 2 * HALO)
    got = [ref[behind, :].astype(F32)[:HALO] for ref in (side, east, west)]
    depth_rim[0:HALO, :] = rims_of(*got, patches)[0]
    rim_homes = (rim_a.at[0], rim_a.at[1], rim_a.at[2], force_rim, depth_rim, west_rim)
    for n in range(3):
        rs = slice(n * wide, (n + 1) * wide)
        got = [ref[rs, :].astype(F32) for ref in (side, east, west)]
        for i, rim in zip((2 * n, 2 * n + 1), rims_of(*got, patches)):
            rim_homes[i][span, :] = rim * (1.0 / GRAVITY) if i in (1, 2, 3) else rim
    _, inside = row_ids(rows, lat_count)
    last = lane_ids(wide) % patches == patches - 1
    rim = depth_rim[span, :]
    left = pltpu.roll(jnp.where(last, rim, ends[1, span, :]), 1, 1)
    first = HALF_DEPTH * (ends[0, span, :] + left)
    outer = lane_ids(wide) % patches >= 3 * HALO
    rim = HALF_DEPTH * (rim + jnp.where(outer, west_rim[span, :], pltpu.roll(rim, 1, 1)))
    hu_rim[0, span, :] = first
    hu_rim[1, span, :] = rim
    hu_rim[2, span, :] = jnp.where(
        last, pltpu.roll(rim, PW - 1, 1), pltpu.roll(first, LANES - 1, 1)
    )
    vertical(depth_rim, hv_rim, hvu_rim, inside, rows)
    hus = [hu_rim.at[0]] + [hu.at[p] for p in range(1, PW)] + [hu_rim.at[1], hu_rim.at[2]]
    hvs = [hv.at[p] for p in range(PW)] + [hv_rim]
    hvus = [hvu.at[p] for p in range(PW)] + [hvu_rim]

    last_mask = jnp.where(lat < lat_count - 1, 1.0, 0.0)
    count = rows // PH

    def embed_step(state, turn, sub):
        step = 2 * turn + sub
        total = None
        for b in range(count):
            cells = state[0, 0:PW, PAD + b * PH : PAD + (b + 1) * PH, :].reshape(PW * PH, LANES)
            cells_t = cells.T.astype(BF16)
            act = jnp.tanh(jnp.dot(cells_t, w_planes[...], preferred_element_type=F32))
            total = act if total is None else total + act
            fall = (1.0 - act * act).astype(BF16)
            for m in range(members):
                rs = slice(m * patches, (m + 1) * patches)
                to = slice(b * patches, (b + 1) * patches)
                patch_t[m, to, :] = cells_t[rs]
                slope[m, to, :] = fall[rs]
        sums = jnp.sum(total.reshape(members, patches, total.shape[1]), axis=1)
        partial[turn, sub * members : (sub + 1) * members, :] = sums
        for m in range(members):
            gram[step * members + m] = lax.dot_general(
                patch_t[m], slope[m], (((0,), (0,)), ((), ())), preferred_element_type=F32
            )

    def step_of(src, src_rim, dst, dst_rim, ending=False):
        flow_step(
            src, src_rim, dst, dst_rim, force, force_rim, hus, hvs, hvus, cu, cv, cv_up, last_mask, rows, patches, ending
        )

    one, two = (state_a, rim_a), (state_b, rim_b)
    step_of(*one, *two)
    for step in range(1, STEPS):
        src, dst = (two, one) if step % 2 else (one, two)
        step_of(*src, *dst, step == STEPS - 1)
        embed_step(src[0], (step - 1) // 2, (step - 1) % 2)
    inner = slice(PAD, PAD + rows)
    final[:, :, inner, :] = state_a[:, :, inner, :]
    embed_step(state_a, STEPS // 2 - 1, 1)


def split(value):
    high = value.astype(BF16)
    return high, (value - high.astype(F32)).astype(BF16)


def dot(a, b, ca=1, cb=0):
    return lax.dot_general(a, b, (((ca,), (cb,)), ((), ())), preferred_element_type=F32)


def mm(a, b, ca=1, cb=0):
    return dot(a[0], b[0], ca, cb) + (dot(a[0], b[1], ca, cb) + dot(a[1], b[0], ca, cb))


def member_terms(
    members, ids_col, props, w_in, b_in, w_out, low_in, ends, low_own, upper_own, w_sum, out_cat
):
    count = props.shape[0]
    half = props.shape[1] // 2
    hot = jnp.where(ids_col[...] == lax.broadcasted_iota(jnp.int32, (count, count), 1), 1.0, 0.0)
    params = jnp.dot(hot, props[...], precision=PRECISE, preferred_element_type=F32)
    low = mm(split(params[:, :half]), split(w_in[:half, :])) + b_in[...]
    ends[...] = params
    low_in[...] = low
    samples = low_own.shape[0]
    slot = lax.broadcasted_iota(jnp.int32, (samples, count), 1)
    row = lax.broadcasted_iota(jnp.int32, (samples, count), 0)
    hot = jnp.where(slot == lax.axis_index("grp") * members + row % members, 1.0, 0.0)
    low_own[...] = jnp.dot(hot, low, precision=PRECISE, preferred_element_type=F32)
    upper_own[...] = jnp.dot(hot, params[:, half:], precision=PRECISE, preferred_element_type=F32)
    high, rest = split(w_in[half:, :])
    w_sum[0] = high
    w_sum[1] = rest
    high, rest = split(w_out[...].T)
    out_cat[...] = jnp.concatenate([high, high, rest], axis=1)


def repeated(rows, count):
    return jnp.concatenate([rows] * count, axis=0)


def flow_grads(lower_in, upper, summary, w_sum, out_cat, b_out):
    half = upper.shape[1]
    width = 2 * half
    sums = split(summary)
    hidden = jnp.tanh(mm(sums, w_sum) + lower_in)
    hid = split(hidden)
    both = dot(hid[0], out_cat[:, width:])
    raw = both[:, :width] + both[:, width:] + dot(hid[1], out_cat[:, :width]) + b_out[...]
    log_scale = jnp.tanh(raw[:, :half])
    grown = upper * jnp.exp(log_scale)
    latent = grown + raw[:, half:]
    d_scale = (latent * grown - 1.0) * (1.0 - log_scale * log_scale)
    d_raw = jnp.concatenate([d_scale, latent], axis=1)
    d_r = split(d_raw)
    d_hidden = dot(jnp.concatenate([d_r[0], d_r[1], d_r[0]], axis=1), out_cat[...], 1, 1)
    d_hidden = d_hidden * (1.0 - hidden * hidden)
    return sums, hid, d_raw, d_r, d_hidden


def local_kernel(
    inv_root, mine, theirs, low_in, upper, w_sum, out_cat, b_out, gram, kept, sent, own, total
):
    sums = (mine[...] + theirs[...]) * inv_root
    count = sums.shape[0]
    items = own.shape[0]
    for part in range(count // items):

        @pl.when(lax.axis_index("lon") == part)
        def _():
            own[...] = sums[part * items : (part + 1) * items, :]

    w_pair = (w_sum[0], w_sum[1])
    d_hidden = flow_grads(low_in[...], upper[...], sums, w_pair, out_cat, b_out)[-1]
    d_summary = mm(split(d_hidden), w_pair, 1, 1) * inv_root
    acc = gram[0] * d_summary[0:1, :]
    for i in range(1, count):
        acc = acc + gram[i] * d_summary[i : i + 1, :]
    total[...] = acc
    cells = acc.shape[0] // 2
    core = lax.axis_index("grp") % 2
    kept[...] = total[pl.ds(pl.multiple_of(core * cells, 8), cells), :]
    sent[...] = total[pl.ds(pl.multiple_of((1 - core) * cells, 8), cells), :]


def couple_kernel(
    members, lat_count, grp_count, order, summary, low_in, ends, w_sum, out_cat, b_out, rows, square, sorted_sums, staged
):
    per = summary.shape[0] // len(order)
    for index, (lat_flip, grp_flip) in enumerate(order):
        block = (lax.axis_index("lat") ^ lat_flip) * grp_count + (lax.axis_index("grp") ^ grp_flip)
        sorted_sums[pl.ds(pl.multiple_of(block * per, per), per), :] = summary[
            index * per : (index + 1) * per, :
        ]
    params = ends[...]
    half = params.shape[1] // 2
    groups = [slice(g * members, (g + 1) * members) for g in range(grp_count)]
    steps = per // members
    spread = lambda value: jnp.concatenate(
        [repeated(value[rs], steps) for rs in groups] * lat_count, axis=0
    )
    lower = spread(params[:, :half])
    sums, hid, d_raw, d_r, d_hidden = flow_grads(
        spread(low_in[...]),
        spread(params[:, half:]),
        sorted_sums[...],
        (w_sum[0], w_sum[1]),
        out_cat,
        b_out,
    )
    low = split(lower)
    context = [jnp.concatenate([sums[n], low[n]], axis=1) for n in range(2)]
    g_in = mm(context, split(d_hidden), 0, 0)
    width = 2 * half
    both = dot(hid[0], jnp.concatenate(d_r, axis=1), 0, 0)
    g_out = both[:, :width] + both[:, width:] + dot(hid[1], d_r[0], 0, 0)
    g_in_b = jnp.sum(d_hidden, axis=0, keepdims=True)
    g_out_b = jnp.sum(d_raw, axis=0, keepdims=True)
    hidden = d_hidden.shape[1]
    per_row = hidden // LANES
    feats = summary.shape[1]
    fold = LANES // width
    base = (half + feats) * per_row
    after = base + per_row
    tail = after + hidden // fold
    rows[base:, :] = jnp.zeros((rows.shape[0] - base, LANES), F32)
    for q in range(per_row):
        cs = slice(q * LANES, (q + 1) * LANES)
        rows[pl.ds(q, half, stride=per_row), :] = g_in[feats:, cs]
        rows[pl.ds(half * per_row + q, feats, stride=per_row), :] = g_in[:feats, cs]
        rows[base + q : base + q + 1, :] = g_in_b[:, cs]
    staged[...] = jnp.concatenate([g_out, jnp.zeros((hidden, LANES - width), F32)], axis=1)
    packed = jnp.zeros((hidden // fold, LANES), F32)
    for j in range(fold):
        packed = packed + turned(staged[pl.ds(j, hidden // fold, stride=fold), :], j * width)
    rows[after:tail, :] = packed
    rows[tail : tail + 1, :] = jnp.concatenate(
        [g_out_b, jnp.zeros((1, LANES - width), F32)], axis=1
    )
    whole = rows[...]
    square[...] = jnp.sum(whole * whole, axis=0, keepdims=True)


def finish_kernel(count, mine, theirs, couple, square, out, whole):
    core = lax.axis_index("grp") % 2
    cells = mine.shape[0]
    per_row = mine.shape[1] // LANES
    for h in range(per_row):
        cs = slice(h * LANES, (h + 1) * LANES)
        whole[h, pl.ds(pl.multiple_of(core * cells, 8), cells), :] = mine[:, cs]
        whole[h, pl.ds(pl.multiple_of((1 - core) * cells, 8), cells), :] = theirs[:, cs]
    conv = whole[...]
    squares = jnp.sum(conv * conv) + jnp.sum(square[...])
    scale = -lax.rsqrt(jnp.full((1, 1), squares, F32) / count + EPSILON)
    for r in range(PH):
        for h in range(per_row):
            part = whole[h, pl.ds(r, PW, stride=PH), :]
            out[pl.ds(r * PW * per_row + h, PW, stride=per_row), :] = part * scale
    used = 2 * cells * per_row
    out[used : used + couple.shape[0], :] = couple[...] * scale


def neighbour(value, axis, step):
    count = lax.axis_size(axis)
    pairs = [(i, (i + step) % count) for i in range(count)]
    return lax.ppermute(value, axis, pairs)


def from_lat(value, step):
    count = lax.axis_size("lat")
    return lax.ppermute(value, "lat", [(i, i + step) for i in range(count) if 0 <= i + step < count])


def swapped(value, axis, flip):
    count = lax.axis_size(axis)
    return lax.ppermute(value, axis, [(i, i ^ flip) for i in range(count)])


def flips(axis):
    count = lax.axis_size(axis)
    return [1 << i for i in range(count.bit_length() - 1)]


def shape(*dims, dtype=F32):
    return jax.ShapeDtypeStruct(dims, dtype)


def shards(
    sea_surface,
    velocity,
    levels,
    wind_basis,
    proposals,
    member_ids,
    conv_weight,
    couple_in,
    couple_in_bias,
    couple_out,
    couple_out_bias,
):
    members, rows, cols = sea_surface.shape
    lat_count, lon_count = lax.axis_size("lat"), lax.axis_size("lon")
    grp_count = lax.axis_size("grp")
    cells, feats = conv_weight.shape
    hid, width = couple_out.shape
    patches = cols // PW
    samples = STEPS * members
    groups = (4 * members + 2) * HALO
    height = rows + 2 * PAD
    inv_root = 1.0 / math.sqrt(rows // PH * (cols * lon_count // PW))

    anywhere = pl.BlockSpec(memory_space=pl.ANY)
    low, high = pl.pallas_call(
        lambda *refs: pack_kernel(members, *refs),
        out_shape=(shape(groups, cols, dtype=BF16), shape(groups, cols, dtype=BF16)),
        in_specs=[anywhere] * 6,
        out_specs=(vmem(), vmem()),
        scratch_shapes=[
            pltpu.SMEM(member_ids.shape, jnp.int32),
            pltpu.VMEM((2, 3, members, HALO, cols), F32),
            pltpu.VMEM((2, 16, cols), jnp.int32),
            pltpu.VMEM((2, wind_basis.shape[0], 16, cols), BF16),
            pltpu.VMEM(proposals.shape, F32),
            pltpu.SemaphoreType.DMA((12,)),
        ],
        compiler_params=params_of(60),
        name="pack_rows",
    )(member_ids, sea_surface, velocity, levels, wind_basis, proposals)

    south = from_lat(high, 1)
    north = from_lat(low, -1)

    planes, side = pl.pallas_call(
        lambda *refs: planar_kernel(members, *refs),
        out_shape=(shape(5, PW, rows, LANES), shape(6 * rows, LANES, dtype=BF16)),
        in_specs=[smem()] + [vmem()] * 5,
        out_specs=(vmem(), vmem()),
        compiler_params=params_of(32),
        cost_estimate=pl.CostEstimate(flops=2 * 10**9, bytes_accessed=6 * MEBI, transcendentals=0),
        name="to_planes",
    )(member_ids, sea_surface, velocity, levels, wind_basis, proposals)

    wide = rows + 2 * HALO
    rim = pl.pallas_call(
        lambda *refs: rim_kernel(members, patches, *refs),
        out_shape=shape(3 * wide + 2 * HALO, LANES, dtype=BF16),
        in_specs=[vmem()] * 3,
        out_specs=vmem(),
        compiler_params=params_of(16),
        name="rim",
    )(south, north, side)
    west = neighbour(rim, "lon", 1)
    east = west if lon_count == 2 else neighbour(rim, "lon", -1)

    def after(value, *others):
        return lax.optimization_barrier((value,) + others)[0]

    b_out = couple_out_bias.reshape(1, -1)
    plane = (PW, height + HALO, LANES)
    prepared = pl.pallas_call(
        lambda *refs: prepare_kernel(members, rows, cols, lat_count, *refs),
        out_shape=(
            shape(3, *plane),
            shape(*plane),
            shape(2, height, LANES),
            shape(*plane),
            shape(*plane),
            shape(*plane),
            shape(height, LANES),
            shape(height, LANES),
            shape(height, LANES),
            shape(cells, feats, dtype=BF16),
            shape(proposals.shape[0], hid),
            shape(*proposals.shape),
            shape(samples, hid),
            shape(samples, width // 2),
            shape(2, feats, hid, dtype=BF16),
            shape(hid, 3 * width, dtype=BF16),
        ),
        in_specs=[vmem()] * 9,
        out_specs=(vmem(),) * 16,
        scratch_shapes=[
            pltpu.VMEM(plane, F32),
            pltpu.VMEM((feats // LANES, cells, LANES), F32),
        ],
        compiler_params=params_of(16),
        cost_estimate=pl.CostEstimate(flops=10**9, bytes_accessed=4 * MEBI, transcendentals=0),
        name="prepare",
    )(
        south,
        north,
        planes,
        conv_weight,
        member_ids.reshape(-1, 1),
        proposals,
        couple_in,
        couple_in_bias.reshape(1, -1),
        couple_out.T,
    )
    prepared, (low_in, ends, low_own, upper_own, w_sum, out_cat) = prepared[:10], prepared[10:]

    partial, gram, final = pl.pallas_call(
        lambda *refs: flow_kernel(members, rows, cols, lat_count, *refs),
        out_shape=(
            shape(STEPS // 2, 2 * members, feats),
            shape(samples, cells, feats),
            shape(3, *plane),
        ),
        in_specs=[vmem()] * 13,
        out_specs=(vmem(),) * 3,
        scratch_shapes=[
            pltpu.VMEM((3, *plane), F32),
            pltpu.VMEM((3, height, LANES), F32),
            pltpu.VMEM((3, height, LANES), F32),
            pltpu.VMEM((height, LANES), F32),
            pltpu.VMEM((height, LANES), F32),
            pltpu.VMEM((height, LANES), F32),
            pltpu.VMEM((3, height, LANES), F32),
            pltpu.VMEM((height, LANES), F32),
            pltpu.VMEM((height, LANES), F32),
            pltpu.VMEM((members, rows // PH * patches, cells), BF16),
            pltpu.VMEM((members, rows // PH * patches, feats), BF16),
            pltpu.VMEM((3, *plane), F32),
        ],
        compiler_params=params_of(32),
        name="flow_embed",
    )(*prepared, rim, east, west)
    partial = partial.reshape(samples, feats)

    if lon_count == 2:
        others = swapped(partial, "lon", 1)
    else:
        others = lax.psum(partial, "lon") - partial
    surface_out, velocity_out = pl.pallas_call(
        lambda *refs: back_kernel(members, *refs),
        out_shape=(shape(members, rows, cols), shape(2, members, rows, cols)),
        in_specs=[vmem()],
        out_specs=(vmem(), vmem()),
        compiler_params=params_of(24),
        cost_estimate=pl.CostEstimate(flops=2 * 10**9, bytes_accessed=6 * MEBI, transcendentals=0),
        name="from_planes",
    )(final)

    others, surface_out, velocity_out = lax.optimization_barrier((others, surface_out, velocity_out))
    summaries = (partial + others) * inv_root

    items = samples // lon_count
    kept, sent, own = pl.pallas_call(
        lambda *refs: local_kernel(inv_root, *refs),
        out_shape=(shape(cells // 2, feats), shape(cells // 2, feats), shape(items, feats)),
        in_specs=[vmem()] * 8,
        out_specs=(vmem(),) * 3,
        scratch_shapes=[pltpu.VMEM((cells, feats), F32)],
        compiler_params=params_of(16),
        name="local_loss",
    )(partial, others, low_own, upper_own, w_sum, out_cat, b_out, gram)

    def gather(axis, flip):
        both = jnp.concatenate([gathered, swapped(gathered, axis, flip)], axis=0)
        return both, order + [(a ^ flip, b) if axis == "lat" else (a, b ^ flip) for a, b in order]

    gathered, order = summaries.astype(jnp.float16), [(0, 0)]
    gathered, order = gather("grp", 2)
    conv = kept + swapped(sent, "grp", 1)
    if lon_count == 2:
        corner = lax.ppermute(
            conv,
            ("lon", "grp"),
            [(i, (i // grp_count ^ 1) * grp_count + (i % grp_count ^ 2)) for i in range(2 * grp_count)],
        )
        by_lon = swapped(conv, "lon", 1)
        gathered = after(gathered, by_lon)
        conv = (conv + corner) + (swapped(conv, "grp", 2) + by_lon)
    else:
        conv = conv + swapped(conv, "grp", 2)
        for flip in flips("lon"):
            conv = conv + swapped(conv, "lon", flip)
    for flip in reversed(flips("lat")):
        by_lat = swapped(conv, "lat", flip)
        if flip > 1:
            gathered, order = gather("lat", flip)
            gathered = after(gathered, conv)
            conv = conv + by_lat
    gathered, order = gather("lat", 1)
    gathered = after(gathered, conv)
    gathered, order = gather("grp", 1)

    low_rows = (couple_in.size + hid + couple_out.size) // LANES + 1
    low_rows = -(-low_rows // 8) * 8
    count = cells * feats + couple_in.size + hid + couple_out.size + width
    couple, square = pl.pallas_call(
        lambda *refs: couple_kernel(members, lat_count, grp_count, order, *refs),
        out_shape=(shape(low_rows, LANES), shape(1, LANES)),
        in_specs=[vmem()] * 6,
        out_specs=(vmem(), vmem()),
        scratch_shapes=[
            pltpu.VMEM((len(order) * samples, feats), F32),
            pltpu.VMEM((hid, LANES), F32),
        ],
        compiler_params=params_of(24),
        cost_estimate=pl.CostEstimate(flops=3 * 10**9, bytes_accessed=3 * MEBI, transcendentals=0),
        name="couple_grads",
    )(gathered.astype(F32), low_in, ends, w_sum, out_cat, b_out)

    conv = conv + after(by_lat, couple, square)
    conv_other = swapped(conv, "grp", 1)

    stepped = pl.pallas_call(
        lambda *refs: finish_kernel(count, *refs),
        out_shape=shape(cells * feats // LANES + low_rows, LANES),
        in_specs=[vmem()] * 4,
        out_specs=vmem(),
        scratch_shapes=[pltpu.VMEM((feats // LANES, cells, LANES), F32)],
        compiler_params=params_of(16),
        name="finish",
    )(conv, conv_other, couple, square)
    weight_step = stepped.reshape(-1)[:count]

    return (surface_out, velocity_out, own.reshape(1, 1, 1, items, feats), weight_step)


def solution(mesh):
    in_specs = (
        P("grp", "lat", "lon"),
        P(None, "grp", "lat", "lon"),
        P("lat", "lon"),
        P(None, "lat", "lon"),
        P(),
        P(),
        P(),
        P(),
        P(),
        P(),
        P(),
    )
    out_specs = (
        P("grp", "lat", "lon"),
        P(None, "grp", "lat", "lon"),
        P("lon", "lat", "grp", None, None),
        P(),
    )
    return jax.shard_map(shards, mesh=mesh, in_specs=in_specs, out_specs=out_specs, check_vma=False)
```
